32 devices in a mesh: dp: 8 (over y, x, core), mp: 4 (over z).
Axes of the slice: x: 2, y: 2, z: 4, core: 2. Of those that a mesh axis runs over, the one named last changes fastest.
Arguments:
- inputs: bfloat16 [8192, 2048], P('dp'), may hold values from -6 to 6
- doc_ids: int32 [8, 1024], P('dp'), may hold values from 0 to 3, never falling along the last dimension, each value on 1 to 512 neighbouring positions
- pad_mask: int32 [8, 1024], P('dp'), may hold values from 0 to 1, as said below
- attn_gain: float32 [2048], replicated, may hold values from 0.5 to 1.5
- attn_shift: float32 [2048], replicated, may hold values from -4 to 4
- w_query: bfloat16 [2048, 2048], P(None, 'mp'), may hold values from -0.125 to 0.125
- b_query: float32 [2048], P('mp'), may hold values from -4 to 4
- w_keyval: bfloat16 [2048, 256], replicated, may hold values from -0.125 to 0.125
- b_value: float32 [128], replicated, may hold values from -4 to 4
- w_out: bfloat16 [2048, 2048], P('mp'), may hold values from -0.5 to 0.5
- b_out: float32 [2048], replicated, may hold values from -4 to 4
- mlp_gain: float32 [2048], replicated, may hold values from 0.5 to 1.5
- mlp_shift: float32 [2048], replicated, may hold values from -4 to 4
- w_up: bfloat16 [2048, 8192], P(None, 'mp'), may hold values from -0.125 to 0.125
- b_up: float32 [8192], P('mp'), may hold values from -4 to 4
- w_down: bfloat16 [8192, 2048], P('mp'), may hold values from -0.0625 to 0.0625
- b_down: float32 [2048], replicated, may hold values from -4 to 4
- cotangent: bfloat16 [8192, 2048], P('dp'), may hold values from -6 to 6
Outputs:
- outputs: bfloat16 [8192, 2048], P('dp')
- input_grad: bfloat16 [8192, 2048], P('dp')
- grad_attn_gain: float32 [2048], replicated
- grad_attn_shift: float32 [2048], replicated
- grad_w_query: float32 [2048, 2048], P('dp', 'mp')
- grad_b_query: float32 [2048], P('mp')
- grad_w_keyval: float32 [2048, 256], replicated
- grad_b_value: float32 [128], replicated
- grad_w_out: float32 [2048, 2048], P('mp', 'dp')
- grad_b_out: float32 [2048], replicated
- grad_mlp_gain: float32 [2048], replicated
- grad_mlp_shift: float32 [2048], replicated
- grad_w_up: float32 [2048, 8192], P('dp', 'mp')
- grad_b_up: float32 [8192], P('mp')
- grad_w_down: float32 [8192, 2048], P('mp', 'dp')
- grad_b_down: float32 [2048], replicated
The draws below stay inside these ranges and needn't reach their ends.
Inputs may be any that keep to these rules, and one draw needn't show every extreme that they name: `doc_ids`: in each row the document numbers never fall and start at 0. `pad_mask`: in each row of 1024 tokens the ones come first, then zeros; a row's first token is a one.
All inputs are finite; a program needn't handle non-finite values.
Results may differ from the reference program's by a relative error of at most 0.012.
Values sent between devices are 32-bit elements; how exact they have to be, the bound alone decides.
A program may use at most 256 MiB of HBM per device.

```python
import math
import jax
import jax.numpy as jnp
import numpy as np
from jax import lax

D = 2048
H = 16
HD = 128
FF = 8192
SEQ = 1024
DOCS = 4
ROWS = 8
TOKENS = 8192


def draw_pad_mask(key, part):
    key = jax.random.fold_in(key, 7)
    cut = jax.random.randint(key, (ROWS, 1), 0, SEQ // 4 + 1)
    keep = jnp.arange(SEQ)[None, :] < SEQ - cut
    return keep.astype(jnp.int32)


def strengthened(result, stream_key, source, target, blocks, factor):
    def block_of(axis_at):
        return (jnp.arange(result.shape[axis_at]) // (result.shape[axis_at] // blocks)).reshape((-1,) + (1,) * (result.ndim - 1 - axis_at))

    one_side = jax.random.permutation(stream_key, blocks)[block_of(target)]
    other_side = (block_of(target) + blocks // 2) % blocks
    return jnp.where((block_of(source) == one_side) | (block_of(source) == other_side), factor * result, result)


def block_levels(stream_key, extent, cuts, least, top_value):
    factor_of, own = 1.0, jax.random.fold_in(stream_key, 6)
    for dim, blocks in cuts:
        heights = jnp.exp(jax.random.uniform(jax.random.fold_in(own, dim), (blocks,), jnp.float32, least / len(cuts), top_value / len(cuts)))
        factor_of = factor_of * jnp.repeat(heights, extent[dim] // blocks).reshape([-1 if axis == dim else 1 for axis in range(len(extent))])
    return factor_of


def profile(amount, total, limit, skew):
    portions = [(1 << 20) // math.isqrt(rank ** skew) + 1 for rank in range(2, amount + 1)]
    rest, given = total - limit - (amount - 1), [1] * (amount - 1)
    while rest > 0:
        free = [i for i in range(amount - 1) if given[i] < limit]
        mass, budget = sum([portions[i] for i in free]), rest
        for i in free:
            more = min(limit - given[i], max(1, budget * portions[i] // mass), rest)
            given[i] = given[i] + more
            rest = rest - more
    return np.array([limit] + given)


def uneven(key, count, total, most, skew):
    if count == 2:
        one = jax.random.randint(key, (), max(1, total - most), min(most, total - 1) + 1)
        return jnp.stack([one, total - one])
    sizes = jnp.asarray(profile(count, total, most, skew), jnp.int32)
    twos = (count - 1) // 2
    giver, taker = sizes[1:1 + 2 * twos:2], sizes[2:2 + 2 * twos:2]
    room = jnp.minimum(giver - 1, most - taker)
    shifted = jax.random.randint(jax.random.fold_in(key, 1), (twos,), 0, 1 << 20) % (room + 1)
    sizes = sizes.at[1:1 + 2 * twos:2].set(giver - shifted).at[2:2 + 2 * twos:2].set(taker + shifted)
    return sizes[jax.random.permutation(jax.random.fold_in(key, 2), count)]


def centred(key, shape, width, most, pieces=(), held_as=jnp.bfloat16):
    level = block_levels(key, shape, pieces, -0.22, 0.18) if pieces else 1.0
    values = jax.random.normal(key, shape, jnp.float32) * width * level
    return jnp.minimum(jnp.maximum(values, -most), most).astype(held_as)


def heavy_noise(key, dims, width, bound, shards, heavy, kind=jnp.bfloat16):
    result = width * jax.random.normal(key, dims, jnp.float32)
    if shards:
        result = result * block_levels(key, dims, shards, -0.22, 0.18)
    return jnp.clip(strengthened(result, jax.random.fold_in(key, 3), *heavy), -bound, bound).astype(kind)


def setup_inputs(seed: int = 0) -> dict:
    key_list = jax.random.split(jax.random.key(seed), 19)
    return {
        "inputs": centred(key_list[0], (TOKENS, D), 1.0, 6.0, ((0, 8),)),
        "doc_ids": jax.vmap(lambda own: jnp.searchsorted(jnp.cumsum(uneven(own, DOCS, SEQ, SEQ // 2, 0)), jnp.arange(SEQ), side="right"))(jax.random.split(key_list[1], ROWS)).reshape((ROWS, SEQ)).astype(jnp.int32),
        "pad_mask": draw_pad_mask(jax.random.fold_in(key_list[18], 71), 0),
        "attn_gain": jnp.clip(1.0 + 0.1 * jax.random.normal(key_list[3], (D,), jnp.float32), 0.5, 1.5),
        "attn_shift": centred(key_list[4], (D,), 0.3, 4.0, (), jnp.float32),
        "w_query": centred(key_list[5], (D, H * HD), D ** -0.5, 0.125, ((1, 4),)),
        "b_query": centred(key_list[6], (H * HD,), 0.3, 4.0, ((0, 4),), jnp.float32),
        "w_keyval": centred(key_list[7], (D, 2 * HD), D ** -0.5, 0.125),
        "b_value": centred(key_list[8], (HD,), 0.3, 4.0, (), jnp.float32),
        "w_out": centred(key_list[9], (H * HD, D), (H * HD // 16) ** -0.5, 0.5, ((0, 4),)),
        "b_out": centred(key_list[10], (D,), 0.3, 4.0, (), jnp.float32),
        "mlp_gain": jnp.clip(1.0 + 0.1 * jax.random.normal(key_list[11], (D,), jnp.float32), 0.5, 1.5),
        "mlp_shift": centred(key_list[12], (D,), 0.3, 4.0, (), jnp.float32),
        "w_up": centred(key_list[13], (D, FF), D ** -0.5, 0.125, ((1, 4),)),
        "b_up": centred(key_list[14], (FF,), 0.3, 4.0, ((0, 4),), jnp.float32),
        "w_down": centred(key_list[15], (FF, D), FF ** -0.5, 0.0625, ((0, 4),)),
        "b_down": centred(key_list[16], (D,), 0.3, 4.0, (), jnp.float32),
        "cotangent": heavy_noise(key_list[17], (TOKENS, D), 1.0, 6.0, ((0, 8),), (0, 1, 8, 2.0)),
    }


EPS = 1e-05

@jax.custom_vjp
def low(v):
    return lax.optimization_barrier(v.astype(jnp.bfloat16)).astype(jnp.float32)

@jax.custom_vjp
def low_back(v):
    return v

def low_keep(v):
    return (low(v), None)

def low_pass(kept, grad):
    return (grad,)

def back_keep(v):
    return (v, None)

def back_low(kept, grad):
    return (low(grad),)
low.defvjp(low_keep, low_pass)
low_back.defvjp(back_keep, back_low)

def matmul(left, right):
    return jnp.dot(left, right, precision=lax.Precision.HIGHEST)

def norm_rows(rows_in, gain, shift):
    center = rows_in - lax.optimization_barrier(jnp.mean(rows_in, axis=-1, keepdims=True))
    spread = lax.optimization_barrier(jnp.mean(center * center, axis=-1, keepdims=True))
    return center * lax.rsqrt(spread + EPS) * gain + shift

def layer_row(weights, row_in, row_doc, row_pad):
    attn_gain, attn_shift, w_query, b_query, w_keyval, b_value, w_out, b_out, mlp_gain, mlp_shift, w_up, b_up, w_down, b_down = weights
    normed_attn = low(norm_rows(row_in, attn_gain, attn_shift))
    queries = low(low_back(matmul(normed_attn, w_query) + b_query))
    bias_full = jnp.concatenate([jnp.zeros((HD,), jnp.float32), b_value])
    keyval = low(low_back(matmul(normed_attn, w_keyval)) + bias_full)
    keys = keyval[:, :HD]
    values = keyval[:, HD:]
    heads = queries.reshape(SEQ, H, HD)
    scores = jnp.einsum('shd,td->hst', heads, keys, precision=lax.Precision.HIGHEST) * (1.0 / math.sqrt(HD))
    scores = low_back(scores)
    places = jnp.arange(SEQ, dtype=jnp.int32)
    allowed = (places[None, :] <= places[:, None]) & (row_doc[None, :] == row_doc[:, None]) & ((row_pad[None, :] == 1) | (places[None, :] == places[:, None]))
    scores = jnp.where(allowed[None], scores, -1e+30)
    row_max = lax.optimization_barrier(jnp.max(scores, axis=-1, keepdims=True))
    raised = jnp.exp(scores - row_max)
    probs = low(raised / lax.optimization_barrier(jnp.sum(raised, axis=-1, keepdims=True)))
    mixed = jnp.einsum('hst,td->shd', probs, values, precision=lax.Precision.HIGHEST).reshape(SEQ, H * HD)
    mixed = low(low_back(mixed))
    branch = low_back(matmul(mixed, w_out) + b_out)
    middle = row_in + branch
    normed_mlp = low(norm_rows(middle, mlp_gain, mlp_shift))
    hidden = low_back(matmul(normed_mlp, w_up) + b_up)
    acts = low(jax.nn.gelu(hidden, approximate=True))
    feed = low_back(matmul(acts, w_down) + b_down)
    return middle + feed

def reference(inputs, doc_ids, pad_mask, attn_gain, attn_shift, w_query, b_query, w_keyval, b_value, w_out, b_out, mlp_gain, mlp_shift, w_up, b_up, w_down, b_down, cotangent):
    params = tuple((param.astype(jnp.float32) for param in (attn_gain, attn_shift, w_query, b_query, w_keyval, b_value, w_out, b_out, mlp_gain, mlp_shift, w_up, b_up, w_down, b_down)))
    rows_x = inputs.astype(jnp.float32).reshape(ROWS, SEQ, D)
    rows_dy = cotangent.astype(jnp.float32).reshape(ROWS, SEQ, D)

    def one_row(totals, item):
        row_x, row_dy, row_doc, row_pad = item

        def forward(weights, row_in):
            return layer_row(weights, row_in, row_doc, row_pad)
        row_out, pull = jax.vjp(forward, params, row_x)
        grads, row_grad = pull(row_dy)
        totals = jax.tree.map(lambda left, right: left + right, totals, grads)
        return (totals, (row_out, row_grad))
    start = jax.tree.map(jnp.zeros_like, params)
    totals, (row_outs, row_grads) = lax.scan(one_row, start, (rows_x, rows_dy, doc_ids, pad_mask))
    return (row_outs.reshape(TOKENS, D).astype(jnp.bfloat16), row_grads.reshape(TOKENS, D).astype(jnp.bfloat16), totals[0], totals[1], totals[2], totals[3], totals[4], totals[5], totals[6], totals[7], totals[8], totals[9], totals[10], totals[11], totals[12], totals[13])
```

```python
import functools
import math

import jax
import jax.numpy as jnp
from jax import lax
from jax.experimental import pallas as pl
from jax.experimental.pallas import tpu as pltpu
from jax.sharding import PartitionSpec as P

EPS = 1e-05
MESH = pl.DeviceIdType.MESH
F32 = jnp.float32
BF16 = jnp.bfloat16
VMEM_LIMIT = 60 * 2**20
HBM = pl.BlockSpec(memory_space=pl.ANY)


def norm_rows(rows_in, gain, shift):
    center = rows_in - jnp.mean(rows_in, axis=-1, keepdims=True)
    spread = jnp.mean(center * center, axis=-1, keepdims=True)
    return center * lax.rsqrt(spread + EPS) * gain + shift


def project(left, right):
    return jnp.dot(left, right, preferred_element_type=F32)


STRIP = 16
COLS = 512
BLOCK = 256
REACH = 3
GROUP = 4
NEG = -1e30


def key_window(c):
    first = max(0, c - REACH + 1) * BLOCK
    return first, (c + 1) * BLOCK - first


def mask_bias(code_col, doc_row, first_key, keys, first_query, queries):
    j = first_key + lax.broadcasted_iota(jnp.int32, (keys, queries), 0)
    i = first_query + lax.broadcasted_iota(jnp.int32, (keys, queries), 1)
    ok = ((j < i) & (code_col == doc_row)) | (j == i)
    return jnp.where(ok, 0.0, NEG)


def dot_t(a, b):
    return lax.dot_general(a, b, (((1,), (1,)), ((), ())), preferred_element_type=F32)


def rows_at(start, count):
    return pl.ds(pl.multiple_of(start, count), count)


def mp_partner(m, r):
    if r == 1:
        return m + 1 - 2 * lax.rem(m, 2)
    if r == 2:
        return m + 2 - 4 * lax.div(m, 2)
    return 3 - m


def flip_bit(d, bit):
    on = lax.rem(lax.div(d, bit), 2)
    return d + bit * (1 - 2 * on)


def front_kernel(
    heads,
    wq, wo, in_hbm, bq, w_kv, gain_ref, shift_ref, kv_bias, code_ref, doc_ref,
    wq_out, wo_out, normed_hbm, q_hbm, mixed_hbm, kv_ref, lse_ref,
    own_q, own_o, gq, go, sq, so, normed, q_ring, mixed_ring, vt, bias_ref, bq_all,
    load_sem, ship_sem, o_sem, ring_sem, z_send, z_recv, b_send, b_recv, n_send, n_recv,
):
    m = lax.axis_index("mp")
    d = lax.axis_index("dp")
    dc, dx, dy = flip_bit(d, 1), flip_bit(d, 2), flip_bit(d, 4)
    dxy = flip_bit(dx, 4)
    g = (gq, go)
    half = (gq.shape[2] // 2, go.shape[2] // 2)
    seq, width = normed.shape
    cols_q = q_ring.shape[2]
    hd = vt.shape[0]
    blocks = seq // BLOCK
    scale = 1.0 / math.sqrt(hd)
    planes = 4

    loads = [
        pltpu.make_async_copy(wq.at[d], own_q, load_sem.at[0]),
        pltpu.make_async_copy(wo.at[d], own_o, load_sem.at[1]),
        pltpu.make_async_copy(in_hbm, normed, load_sem.at[2]),
        pltpu.make_async_copy(wq, sq.at[m], load_sem.at[3]),
        pltpu.make_async_copy(wq, wq_out.at[m], load_sem.at[4]),
        pltpu.make_async_copy(wo, wo_out.at[m], load_sem.at[5]),
    ]
    for c in loads:
        c.start()
    bar = pltpu.get_barrier_semaphore()
    for r in (1, 2, 3):
        pl.semaphore_signal(bar, inc=1, device_id={"mp": mp_partner(m, r)}, device_id_type=MESH)
    for n in (dc, dx, dy):
        pl.semaphore_signal(bar, inc=1, device_id={"dp": n}, device_id_type=MESH)
    loads[0].wait()
    gq[m, d] = own_q[...].astype(F32)
    loads[1].wait()
    go[m, d] = own_o[...].astype(F32)
    bq_all[m] = bq[...]
    pl.semaphore_wait(bar, 6)

    def z_copy(w, r, eighth_of):
        ref = g[w].at[eighth_of, d]
        return pltpu.make_async_remote_copy(
            ref, ref, z_send.at[w, r - 1], z_recv.at[w, r - 1],
            device_id={"mp": mp_partner(m, r)}, device_id_type=MESH,
        )

    def z_send_copy(w, r):
        return z_copy(w, r, m)

    def z_land(w, r):
        return z_copy(w, r, mp_partner(m, r))

    def bias_copy(r, plane):
        return pltpu.make_async_remote_copy(
            bq_all.at[plane], bq_all.at[plane], b_send.at[r - 1], b_recv.at[r - 1],
            device_id={"mp": mp_partner(m, r)}, device_id_type=MESH,
        )

    sent_eighth = (d, d, d, dx, dy, dx, dy, dxy)
    landed_eighth = (dx, dy, dc, flip_bit(dx, 1), flip_bit(dy, 1), dxy, dxy, flip_bit(dxy, 1))
    sent_to = (dx, dy, dc, dc, dc, dy, dx, dc)

    def near(kind, w, r, eighths):
        q = mp_partner(m, r)
        ref = g[w].at[q, eighths[kind]]
        if kind == 5:
            ref = g[w].at[q, eighths[kind], pl.ds(0, half[w])]
        if kind == 6:
            ref = g[w].at[q, eighths[kind], pl.ds(half[w], half[w])]
        return pltpu.make_async_remote_copy(
            ref, ref, n_send.at[kind, w, r - 1], n_recv.at[kind, w, r - 1],
            device_id={"dp": sent_to[kind]}, device_id_type=MESH,
        )

    def go_near(kind, w, r):
        near(kind, w, r, sent_eighth).start()

    def landed(kind, w, r):
        near(kind, w, r, landed_eighth).wait_recv()

    shipped = []
    ring = so.shape[0]

    def ship(w, r, eighth):
        q = mp_partner(m, r)
        n = sum(1 for v, _ in shipped if v == w)
        if w == 0:
            sq[q, eighth] = gq[q, eighth].astype(BF16)
            c = pltpu.make_async_copy(sq.at[q, eighth], wq_out.at[q, eighth], ship_sem.at[n])
        else:
            slot = n % ring
            if n >= ring:
                [c for v, c in shipped if v == 1][n - ring].wait()
            so[slot] = go[q, eighth].astype(BF16)
            c = pltpu.make_async_copy(so.at[slot], wo_out.at[q, eighth], o_sem.at[slot])
        c.start()
        shipped.append((w, c))

    def store_q(q, c, slot):
        at = pl.ds(c * BLOCK, BLOCK)
        return pltpu.make_async_copy(
            q_ring.at[slot], q_hbm.at[at, rows_at(q * cols_q, cols_q)], ring_sem.at[0, slot]
        )

    def store_mixed(q, c, slot):
        at = pl.ds(c * BLOCK, BLOCK)
        return pltpu.make_async_copy(
            mixed_ring.at[slot], mixed_hbm.at[at, rows_at(q * cols_q, cols_q)], ring_sem.at[1, slot]
        )

    def set_bias(c):
        first, count = key_window(c)
        bias_ref[pl.ds(0, count), :] = mask_bias(
            code_ref[pl.ds(first, count), :], doc_ref[:, pl.ds(c * BLOCK, BLOCK)],
            first, count, c * BLOCK, BLOCK,
        )

    def attend_block(q, c, n):
        slot = lax.rem(n, 2) if not isinstance(n, int) else n % 2
        first, count = key_window(c)
        keys, at = pl.ds(first, count), pl.ds(c * BLOCK, BLOCK)

        def free():
            store_q(q, c, slot).wait()
            store_mixed(q, c, slot).wait()

        if not isinstance(n, int) or n >= 2:
            free()
        w = sq[q].reshape(width, cols_q)
        q_ring[slot] = (project(normed[at, :], w) + bq_all[q]).astype(BF16)
        store_q(q, c, slot).start()
        for u in range(cols_q // hd):
            head = pl.ds(u * hd, hd)
            s = dot_t(kv_ref[keys, pl.ds(0, hd)], q_ring[slot, :, head]) * scale
            s = s + bias_ref[pl.ds(0, count), :]
            top = jnp.max(s, axis=0, keepdims=True)
            e = jnp.exp(s - top)
            total = jnp.sum(e, axis=0, keepdims=True)
            probs = (e * (1.0 / total)).astype(BF16)
            mixed_ring[slot, :, head] = project(vt[:, keys], probs).T.astype(BF16)
            lse_ref[pl.ds(q * (cols_q // hd) + u, 1), at] = top + jnp.log(total)
        store_mixed(q, c, slot).start()

    def own_plane(c):
        set_bias(c)
        attend_block(m, c, c)

    def other_planes(c):
        set_bias(c)

        def one(r, carry):
            attend_block(lax.rem(m + r, planes), c, blocks + c * (planes - 1) + r - 1)
            return carry

        lax.fori_loop(1, planes, one, 0)

    stream = [(w, r) for w in (0, 1) for r in (1, 2, 3)]

    def stage(s):
        if s < len(stream):
            w, r = stream[s]
            z_land(w, r).wait_recv()
            if w == 0:
                z_send_copy(1, r).start()
            for kind in (0, 1, 2):
                go_near(kind, w, r)
            ship(w, r, d)
        if 1 <= s <= len(stream):
            w, r = stream[s - 1]
            landed(0, w, r)
            go_near(5, w, r)
            go_near(3, w, r)
            ship(w, r, dx)
            landed(1, w, r)
            go_near(6, w, r)
            go_near(4, w, r)
            ship(w, r, dy)
            landed(2, w, r)
            ship(w, r, dc)
        if 2 <= s <= len(stream) + 1:
            w, r = stream[s - 2]
            landed(5, w, r)
            landed(6, w, r)
            go_near(7, w, r)
            ship(w, r, dxy)
            for kind in (3, 4):
                landed(kind, w, r)
                ship(w, r, landed_eighth[kind])
            landed(7, w, r)
            ship(w, r, landed_eighth[7])

    for r in (1, 2, 3):
        z_send_copy(0, r).start()
    for r in (1, 2, 3):
        bias_copy(r, m).start()

    loads[2].wait()

    def norm_strip(i, carry):
        at = rows_at(i * STRIP, STRIP)
        normed[at, :] = norm_rows(normed[at, :].astype(F32), gain_ref[...], shift_ref[...]).astype(BF16)
        return carry

    lax.fori_loop(0, seq // STRIP, norm_strip, 0)
    keep_normed = pltpu.make_async_copy(normed, normed_hbm, load_sem.at[2])
    keep_normed.start()
    for c in range(blocks):
        at = pl.ds(c * BLOCK, BLOCK)
        kv = project(normed[at, :], w_kv[...]) + kv_bias[...]
        kv_ref[at, :] = kv.astype(BF16)
        vt[:, at] = kv[:, hd:].T.astype(BF16)
    loads[3].wait()

    stage(0)
    own_plane(0)
    stage(1)
    own_plane(1)
    own_plane(2)
    stage(2)
    own_plane(3)
    for r in (1, 2, 3):
        bias_copy(r, mp_partner(m, r)).wait_recv()
    stage(3)
    stage(4)
    other_planes(0)
    stage(5)
    other_planes(1)
    stage(6)
    other_planes(2)
    stage(7)
    other_planes(3)

    for slot in (0, 1):
        store_q(m, 0, slot).wait()
        store_mixed(m, 0, slot).wait()
    for w, r in stream:
        z_send_copy(w, r).wait_send()
        for kind in range(8):
            near(kind, w, r, sent_eighth).wait_send()
    for r in (1, 2, 3):
        bias_copy(r, m).wait_send()
    rows_o = [c for v, c in shipped if v == 1]
    for c in [c for v, c in shipped if v == 0] + rows_o[-ring:]:
        c.wait()
    keep_normed.wait()
    loads[4].wait()
    loads[5].wait()


def gather_by_sum(shard):
    blank = jnp.zeros((lax.axis_size("mp"),) + shard.shape, F32)
    half = shard.astype(F32) * 0.5
    own = lax.dynamic_update_index_in_dim(blank, half, lax.axis_index("mp"), 0)
    return lax.psum(own, "mp") * 2.0


def attention_front(
    inputs, w_query, b_query, w_keyval, kv_bias, w_out, gain, shift, codes, docs
):
    dp, mp = lax.axis_size("dp"), lax.axis_size("mp")
    width, cols = w_query.shape
    rows = w_out.shape[0]
    seq = inputs.shape[0]
    hd = w_keyval.shape[1] // 2
    code_col, doc_row = codes.reshape(seq, 1), docs.reshape(1, seq)
    if (dp, mp) != (8, 4):
        all_query, all_out, all_bias = (
            gather_by_sum(a).astype(a.dtype) for a in (w_query, w_out, b_query)
        )
        normed = norm_rows(inputs.astype(F32), gain, shift).astype(BF16)
        keyval = (project(normed, w_keyval) + kv_bias).astype(BF16)
        queries = jnp.concatenate(
            [project(normed, all_query[i]) + all_bias[i] for i in range(mp)], 1
        ).astype(BF16)
        mixed, lse = attend(queries, keyval, code_col, doc_row)
        return all_query, all_out.reshape(-1, width), normed, queries, mixed, keyval, lse
    wq = w_query.reshape(dp, width // dp, cols)
    wo = w_out.reshape(dp, rows // dp, width)
    dma = pltpu.SemaphoreType.DMA
    vmem = pl.BlockSpec(memory_space=pltpu.VMEM)
    full_q, full_o = (mp,) + wq.shape, (mp,) + wo.shape
    heads = mp * cols // hd
    shape = jax.ShapeDtypeStruct
    out_q, out_o, normed, queries, mixed, keyval, lse = pl.pallas_call(
        functools.partial(front_kernel, heads),
        out_shape=(
            shape(full_q, BF16),
            shape(full_o, BF16),
            shape((seq, width), BF16),
            shape((seq, mp * cols), BF16),
            shape((seq, mp * cols), BF16),
            shape((seq, 2 * hd), BF16),
            shape((heads, seq), F32),
        ),
        in_specs=[HBM] * 3 + [vmem] * 7,
        out_specs=(HBM,) * 5 + (vmem,) * 2,
        scratch_shapes=[
            pltpu.VMEM(wq.shape[1:], BF16),
            pltpu.VMEM(wo.shape[1:], BF16),
            pltpu.VMEM(full_q, F32),
            pltpu.VMEM(full_o, F32),
            pltpu.VMEM(full_q, BF16),
            pltpu.VMEM((4,) + wo.shape[1:], BF16),
            pltpu.VMEM((seq, width), BF16),
            pltpu.VMEM((2, BLOCK, cols), BF16),
            pltpu.VMEM((2, BLOCK, cols), BF16),
            pltpu.VMEM((hd, seq), BF16),
            pltpu.VMEM((REACH * BLOCK, BLOCK), F32),
            pltpu.VMEM((mp, 1, cols), F32),
            dma((6,)),
            dma((3 * dp,)),
            dma((4,)),
            dma((2, 2)),
            dma((2, 3)),
            dma((2, 3)),
            dma((3,)),
            dma((3,)),
            dma((8, 2, 3)),
            dma((8, 2, 3)),
        ],
        compiler_params=pltpu.CompilerParams(
            collective_id=0, has_side_effects=True, vmem_limit_bytes=VMEM_LIMIT
        ),
        name="attention_front",
    )(
        wq, wo, inputs, b_query.reshape(1, cols), w_keyval, gain.reshape(1, width),
        shift.reshape(1, width), kv_bias.reshape(1, 2 * hd), code_col, doc_row,
    )
    return (
        out_q.reshape(mp, width, cols), out_o.reshape(mp * rows, width),
        normed, queries, mixed, keyval, lse,
    )


PIECE = 32
CROSS_LATE = 2
LATE = 5
AHEAD = 3


class LineSum:
    scratch = staticmethod(
        lambda rows, width: [pltpu.VMEM((rows, width), F32)] * 3
        + [pltpu.SemaphoreType.DMA((rows // PIECE,))] * 5
    )

    def __init__(self, refs):
        self.part, self.total, self.cross, *sems = refs
        self.in_send, self.in_recv, self.over_send, self.over_recv, self.out_send = sems
        self.pieces = self.part.shape[0] // PIECE
        m = lax.axis_index("mp")
        self.is_end = (m == 0) | (m == 3)
        self.is_mid = (m == 1) | (m == 2)
        self.buddy = {"mp": mp_partner(m, 1)}
        self.across = {"mp": 3 - m}

    def greet(self, others=()):
        bar = pltpu.get_barrier_semaphore()
        pl.semaphore_signal(bar, inc=1, device_id=self.buddy, device_id_type=MESH)
        for other in others:
            pl.semaphore_signal(bar, inc=1, device_id=other, device_id_type=MESH)

        @pl.when(self.is_mid)
        def _():
            pl.semaphore_signal(bar, inc=1, device_id=self.across, device_id_type=MESH)

    def meet(self, others=()):
        bar = pltpu.get_barrier_semaphore()

        @pl.when(self.is_end)
        def _():
            pl.semaphore_wait(bar, 1 + len(others))

        @pl.when(self.is_mid)
        def _():
            pl.semaphore_wait(bar, 2 + len(others))

    def inward(self, k):
        at = rows_at(k * PIECE, PIECE)
        return pltpu.make_async_remote_copy(
            self.part.at[at], self.total.at[at], self.in_send.at[k], self.in_recv.at[k],
            device_id=self.buddy, device_id_type=MESH,
        )

    def over(self, k):
        at = rows_at(k * PIECE, PIECE)
        return pltpu.make_async_remote_copy(
            self.part.at[at], self.cross.at[at], self.over_send.at[k], self.over_recv.at[k],
            device_id=self.across, device_id_type=MESH,
        )

    def outward(self, k):
        at = rows_at(k * PIECE, PIECE)
        return pltpu.make_async_remote_copy(
            self.total.at[at], self.total.at[at], self.out_send.at[k], self.in_recv.at[k],
            device_id=self.buddy, device_id_type=MESH,
        )

    def tick(self, k):
        n = self.pieces

        @pl.when(self.is_end)
        def _():
            @pl.when(k < n)
            def _():
                @pl.when(k >= AHEAD)
                def _():
                    self.inward(k - AHEAD).wait_send()

                self.inward(k).start()

            @pl.when((k >= LATE) & (k < n + LATE))
            def _():
                self.outward(k - LATE).wait_recv()

        @pl.when(self.is_mid)
        def _():
            @pl.when(k < n)
            def _():
                at = rows_at(k * PIECE, PIECE)
                self.inward(k).wait_recv()
                self.part[at, :] += self.total[at, :]
                self.over(k).start()

            @pl.when((k >= CROSS_LATE) & (k < n + CROSS_LATE))
            def _():
                j = k - CROSS_LATE
                at = rows_at(j * PIECE, PIECE)
                self.over(j).wait_recv()
                self.total[at, :] = self.part[at, :] + self.cross[at, :]
                self.outward(j).start()

    def finish(self):
        n = self.pieces

        @pl.when(self.is_end)
        def _():
            for k in range(n - AHEAD, n):
                self.inward(k).wait_send()

        @pl.when(self.is_mid)
        def _():
            def sent(k, c):
                self.over(k).wait_send()
                self.outward(k).wait_send()
                return c

            lax.fori_loop(0, n, sent, 0)


def attend_kernel(seq, heads, q_ref, kv_ref, vt_ref, code_ref, doc_ref, mixed_ref, lse_ref, bias_ref):
    hd = vt_ref.shape[0]
    scale = 1.0 / math.sqrt(hd)
    for c in range(seq // BLOCK):

        @pl.when(pl.program_id(0) == c)
        def _(c=c):
            first, count = key_window(c)
            keys = pl.ds(first, count)
            bias_ref[pl.ds(0, count), :] = mask_bias(
                code_ref[keys, :], doc_ref[...], first, count, c * BLOCK, BLOCK
            )

            def some_heads(g, carry):
                for u in range(GROUP):
                    h = g * GROUP + u
                    cols = pl.ds(pl.multiple_of(h * hd, hd), hd)
                    s = dot_t(kv_ref[keys, pl.ds(0, hd)], q_ref[:, cols]) * scale
                    s = s + bias_ref[pl.ds(0, count), :]
                    top = jnp.max(s, axis=0, keepdims=True)
                    e = jnp.exp(s - top)
                    total = jnp.sum(e, axis=0, keepdims=True)
                    probs = (e * (1.0 / total)).astype(BF16)
                    mixed = project(vt_ref[:, keys], probs)
                    mixed_ref[:, cols] = mixed.T.astype(BF16)
                    lse_ref[pl.ds(h, 1), :] = top + jnp.log(total)
                return carry

            lax.fori_loop(0, heads // GROUP, some_heads, 0)


def attend(queries, keyval, code_col, doc_row):
    seq, width = queries.shape
    hd = keyval.shape[1] // 2
    heads = width // hd
    values_t = keyval[:, hd:].T
    whole = lambda *shape: pl.BlockSpec(shape, lambda c: (0,) * len(shape))
    return pl.pallas_call(
        functools.partial(attend_kernel, seq, heads),
        grid=(seq // BLOCK,),
        out_shape=(
            jax.ShapeDtypeStruct((seq, width), BF16),
            jax.ShapeDtypeStruct((heads, seq), F32),
        ),
        in_specs=[
            pl.BlockSpec((BLOCK, width), lambda c: (c, 0)),
            whole(seq, 2 * hd),
            whole(hd, seq),
            whole(seq, 1),
            pl.BlockSpec((1, BLOCK), lambda c: (0, c)),
        ],
        out_specs=(
            pl.BlockSpec((BLOCK, width), lambda c: (c, 0)),
            pl.BlockSpec((heads, BLOCK), lambda c: (0, c)),
        ),
        scratch_shapes=[pltpu.VMEM((REACH * BLOCK, BLOCK), F32)],
        compiler_params=pltpu.CompilerParams(vmem_limit_bytes=VMEM_LIMIT),
        name="attend",
    )(queries, keyval, values_t, code_col, doc_row)


def norm_back_rows(x, grad, gain):
    mean = jnp.mean(x, axis=-1, keepdims=True)
    center = x - mean
    scale = lax.rsqrt(jnp.mean(center * center, axis=-1, keepdims=True) + EPS)
    xhat = center * scale
    e = grad * gain
    weighted = grad * xhat
    d_in = scale * (
        e - jnp.mean(e, axis=-1, keepdims=True) - xhat * jnp.mean(e * xhat, axis=-1, keepdims=True)
    )
    return d_in, weighted


def fold_rows(x):
    return jnp.sum(x.reshape(-1, 8, x.shape[-1]), axis=0)


def mlp_attend_back_kernel(
    heads,
    dh_hbm, w_up_hbm, w_out_hbm, mid_hbm, cot_hbm, q_hbm,
    kv_ref, kt_ref, code_ref, doc_ref, lse_ref, gain_ref,
    d_mid_hbm, d_branch_hbm, dq_hbm, dkv_ref, sums_ref,
    w_up, w_out, dh, mid, cot, q, d_branch, d_mixed, dq, bias_ref, load_sem, out_sem, *line_refs,
):
    line = LineSum(line_refs)
    seq, width = line.part.shape
    hd = kt_ref.shape[0]
    chunks = seq // BLOCK
    pieces = BLOCK // PIECE
    count = REACH * BLOCK
    scale = 1.0 / math.sqrt(hd)

    def load(i, src, dst):
        return pltpu.make_async_copy(src, dst, load_sem.at[i])

    def load_dh(c):
        return load(2, dh_hbm.at[rows_at(c * BLOCK, BLOCK)], dh)

    def load_chunk(c):
        at = rows_at(c * BLOCK, BLOCK)
        return [
            load(3, mid_hbm.at[at], mid),
            load(4, cot_hbm.at[at], cot),
            load(5, q_hbm.at[at], q),
        ]

    def store(i, src, dst, c):
        return pltpu.make_async_copy(src, dst.at[rows_at(c * BLOCK, BLOCK)], out_sem.at[i])

    def stores(c, which=(0, 1, 2)):
        pairs = ((mid, d_mid_hbm), (d_branch, d_branch_hbm), (dq, dq_hbm))
        return [store(i, *pairs[i], c) for i in which]

    load(0, w_up_hbm, w_up).start()
    load_dh(0).start()
    load(1, w_out_hbm, w_out).start()
    line.greet()
    dkv_ref[...] = jnp.zeros_like(dkv_ref)
    sums_ref[...] = jnp.zeros_like(sums_ref)

    def produce(c):
        at = rows_at(c * BLOCK, BLOCK)
        load_dh(c).wait()

        def cols(n, carry):
            there = rows_at(n * COLS, COLS)
            line.part[at, there] = dot_t(dh[...], w_up[there, :])
            return carry

        lax.fori_loop(0, width // COLS, cols, 0)

        @pl.when(c + 1 < chunks)
        def _():
            load_dh(c + 1).start()

    def norm_step(c, half):
        def strip(i, carry):
            row = half * (BLOCK // 2) + i * STRIP
            at = rows_at(row, STRIP)
            grad = line.total[rows_at(c * BLOCK + row, STRIP), :]
            d_in, weighted = norm_back_rows(mid[at, :], grad, gain_ref[...])
            d_mid = cot[at, :].astype(F32) + d_in
            low = d_mid.astype(BF16)
            mid[at, :] = d_mid
            d_branch[at, :] = low
            sums_ref[0] += fold_rows(weighted)
            sums_ref[1] += fold_rows(grad)
            sums_ref[2] += fold_rows(low.astype(F32))
            return carry

        lax.fori_loop(0, BLOCK // 2 // STRIP, strip, 0)

    def mixed_step(c):
        def cols(n, carry):
            there = rows_at(n * COLS, COLS)
            d_mixed[:, there] = dot_t(d_branch[...], w_out[there, :]).astype(BF16)
            return carry

        lax.fori_loop(0, width // COLS, cols, 0)
        keys = pl.ds(pl.multiple_of(c * BLOCK, BLOCK), count)
        bias_ref[...] = mask_bias(
            code_ref[keys, :], doc_ref[:, rows_at(c * BLOCK, BLOCK)],
            (c - REACH + 1) * BLOCK, count, c * BLOCK, BLOCK,
        )

    def heads_step(c, g):
        keys = pl.ds(pl.multiple_of(c * BLOCK, BLOCK), count)
        queries = rows_at(c * BLOCK, BLOCK)
        dk = jnp.zeros((count, hd), F32)
        dv = jnp.zeros((count, hd), F32)
        for u in range(GROUP):
            h = g * GROUP + u
            cols = rows_at(h * hd, hd)
            qh = q[:, cols]
            dm = d_mixed[:, cols]
            s = dot_t(kv_ref[keys, pl.ds(0, hd)], qh) * scale + bias_ref[...]
            probs = jnp.exp(s - lse_ref[pl.ds(h, 1), queries])
            d_probs = dot_t(kv_ref[keys, pl.ds(hd, hd)], dm)
            t = probs * d_probs
            inner = jnp.sum(t, axis=0, keepdims=True)
            ds = (t - probs * inner).astype(BF16)
            dqh = project(kt_ref[:, keys], ds) * scale
            dq[:, cols] = dqh.T.astype(BF16)
            dk = dk + project(ds, qh)
            dv = dv + project(probs.astype(BF16), dm)
        dkv_ref[keys, pl.ds(0, hd)] += dk * scale
        dkv_ref[keys, pl.ds(hd, hd)] += dv

    load(0, w_up_hbm, w_up).wait()
    produce(0)
    line.meet()
    for k in range(3):
        line.tick(k)
    load(1, w_out_hbm, w_out).wait()

    def cycle(u, carry):
        c = u - 1
        base = u * pieces + 3

        @pl.when(u >= 2)
        def _():
            for i in stores(u - 2):
                i.wait()

        @pl.when(u >= 1)
        def _():
            for i in load_chunk(c):
                i.start()

        line.tick(base)

        @pl.when(u + 1 < chunks)
        def _():
            produce(u + 1)

        line.tick(base + 1)

        @pl.when(u >= 1)
        def _():
            for i in load_chunk(c):
                i.wait()
            norm_step(c, 0)

        line.tick(base + 2)

        @pl.when(u >= 1)
        def _():
            norm_step(c, 1)
            for i in stores(c, (0, 1)):
                i.start()

        line.tick(base + 3)

        @pl.when(u >= 1)
        def _():
            mixed_step(c)

        def some_heads(g, carry):
            line.tick(base + 4 + g)

            @pl.when(u >= 1)
            def _():
                heads_step(c, g)

            return carry

        lax.fori_loop(0, heads // GROUP, some_heads, 0)

        @pl.when(u >= 1)
        def _():
            stores(c, (2,))[0].start()

        return carry

    lax.fori_loop(0, chunks + 1, cycle, 0)
    for i in stores(chunks - 1):
        i.wait()
    line.finish()


def padded_keys(keyval):
    return jnp.pad(keyval, (((REACH - 1) * BLOCK, 0), (0, 0)))


def mlp_attend_back(d_hidden, w_up, w_out, middle, cotangent, queries, keyval, codes, docs, lse, gain):
    seq, width = queries.shape
    hd = keyval.shape[1] // 2
    heads = width // hd
    front = (REACH - 1) * BLOCK
    kv = padded_keys(keyval)
    code_col = jnp.pad(codes, (front, 0), constant_values=-2).reshape(-1, 1)
    vmem = pl.BlockSpec(memory_space=pltpu.VMEM)
    dma = pltpu.SemaphoreType.DMA
    block = lambda dtype: pltpu.VMEM((BLOCK, width), dtype)
    d_middle, d_branch, d_queries, d_kv, sums = pl.pallas_call(
        functools.partial(mlp_attend_back_kernel, heads),
        out_shape=(
            jax.ShapeDtypeStruct((seq, width), F32),
            jax.ShapeDtypeStruct((seq, width), BF16),
            jax.ShapeDtypeStruct((seq, width), BF16),
            jax.ShapeDtypeStruct(kv.shape, F32),
            jax.ShapeDtypeStruct((3, 8, width), F32),
        ),
        in_specs=[HBM] * 6 + [vmem] * 6,
        out_specs=(HBM, HBM, HBM, vmem, vmem),
        scratch_shapes=[
            pltpu.VMEM(w_up.shape, BF16),
            pltpu.VMEM(w_out.shape, BF16),
            pltpu.VMEM((BLOCK, d_hidden.shape[1]), BF16),
            block(F32),
            block(BF16),
            block(BF16),
            block(BF16),
            block(BF16),
            block(BF16),
            pltpu.VMEM((REACH * BLOCK, BLOCK), F32),
            dma((6,)),
            dma((3,)),
        ]
        + LineSum.scratch(seq, width),
        compiler_params=pltpu.CompilerParams(
            collective_id=1, has_side_effects=True, vmem_limit_bytes=VMEM_LIMIT
        ),
        cost_estimate=pl.CostEstimate(
            flops=200 * 10**9, bytes_accessed=2**25, transcendentals=0
        ),
        name="mlp_attend_back",
    )(
        d_hidden, w_up, w_out, middle, cotangent, queries,
        kv, kv[:, :hd].T, code_col, docs.reshape(1, seq), lse, gain.reshape(1, width),
    )
    return d_middle, d_branch, d_queries, d_kv[front:], jnp.sum(sums, axis=1)


def feed_kernel(
    rounds,
    acts_hbm, w_down_hbm, mid_hbm, dq_hbm, w_q_hbm, in_hbm, d_mid_hbm,
    dkv_ref, w_kv_ref, gain_ref, bias_ref,
    out_hbm, in_grad_hbm, sums_ref,
    w_down, w_q, acts, mid, dq, xs, d_mid, spread, low, in_grad, trade, trade_in,
    load_sem, out_sem, t_send, t_recv, *line_refs,
):
    line = LineSum(line_refs)
    seq, width = line.part.shape
    chunks = seq // BLOCK
    pieces = BLOCK // PIECE
    planes, _, cols_q = w_q.shape
    m = lax.axis_index("mp")
    d = lax.axis_index("dp")
    peers = [{"dp": flip_bit(d, 1 << r)} for r in range(rounds)]

    def load(i, src, dst):
        return pltpu.make_async_copy(src, dst, load_sem.at[i])

    def load_feed(c):
        at = rows_at(c * BLOCK, BLOCK)
        return [load(2, acts_hbm.at[at], acts), load(3, mid_hbm.at[at], mid)]

    def load_grad(c):
        at = rows_at(c * BLOCK, BLOCK)
        return [
            load(4, dq_hbm.at[at], dq),
            load(5, in_hbm.at[at], xs),
            load(6, d_mid_hbm.at[at], d_mid),
        ]

    def store(i, src, dst, c):
        return pltpu.make_async_copy(src, dst.at[rows_at(c * BLOCK, BLOCK)], out_sem.at[i])

    load(0, w_down_hbm, w_down).start()
    for i in load_feed(0):
        i.start()
    load(1, w_q_hbm, w_q).start()
    line.greet(peers)
    sums_ref[...] = jnp.zeros_like(sums_ref)

    def produce(c):
        at = rows_at(c * BLOCK, BLOCK)
        for i in load_feed(c):
            i.wait()

        def cols(n, carry):
            there = rows_at(n * COLS, COLS)
            line.part[at, there] = project(acts[...], w_down[:, there])
            return carry

        lax.fori_loop(0, width // COLS, cols, 0)

        @pl.when(m == 0)
        def _():
            line.part[at, :] += mid[...]

        @pl.when(c + 1 < chunks)
        def _():
            for i in load_feed(c + 1):
                i.start()

    def output_step(c):
        def strip(i, carry):
            at = rows_at(i * STRIP, STRIP)
            there = rows_at(c * BLOCK + i * STRIP, STRIP)
            low[at, :] = (line.total[there, :] + bias_ref[...]).astype(BF16)
            return carry

        lax.fori_loop(0, BLOCK // STRIP, strip, 0)

    def spread_step(c):
        rows = rows_at(c * BLOCK, BLOCK)

        def cols(n, carry):
            there = rows_at(n * COLS, COLS)
            total = dot_t(dkv_ref[rows, :], w_kv_ref[there, :])
            for i in range(planes):
                total = total + dot_t(dq[:, pl.ds(i * cols_q, cols_q)], w_q[i, there, :])
            spread[:, there] = total
            return carry

        lax.fori_loop(0, width // COLS, cols, 0)

    def norm_step(c, half):
        def strip(i, carry):
            at = rows_at(half * (BLOCK // 2) + i * STRIP, STRIP)
            grad = spread[at, :]
            d_in, weighted = norm_back_rows(xs[at, :].astype(F32), grad, gain_ref[...])
            in_grad[at, :] = (d_mid[at, :] + d_in).astype(BF16)
            sums_ref[0] += fold_rows(weighted)
            sums_ref[1] += fold_rows(grad)
            return carry

        lax.fori_loop(0, BLOCK // 2 // STRIP, strip, 0)

    def swap(r):
        return pltpu.make_async_remote_copy(
            trade.at[r], trade_in.at[r], t_send.at[r], t_recv.at[r],
            device_id=peers[r], device_id_type=MESH,
        )

    load(0, w_down_hbm, w_down).wait()
    produce(0)
    line.meet(peers)
    for k in range(3):
        line.tick(k)
    load(1, w_q_hbm, w_q).wait()

    def cycle(u, carry):
        c = u - 1
        base = u * pieces + 3

        @pl.when(u < chunks)
        def _():
            for i in load_grad(u):
                i.start()

        line.tick(base)

        @pl.when(u + 1 < chunks)
        def _():
            produce(u + 1)

        line.tick(base + 1)

        @pl.when(u >= 1)
        def _():
            @pl.when(u >= 2)
            def _():
                store(0, low, out_hbm, u - 2).wait()

            output_step(c)
            store(0, low, out_hbm, c).start()

        line.tick(base + 2)

        @pl.when(u < chunks)
        def _():
            for i in load_grad(u):
                i.wait()
            spread_step(u)

        line.tick(base + 3)
        line.tick(base + 4)

        @pl.when(u < chunks)
        def _():
            @pl.when(u >= 1)
            def _():
                store(1, in_grad, in_grad_hbm, u - 1).wait()

            norm_step(u, 0)

        line.tick(base + 5)
        line.tick(base + 6)

        @pl.when(u < chunks)
        def _():
            norm_step(u, 1)
            store(1, in_grad, in_grad_hbm, u).start()

        line.tick(base + 7)

        @pl.when(u == chunks - 1)
        def _():
            trade[0, 0:8] = sums_ref[0]
            trade[0, 8:16] = sums_ref[1]
            for r in range(rounds):
                swap(r).start()
                swap(r).wait()
                trade[r + 1] = trade[r] + trade_in[r]
            sums_ref[0] = trade[rounds, 0:8]
            sums_ref[1] = trade[rounds, 8:16]

        return carry

    lax.fori_loop(0, chunks + 1, cycle, 0)
    store(0, low, out_hbm, chunks - 1).wait()
    store(1, in_grad, in_grad_hbm, chunks - 1).wait()
    line.finish()


def feed_and_input_grad(
    acts, w_down, middle, b_down, d_queries, all_query, d_keyval, w_keyval, inputs, d_middle, gain
):
    seq, width = inputs.shape
    rounds = (lax.axis_size("dp") - 1).bit_length()
    vmem = pl.BlockSpec(memory_space=pltpu.VMEM)
    dma = pltpu.SemaphoreType.DMA
    block = lambda dtype: pltpu.VMEM((BLOCK, width), dtype)
    outputs, input_grad, sums = pl.pallas_call(
        functools.partial(feed_kernel, rounds),
        out_shape=(
            jax.ShapeDtypeStruct((seq, width), BF16),
            jax.ShapeDtypeStruct((seq, width), BF16),
            jax.ShapeDtypeStruct((2, 8, width), F32),
        ),
        in_specs=[HBM] * 7 + [vmem] * 4,
        out_specs=(HBM, HBM, vmem),
        scratch_shapes=[
            pltpu.VMEM(w_down.shape, BF16),
            pltpu.VMEM(all_query.shape, BF16),
            pltpu.VMEM((BLOCK, acts.shape[1]), BF16),
            block(F32),
            block(BF16),
            block(BF16),
            block(F32),
            block(F32),
            block(BF16),
            block(BF16),
            pltpu.VMEM((rounds + 1, 16, width), F32),
            pltpu.VMEM((rounds, 16, width), F32),
            dma((7,)),
            dma((2,)),
            dma((rounds,)),
            dma((rounds,)),
        ]
        + LineSum.scratch(seq, width),
        compiler_params=pltpu.CompilerParams(
            collective_id=2, has_side_effects=True, vmem_limit_bytes=VMEM_LIMIT
        ),
        cost_estimate=pl.CostEstimate(
            flops=200 * 10**9, bytes_accessed=2**25, transcendentals=0
        ),
        name="feed_and_input_grad",
    )(
        acts, w_down, middle, d_queries, all_query, inputs, d_middle,
        d_keyval, w_keyval, gain.reshape(1, width), b_down.reshape(1, width),
    )
    return outputs, input_grad, jnp.sum(sums, axis=1)


def sum_packed(table, vectors):
    width = table.shape[1]
    rows = [jnp.pad(v, (0, width - v.shape[0])).reshape(1, width) for v in vectors]
    total = lax.psum(jnp.concatenate([table] + rows, 0), "dp")
    head = table.shape[0]
    return total[:head], [total[head + i, : v.shape[0]] for i, v in enumerate(vectors)]


def shards(
    inputs,
    doc_ids,
    pad_mask,
    attn_gain,
    attn_shift,
    w_query,
    b_query,
    w_keyval,
    b_value,
    w_out,
    b_out,
    mlp_gain,
    mlp_shift,
    w_up,
    b_up,
    w_down,
    b_down,
    cotangent,
):
    seq = doc_ids.shape[1]
    hd = b_value.shape[0]
    width = inputs.shape[1]
    own_cols = w_query.shape[1]
    own = lax.axis_index("mp") * own_cols
    inputs_f = inputs.astype(F32)
    bias_full = jnp.concatenate([jnp.zeros((hd,), F32), b_value])
    docs = doc_ids[0]
    codes = jnp.where(pad_mask[0] == 1, docs, -1)

    all_query, all_out, normed_attn, queries, mixed, keyval, lse = attention_front(
        inputs, w_query, b_query, w_keyval, bias_full, w_out, attn_gain, attn_shift, codes, docs
    )
    middle = inputs_f + project(mixed, all_out) + b_out
    normed_mlp = norm_rows(middle, mlp_gain, mlp_shift).astype(BF16)
    hidden = project(normed_mlp, w_up) + b_up
    acts = jax.nn.gelu(hidden, approximate=True).astype(BF16)
    grad_w_down = jnp.einsum("tf,td->fd", acts, cotangent, preferred_element_type=F32)
    grad_b_down = jnp.sum(cotangent.astype(F32), axis=0)
    d_acts = jnp.einsum("td,fd->tf", cotangent, w_down, preferred_element_type=F32)
    _, gelu_pull = jax.vjp(functools.partial(jax.nn.gelu, approximate=True), hidden)
    d_hidden = gelu_pull(d_acts)[0].astype(BF16)
    grad_b_up = jnp.sum(d_hidden.astype(F32), axis=0)
    grad_w_up = jnp.einsum("td,tf->df", normed_mlp, d_hidden, preferred_element_type=F32)
    d_hidden, grad_w_up, grad_w_down = lax.optimization_barrier((d_hidden, grad_w_up, grad_w_down))
    grad_w_up = lax.psum_scatter(grad_w_up, "dp", scatter_dimension=0, tiled=True)
    grad_w_down = lax.psum_scatter(grad_w_down, "dp", scatter_dimension=1, tiled=True)

    d_middle, d_branch, d_queries, d_keyval_sum, sums = mlp_attend_back(
        d_hidden, w_up, all_out, middle, cotangent, queries, keyval, codes, docs, lse, mlp_gain
    )
    d_keyval_sum, grad_w_down, grad_w_up = lax.optimization_barrier(
        (d_keyval_sum, grad_w_down, grad_w_up)
    )
    grad_mlp_gain, grad_mlp_shift, grad_b_out = sums[0], sums[1], sums[2]
    own_mixed = lax.dynamic_slice_in_dim(mixed, own, own_cols, 1)
    grad_w_out = jnp.einsum("tq,td->qd", own_mixed, d_branch, preferred_element_type=F32)
    grad_b_value = jnp.sum(d_keyval_sum[:, hd:], axis=0)
    d_keyval = d_keyval_sum.astype(BF16)
    own_d_queries = lax.dynamic_slice_in_dim(d_queries, own, own_cols, 1)
    grad_b_query = jnp.sum(own_d_queries.astype(F32), axis=0)
    grad_w_query = jnp.einsum("td,tq->dq", normed_attn, own_d_queries, preferred_element_type=F32)
    grad_w_keyval = jnp.einsum("tk,td->kd", d_keyval, normed_attn, preferred_element_type=F32)
    small = (
        grad_b_query,
        grad_b_value,
        grad_b_out,
        grad_mlp_gain,
        grad_mlp_shift,
        grad_b_up,
        grad_b_down,
    )
    acts, small, grad_w_keyval, grad_w_out, grad_w_query = lax.optimization_barrier(
        (acts, small, grad_w_keyval, grad_w_out, grad_w_query)
    )
    grad_w_out = lax.psum_scatter(grad_w_out, "dp", scatter_dimension=1, tiled=True)
    grad_w_query = lax.psum_scatter(grad_w_query, "dp", scatter_dimension=0, tiled=True)
    grad_w_keyval, small = sum_packed(grad_w_keyval, small)
    grad_w_keyval = grad_w_keyval.T
    grad_b_query, grad_b_value, grad_b_out, grad_mlp_gain, grad_mlp_shift, grad_b_up, grad_b_down = small
    outputs, input_grad, sums = feed_and_input_grad(
        acts, w_down, middle, b_down, d_queries, all_query, d_keyval, w_keyval, inputs, d_middle, attn_gain
    )
    grad_attn_gain, grad_attn_shift = sums[0], sums[1]
    return (
        outputs,
        input_grad,
        grad_attn_gain,
        grad_attn_shift,
        grad_w_query,
        grad_b_query,
        grad_w_keyval,
        grad_b_value,
        grad_w_out,
        grad_b_out,
        grad_mlp_gain,
        grad_mlp_shift,
        grad_w_up,
        grad_b_up,
        grad_w_down,
        grad_b_down,
    )


def solution(mesh):
    return jax.shard_map(
        shards,
        mesh=mesh,
        in_specs=(
            P("dp", None),
            P("dp", None),
            P("dp", None),
            P(),
            P(),
            P(None, "mp"),
            P("mp"),
            P(),
            P(),
            P("mp", None),
            P(),
            P(),
            P(),
            P(None, "mp"),
            P("mp"),
            P("mp", None),
            P(),
            P("dp", None),
        ),
        out_specs=(
            P("dp", None),
            P("dp", None),
            P(),
            P(),
            P("dp", "mp"),
            P("mp"),
            P(),
            P(),
            P("mp", "dp"),
            P(),
            P(),
            P(),
            P("dp", "mp"),
            P("mp"),
            P("mp", "dp"),
            P(),
        ),
        check_vma=False,
    )
```

```python
import functools
import math

import jax
import jax.numpy as jnp
from jax import lax
from jax.experimental import pallas as pl
from jax.experimental.pallas import tpu as pltpu
from jax.sharding import PartitionSpec as P

EPS = 1e-05
MESH = pl.DeviceIdType.MESH
F32 = jnp.float32
BF16 = jnp.bfloat16
VMEM_LIMIT = 60 * 2**20
HBM = pl.BlockSpec(memory_space=pl.ANY)


def norm_rows(rows_in, gain, shift):
    center = rows_in - jnp.mean(rows_in, axis=-1, keepdims=True)
    spread = jnp.mean(center * center, axis=-1, keepdims=True)
    return center * lax.rsqrt(spread + EPS) * gain + shift


def project(left, right):
    return jnp.dot(left, right, preferred_element_type=F32)


STRIP = 16
COLS = 512
BLOCK = 256
REACH = 3
GROUP = 4
NEG = -1e30
FRONT = (REACH - 1) * BLOCK


def key_window(c):
    first = max(0, c - REACH + 1) * BLOCK
    return first, (c + 1) * BLOCK - first


def mask_bias(code_col, doc_row, first_key, keys, first_query, queries):
    j = first_key + lax.broadcasted_iota(jnp.int32, (keys, queries), 0)
    i = first_query + lax.broadcasted_iota(jnp.int32, (keys, queries), 1)
    ok = ((j < i) & (code_col == doc_row)) | (j == i)
    return jnp.where(ok, 0.0, NEG)


def dot_t(a, b):
    return lax.dot_general(a, b, (((1,), (1,)), ((), ())), preferred_element_type=F32)


def rows_at(start, count):
    return pl.ds(pl.multiple_of(start, count), count)


def mp_partner(m, r):
    if r == 1:
        return m + 1 - 2 * lax.rem(m, 2)
    if r == 2:
        return m + 2 - 4 * lax.div(m, 2)
    return 3 - m


def flip_bit(d, bit):
    on = lax.rem(lax.div(d, bit), 2)
    return d + bit * (1 - 2 * on)


def front_kernel(
    heads,
    wq, wo, in_hbm, cot_hbm, w_down_hbm, bq, w_kv, gain_ref, shift_ref, bv_ref, code_ref, doc_ref,
    wq_out, wo_out, normed_hbm, q_hbm, mixed_hbm, d_acts_hbm, kv_ref, kt_ref, lse_ref,
    own_q, own_o, gq, go, sq, so, normed, q_ring, mixed_ring, vt, bias_ref, bq_all, cot, down, d_acts,
    load_sem, cot_sem, down_sem, d_acts_sem, ship_sem, o_sem, ring_sem, z_send, z_recv, b_send, b_recv, n_send, n_recv,
):
    m = lax.axis_index("mp")
    d = lax.axis_index("dp")
    dc, dx, dy = flip_bit(d, 1), flip_bit(d, 2), flip_bit(d, 4)
    dxy = flip_bit(dx, 4)
    is_mid = (m == 1) | (m == 2)
    buddy, across = {"mp": mp_partner(m, 1)}, {"mp": 3 - m}
    upper = lax.div(m, 2)
    inner = lax.rem(m + upper, 2)

    def plane_at(s):
        q = (1 - inner, 2, 3)[s]
        return q + upper * (3 - 2 * q)

    g = (gq, go)
    half = (gq.shape[2] // 2, go.shape[2] // 2)
    seq, width = normed.shape
    cols_q = q_ring.shape[2]
    hd = vt.shape[0]
    blocks = seq // BLOCK
    scale = 1.0 / math.sqrt(hd)
    planes = 4

    loads = [
        pltpu.make_async_copy(wq.at[d], own_q, load_sem.at[0]),
        pltpu.make_async_copy(wo.at[d], own_o, load_sem.at[1]),
        pltpu.make_async_copy(in_hbm, normed, load_sem.at[2]),
        pltpu.make_async_copy(wq, sq.at[m], load_sem.at[3]),
        pltpu.make_async_copy(wq, wq_out.at[m], load_sem.at[4]),
        pltpu.make_async_copy(wo, wo_out.at[m], load_sem.at[5]),
    ]
    for c in loads:
        c.start()
    bar = pltpu.get_barrier_semaphore()
    for r in (1, 2, 3):
        pl.semaphore_signal(bar, inc=1, device_id={"mp": mp_partner(m, r)}, device_id_type=MESH)
    for n in (dc, dx, dy):
        pl.semaphore_signal(bar, inc=1, device_id={"dp": n}, device_id_type=MESH)
    loads[0].wait()
    gq[m, d] = own_q[...].astype(F32)
    loads[1].wait()
    go[m, d] = own_o[...].astype(F32)
    bq_all[m] = bq[...]
    pl.semaphore_wait(bar, 6)

    def z_copy(w, plane, to, i):
        ref = g[w].at[plane, d]
        return pltpu.make_async_remote_copy(
            ref, ref, z_send.at[w, i], z_recv.at[w, plane], device_id=to, device_id_type=MESH
        )

    def z_own(w, wait=False):
        def go_or_wait(c):
            if wait:
                c.wait_send()
            else:
                c.start()

        go_or_wait(z_copy(w, m, buddy, 0))

        @pl.when(is_mid)
        def _():
            go_or_wait(z_copy(w, m, across, 1))

    def z_forward(w, s, wait=False):
        @pl.when(is_mid)
        def _():
            c = z_copy(w, plane_at(s), across if s == 0 else buddy, 2 + s)
            if wait:
                c.wait_send()
            else:
                c.start()

    def z_land(w, s):
        z_copy(w, plane_at(s), buddy, 0).wait_recv()

    def bias_copy(r, plane):
        return pltpu.make_async_remote_copy(
            bq_all.at[plane], bq_all.at[plane], b_send.at[r - 1], b_recv.at[r - 1],
            device_id={"mp": mp_partner(m, r)}, device_id_type=MESH,
        )

    sent_eighth = (d, d, d, dx, dy, dx, dy, dxy)
    landed_eighth = (dx, dy, dc, flip_bit(dx, 1), flip_bit(dy, 1), dxy, dxy, flip_bit(dxy, 1))
    sent_to = (dx, dy, dc, dc, dc, dy, dx, dc)

    def near(kind, w, r, eighths):
        q = plane_at(r)
        ref = g[w].at[q, eighths[kind]]
        if kind == 5:
            ref = g[w].at[q, eighths[kind], pl.ds(0, half[w])]
        if kind == 6:
            ref = g[w].at[q, eighths[kind], pl.ds(half[w], half[w])]
        return pltpu.make_async_remote_copy(
            ref, ref, n_send.at[kind, w, r], n_recv.at[kind, w, r],
            device_id={"dp": sent_to[kind]}, device_id_type=MESH,
        )

    def go_near(kind, w, r):
        near(kind, w, r, sent_eighth).start()

    def landed(kind, w, r):
        near(kind, w, r, landed_eighth).wait_recv()

    shipped = []
    ring = so.shape[0]

    def ship(w, r, eighth):
        q = plane_at(r)
        n = sum(1 for v, _ in shipped if v == w)
        if w == 0:
            sq[q, eighth] = gq[q, eighth].astype(BF16)
            c = pltpu.make_async_copy(sq.at[q, eighth], wq_out.at[q, eighth], ship_sem.at[n])
        else:
            slot = n % ring
            if n >= ring:
                [c for v, c in shipped if v == 1][n - ring].wait()
            so[slot] = go[q, eighth].astype(BF16)
            c = pltpu.make_async_copy(so.at[slot], wo_out.at[q, eighth], o_sem.at[slot])
        c.start()
        shipped.append((w, c))

    def store_q(q, c, slot):
        at = pl.ds(c * BLOCK, BLOCK)
        return pltpu.make_async_copy(
            q_ring.at[slot], q_hbm.at[at, rows_at(q * cols_q, cols_q)], ring_sem.at[0, slot]
        )

    def store_mixed(q, c, slot):
        at = pl.ds(c * BLOCK, BLOCK)
        return pltpu.make_async_copy(
            mixed_ring.at[slot], mixed_hbm.at[at, rows_at(q * cols_q, cols_q)], ring_sem.at[1, slot]
        )

    def set_bias(c):
        first, count = key_window(c)
        bias_ref[pl.ds(0, count), :] = mask_bias(
            code_ref[pl.ds(FRONT + first, count), :], doc_ref[:, pl.ds(c * BLOCK, BLOCK)],
            first, count, c * BLOCK, BLOCK,
        )

    def attend_block(q, c, n):
        slot = lax.rem(n, 2) if not isinstance(n, int) else n % 2
        first, count = key_window(c)
        keys, at = pl.ds(FRONT + first, count), pl.ds(c * BLOCK, BLOCK)

        def free():
            store_q(q, c, slot).wait()
            store_mixed(q, c, slot).wait()

        if not isinstance(n, int) or n >= 2:
            free()
        w = sq[q].reshape(width, cols_q)
        q_ring[slot] = (project(normed[at, :], w) + bq_all[q]).astype(BF16)
        store_q(q, c, slot).start()
        for u in range(cols_q // hd):
            head = pl.ds(u * hd, hd)
            s = dot_t(kv_ref[keys, pl.ds(0, hd)], q_ring[slot, :, head]) * scale
            s = s + bias_ref[pl.ds(0, count), :]
            top = jnp.max(s, axis=0, keepdims=True)
            e = jnp.exp(s - top)
            total = jnp.sum(e, axis=0, keepdims=True)
            probs = (e * (1.0 / total)).astype(BF16)
            mixed_ring[slot, :, head] = project(vt[:, pl.ds(first, count)], probs).T.astype(BF16)
            lse_ref[pl.ds(q * (cols_q // hd) + u, 1), at] = top + jnp.log(total)
        store_mixed(q, c, slot).start()

    bands = w_down_hbm.shape[0] // down.shape[1]

    def load_cot(i):
        at = rows_at(lax.rem(i, blocks) * BLOCK, BLOCK)
        slot = lax.rem(i, 2)
        return pltpu.make_async_copy(cot_hbm.at[at], cot.at[slot], cot_sem.at[slot])

    def load_down(n):
        at = pl.ds(n * down.shape[1], down.shape[1])
        return pltpu.make_async_copy(w_down_hbm.at[at], down.at[n % 2], down_sem.at[n % 2])

    def store_d_acts(n, i):
        slot = lax.rem(i, 2)
        rows = rows_at(lax.rem(i, blocks) * BLOCK, BLOCK)
        cols = pl.ds(n * down.shape[1], down.shape[1])
        return pltpu.make_async_copy(
            d_acts.at[slot], d_acts_hbm.at[rows, cols], d_acts_sem.at[slot]
        )

    def d_acts_band(n):
        load_down(n).wait()
        if n + 1 < bands:
            load_down(n + 1).start()

        def one(i, carry):
            slot = lax.rem(i, 2)
            load_cot(i).wait()

            @pl.when(i + 1 < bands * blocks)
            def _():
                load_cot(i + 1).start()

            @pl.when(i >= 2)
            def _():
                store_d_acts(n, i).wait()

            d_acts[slot] = dot_t(cot[slot], down[n % 2])
            store_d_acts(n, i).start()
            return carry

        lax.fori_loop(n * blocks, (n + 1) * blocks, one, 0)

    def own_plane(c):
        set_bias(c)
        attend_block(m, c, c)

    def other_planes(c, first, end):
        if first == 1:
            set_bias(c)

        def one(r, carry):
            attend_block(lax.rem(m + r, planes), c, blocks + c * (planes - 1) + r - 1)
            return carry

        lax.fori_loop(first, end, one, 0)

    stream = [(w, r) for w in (0, 1) for r in range(3)]

    def pass_on(i):
        w, s = stream[i]

        @pl.when(is_mid)
        def _():
            z_land(w, s)
            z_forward(w, s)

        if i == 2:
            z_own(1)

    def from_line(i):
        w, s = stream[i]

        @pl.when(jnp.logical_not(is_mid))
        def _():
            z_land(w, s)

        for kind in (0, 1, 2):
            go_near(kind, w, s)
        ship(w, s, d)

    def from_near(i):
        w, s = stream[i]
        landed(0, w, s)
        go_near(5, w, s)
        go_near(3, w, s)
        ship(w, s, dx)
        landed(1, w, s)
        go_near(6, w, s)
        go_near(4, w, s)
        ship(w, s, dy)
        landed(2, w, s)
        ship(w, s, dc)

    def from_far(i):
        w, s = stream[i]
        landed(5, w, s)
        landed(6, w, s)
        go_near(7, w, s)
        ship(w, s, dxy)
        for kind in (3, 4):
            landed(kind, w, s)
            ship(w, s, landed_eighth[kind])
        landed(7, w, s)
        ship(w, s, landed_eighth[7])

    z_own(0)
    for r in (1, 2, 3):
        bias_copy(r, m).start()

    load_down(0).start()
    load_cot(0).start()
    loads[2].wait()

    def norm_strip(i, carry):
        at = rows_at(i * STRIP, STRIP)
        normed[at, :] = norm_rows(normed[at, :].astype(F32), gain_ref[...], shift_ref[...]).astype(BF16)
        return carry

    lax.fori_loop(0, seq // STRIP, norm_strip, 0)
    keep_normed = pltpu.make_async_copy(normed, normed_hbm, load_sem.at[2])
    keep_normed.start()
    kv_ref[pl.ds(0, FRONT), :] = jnp.zeros((FRONT, 2 * hd), BF16)
    kt_ref[:, pl.ds(0, FRONT)] = jnp.zeros((hd, FRONT), BF16)
    for c in range(blocks):
        at, put = pl.ds(c * BLOCK, BLOCK), pl.ds(FRONT + c * BLOCK, BLOCK)
        kv = project(normed[at, :], w_kv[...])
        keys, values = kv[:, :hd], kv[:, hd:] + bv_ref[...]
        kv_ref[put, pl.ds(0, hd)] = keys.astype(BF16)
        kv_ref[put, pl.ds(hd, hd)] = values.astype(BF16)
        kt_ref[:, put] = keys.T.astype(BF16)
        vt[:, at] = values.T.astype(BF16)
    loads[3].wait()

    def stage(s):
        if s == 0:
            pass_on(0)
        if s + 1 < len(stream):
            pass_on(s + 1)
        if s < len(stream):
            from_line(s)
        if 1 <= s <= len(stream):
            from_near(s - 1)
        if s >= 2:
            from_far(s - 2)

    stage(0)
    own_plane(0)
    own_plane(1)
    stage(1)
    own_plane(2)
    own_plane(3)
    stage(2)
    for n in range(bands // 2):
        d_acts_band(n)
    stage(3)
    for n in range(bands // 2, bands):
        d_acts_band(n)
    for r in (1, 2, 3):
        bias_copy(r, mp_partner(m, r)).wait_recv()
    stage(4)
    other_planes(0, 1, planes)
    other_planes(1, 1, planes)
    from_line(5)
    other_planes(2, 1, 2)
    from_near(4)
    other_planes(2, 2, planes)
    from_far(3)
    other_planes(3, 1, 2)
    from_near(5)
    other_planes(3, 2, planes)
    from_far(4)
    from_far(5)

    for i in (0, 1):
        store_d_acts(0, i).wait()
    for slot in (0, 1):
        store_q(m, 0, slot).wait()
        store_mixed(m, 0, slot).wait()
    for w in (0, 1):
        z_own(w, wait=True)
    for w, r in stream:
        z_forward(w, r, wait=True)
        for kind in range(8):
            near(kind, w, r, sent_eighth).wait_send()
    for r in (1, 2, 3):
        bias_copy(r, m).wait_send()
    rows_o = [c for v, c in shipped if v == 1]
    for c in [c for v, c in shipped if v == 0] + rows_o[-ring:]:
        c.wait()
    keep_normed.wait()
    loads[4].wait()
    loads[5].wait()


def gather_by_sum(shard):
    blank = jnp.zeros((lax.axis_size("mp"),) + shard.shape, F32)
    half = shard.astype(F32) * 0.5
    own = lax.dynamic_update_index_in_dim(blank, half, lax.axis_index("mp"), 0)
    return lax.psum(own, "mp") * 2.0


def attention_front(
    inputs, w_query, b_query, w_keyval, b_value, w_out, gain, shift, code_col, doc_row, cotangent, w_down
):
    dp, mp = lax.axis_size("dp"), lax.axis_size("mp")
    width, cols = w_query.shape
    rows = w_out.shape[0]
    seq = inputs.shape[0]
    hd = w_keyval.shape[1] // 2
    if (dp, mp) != (8, 4):
        all_query, all_out, all_bias = (
            gather_by_sum(a).astype(a.dtype) for a in (w_query, w_out, b_query)
        )
        normed = norm_rows(inputs.astype(F32), gain, shift).astype(BF16)
        kv_bias = jnp.concatenate([jnp.zeros((hd,), F32), b_value])
        keyval = (project(normed, w_keyval) + kv_bias).astype(BF16)
        queries = jnp.concatenate(
            [project(normed, all_query[i]) + all_bias[i] for i in range(mp)], 1
        ).astype(BF16)
        mixed, lse = attend(queries, keyval, code_col[FRONT:], doc_row)
        keyval = jnp.pad(keyval, ((FRONT, 0), (0, 0)))
        keys_t = keyval[:, :hd].T
        d_acts = jnp.einsum("td,fd->tf", cotangent, w_down, preferred_element_type=F32)
        return all_query, all_out.reshape(-1, width), normed, queries, mixed, d_acts, keyval, keys_t, lse
    wq = w_query.reshape(dp, width // dp, cols)
    wo = w_out.reshape(dp, rows // dp, width)
    dma = pltpu.SemaphoreType.DMA
    vmem = pl.BlockSpec(memory_space=pltpu.VMEM)
    full_q, full_o = (mp,) + wq.shape, (mp,) + wo.shape
    heads = mp * cols // hd
    shape = jax.ShapeDtypeStruct
    out_q, out_o, normed, queries, mixed, d_acts, keyval, keys_t, lse = pl.pallas_call(
        functools.partial(front_kernel, heads),
        out_shape=(
            shape(full_q, BF16),
            shape(full_o, BF16),
            shape((seq, width), BF16),
            shape((seq, mp * cols), BF16),
            shape((seq, mp * cols), BF16),
            shape((seq, w_down.shape[0]), F32),
            shape((FRONT + seq, 2 * hd), BF16),
            shape((hd, FRONT + seq), BF16),
            shape((heads, seq), F32),
        ),
        in_specs=[HBM] * 5 + [vmem] * 7,
        out_specs=(HBM,) * 6 + (vmem,) * 3,
        scratch_shapes=[
            pltpu.VMEM(wq.shape[1:], BF16),
            pltpu.VMEM(wo.shape[1:], BF16),
            pltpu.VMEM(full_q, F32),
            pltpu.VMEM(full_o, F32),
            pltpu.VMEM(full_q, BF16),
            pltpu.VMEM((4,) + wo.shape[1:], BF16),
            pltpu.VMEM((seq, width), BF16),
            pltpu.VMEM((2, BLOCK, cols), BF16),
            pltpu.VMEM((2, BLOCK, cols), BF16),
            pltpu.VMEM((hd, seq), BF16),
            pltpu.VMEM((REACH * BLOCK, BLOCK), F32),
            pltpu.VMEM((mp, 1, cols), F32),
            pltpu.VMEM((2, BLOCK, width), BF16),
            pltpu.VMEM((2, COLS, width), BF16),
            pltpu.VMEM((2, BLOCK, COLS), F32),
            dma((6,)),
            dma((2,)),
            dma((2,)),
            dma((2,)),
            dma((3 * dp,)),
            dma((4,)),
            dma((2, 2)),
            dma((2, 5)),
            dma((2, mp)),
            dma((3,)),
            dma((3,)),
            dma((8, 2, 3)),
            dma((8, 2, 3)),
        ],
        compiler_params=pltpu.CompilerParams(
            collective_id=0, has_side_effects=True, vmem_limit_bytes=VMEM_LIMIT
        ),
        name="attention_front",
    )(
        wq, wo, inputs, cotangent, w_down, b_query.reshape(1, cols), w_keyval, gain.reshape(1, width),
        shift.reshape(1, width), b_value.reshape(1, hd), code_col, doc_row,
    )
    return (
        out_q.reshape(mp, width, cols), out_o.reshape(mp * rows, width),
        normed, queries, mixed, d_acts, keyval, keys_t, lse,
    )


PIECE = 32
SLOT = 1
CROSS_LATE = 2 * SLOT
LATE = 5 * SLOT
AHEAD = 3 * SLOT


class LineSum:
    scratch = staticmethod(
        lambda rows, pieces, width: [pltpu.VMEM((rows, width), F32)] * 3
        + [pltpu.SemaphoreType.DMA((pieces,))] * 5
    )

    def __init__(self, refs):
        self.part, self.total, self.cross, *sems = refs
        self.in_send, self.in_recv, self.over_send, self.over_recv, self.out_send = sems
        self.slots = self.part.shape[0] // PIECE
        self.pieces = self.in_send.shape[0]
        m = lax.axis_index("mp")
        self.is_end = (m == 0) | (m == 3)
        self.is_mid = (m == 1) | (m == 2)
        self.buddy = {"mp": mp_partner(m, 1)}
        self.across = {"mp": 3 - m}

    def greet(self, others=()):
        bar = pltpu.get_barrier_semaphore()
        pl.semaphore_signal(bar, inc=1, device_id=self.buddy, device_id_type=MESH)
        for other in others:
            pl.semaphore_signal(bar, inc=1, device_id=other, device_id_type=MESH)

        @pl.when(self.is_mid)
        def _():
            pl.semaphore_signal(bar, inc=1, device_id=self.across, device_id_type=MESH)

    def meet(self, others=()):
        bar = pltpu.get_barrier_semaphore()

        @pl.when(self.is_end)
        def _():
            pl.semaphore_wait(bar, 1 + len(others))

        @pl.when(self.is_mid)
        def _():
            pl.semaphore_wait(bar, 2 + len(others))

    def at(self, k):
        slot = k if self.slots == self.pieces else k % self.slots
        return rows_at(slot * PIECE, PIECE)

    def inward(self, k):
        at = self.at(k)
        return pltpu.make_async_remote_copy(
            self.part.at[at], self.total.at[at], self.in_send.at[k], self.in_recv.at[k],
            device_id=self.buddy, device_id_type=MESH,
        )

    def over(self, k):
        at = self.at(k)
        return pltpu.make_async_remote_copy(
            self.part.at[at], self.cross.at[at], self.over_send.at[k], self.over_recv.at[k],
            device_id=self.across, device_id_type=MESH,
        )

    def outward(self, k):
        at = self.at(k)
        return pltpu.make_async_remote_copy(
            self.total.at[at], self.total.at[at], self.out_send.at[k], self.in_recv.at[k],
            device_id=self.buddy, device_id_type=MESH,
        )

    def slot(self, i):
        for j in range(SLOT):
            self.tick(i * SLOT + j)

    def tick(self, k):
        n = self.pieces

        @pl.when(self.is_end)
        def _():
            @pl.when(k < n)
            def _():
                @pl.when(k >= AHEAD)
                def _():
                    self.inward(k - AHEAD).wait_send()

                self.inward(k).start()

            @pl.when((k >= LATE) & (k < n + LATE))
            def _():
                self.outward(k - LATE).wait_recv()

        @pl.when(self.is_mid)
        def _():
            @pl.when(k < n)
            def _():
                at = self.at(k)
                self.inward(k).wait_recv()
                self.part[at, :] += self.total[at, :]
                self.over(k).start()

            @pl.when((k >= CROSS_LATE) & (k < n + CROSS_LATE))
            def _():
                j = k - CROSS_LATE
                at = self.at(j)
                self.over(j).wait_recv()
                self.total[at, :] = self.part[at, :] + self.cross[at, :]
                self.outward(j).start()

    def free(self, first, count):
        @pl.when(self.is_mid)
        def _():
            def sent(k, c):
                self.over(k).wait_send()
                self.outward(k).wait_send()
                return c

            lax.fori_loop(first, first + count, sent, 0)

    def finish(self, freed=0):
        n = self.pieces

        @pl.when(self.is_end)
        def _():
            for k in range(n - AHEAD, n):
                self.inward(k).wait_send()

        self.free(freed, n - freed)


def attend_kernel(seq, heads, q_ref, kv_ref, vt_ref, code_ref, doc_ref, mixed_ref, lse_ref, bias_ref):
    hd = vt_ref.shape[0]
    scale = 1.0 / math.sqrt(hd)
    for c in range(seq // BLOCK):

        @pl.when(pl.program_id(0) == c)
        def _(c=c):
            first, count = key_window(c)
            keys = pl.ds(first, count)
            bias_ref[pl.ds(0, count), :] = mask_bias(
                code_ref[keys, :], doc_ref[...], first, count, c * BLOCK, BLOCK
            )

            def some_heads(g, carry):
                for u in range(GROUP):
                    h = g * GROUP + u
                    cols = pl.ds(pl.multiple_of(h * hd, hd), hd)
                    s = dot_t(kv_ref[keys, pl.ds(0, hd)], q_ref[:, cols]) * scale
                    s = s + bias_ref[pl.ds(0, count), :]
                    top = jnp.max(s, axis=0, keepdims=True)
                    e = jnp.exp(s - top)
                    total = jnp.sum(e, axis=0, keepdims=True)
                    probs = (e * (1.0 / total)).astype(BF16)
                    mixed = project(vt_ref[:, keys], probs)
                    mixed_ref[:, cols] = mixed.T.astype(BF16)
                    lse_ref[pl.ds(h, 1), :] = top + jnp.log(total)
                return carry

            lax.fori_loop(0, heads // GROUP, some_heads, 0)


def attend(queries, keyval, code_col, doc_row):
    seq, width = queries.shape
    hd = keyval.shape[1] // 2
    heads = width // hd
    values_t = keyval[:, hd:].T
    whole = lambda *shape: pl.BlockSpec(shape, lambda c: (0,) * len(shape))
    return pl.pallas_call(
        functools.partial(attend_kernel, seq, heads),
        grid=(seq // BLOCK,),
        out_shape=(
            jax.ShapeDtypeStruct((seq, width), BF16),
            jax.ShapeDtypeStruct((heads, seq), F32),
        ),
        in_specs=[
            pl.BlockSpec((BLOCK, width), lambda c: (c, 0)),
            whole(seq, 2 * hd),
            whole(hd, seq),
            whole(seq, 1),
            pl.BlockSpec((1, BLOCK), lambda c: (0, c)),
        ],
        out_specs=(
            pl.BlockSpec((BLOCK, width), lambda c: (c, 0)),
            pl.BlockSpec((heads, BLOCK), lambda c: (0, c)),
        ),
        scratch_shapes=[pltpu.VMEM((REACH * BLOCK, BLOCK), F32)],
        compiler_params=pltpu.CompilerParams(vmem_limit_bytes=VMEM_LIMIT),
        name="attend",
    )(queries, keyval, values_t, code_col, doc_row)


def norm_back_rows(x, grad, gain):
    mean = jnp.mean(x, axis=-1, keepdims=True)
    center = x - mean
    scale = lax.rsqrt(jnp.mean(center * center, axis=-1, keepdims=True) + EPS)
    xhat = center * scale
    e = grad * gain
    weighted = grad * xhat
    d_in = scale * (
        e - jnp.mean(e, axis=-1, keepdims=True) - xhat * jnp.mean(e * xhat, axis=-1, keepdims=True)
    )
    return d_in, weighted


def fold_rows(x):
    return jnp.sum(x.reshape(-1, 8, x.shape[-1]), axis=0)


def mlp_attend_back_kernel(
    heads,
    dh_hbm, w_up_hbm, w_out_hbm, mid_hbm, cot_hbm, q_hbm, acts_hbm, w_down_hbm,
    kv_ref, kt_ref, code_ref, doc_ref, lse_ref, gain_ref,
    d_mid_hbm, d_branch_hbm, dq_hbm, feed_hbm, dkv_ref, sums_ref,
    w_up, w_out, dh, mid, cot, q, d_branch, d_mixed, dq, bias_ref, load_sem, out_sem, *line_refs,
):
    line = LineSum(line_refs)
    seq, width = line.part.shape
    hd = kt_ref.shape[0]
    chunks = seq // BLOCK
    slots = BLOCK // (PIECE * SLOT)
    count = REACH * BLOCK
    scale = 1.0 / math.sqrt(hd)

    def load(i, src, dst):
        return pltpu.make_async_copy(src, dst, load_sem.at[i])

    def load_dh(c):
        return load(2, dh_hbm.at[rows_at(c * BLOCK, BLOCK)], dh)

    def load_chunk(c):
        at = rows_at(c * BLOCK, BLOCK)
        return [
            load(3, mid_hbm.at[at], mid),
            load(4, cot_hbm.at[at], cot),
            load(5, q_hbm.at[at], q),
        ]

    def store(i, src, dst, c):
        return pltpu.make_async_copy(src, dst.at[rows_at(c * BLOCK, BLOCK)], out_sem.at[i])

    def stores(c, which=(0, 1, 2)):
        pairs = ((mid, d_mid_hbm), (d_branch, d_branch_hbm), (dq, dq_hbm))
        return [store(i, *pairs[i], c) for i in which]

    load(0, w_up_hbm, w_up).start()
    load_dh(0).start()
    load(1, w_out_hbm, w_out).start()
    load_acts = load(2, acts_hbm.at[pl.ds(0, BLOCK)], dh)
    load_down = load(0, w_down_hbm, w_up)
    line.greet()
    dkv_ref[...] = jnp.zeros_like(dkv_ref)
    sums_ref[...] = jnp.zeros_like(sums_ref)

    def produce(c):
        at = rows_at(c * BLOCK, BLOCK)
        load_dh(c).wait()

        def cols(n, carry):
            there = rows_at(n * COLS, COLS)
            line.part[at, there] = dot_t(dh[...], w_up[there, :])
            return carry

        lax.fori_loop(0, width // COLS, cols, 0)

        @pl.when(c + 1 < chunks)
        def _():
            load_dh(c + 1).start()

        @pl.when(c + 1 == chunks)
        def _():
            load_acts.start()
            load_down.start()

    def produce_feed():
        at = pl.ds(0, BLOCK)
        load_acts.wait()
        load_down.wait()
        line.free(0, BLOCK // PIECE)

        def cols(n, carry):
            there = rows_at(n * COLS, COLS)
            line.part[at, there] = project(dh[...], w_up[:, there])
            return carry

        lax.fori_loop(0, width // COLS, cols, 0)

    def norm_step(c, half):
        def strip(i, carry):
            row = half * (BLOCK // 2) + i * STRIP
            at = rows_at(row, STRIP)
            grad = line.total[rows_at(c * BLOCK + row, STRIP), :]
            d_in, weighted = norm_back_rows(mid[at, :], grad, gain_ref[...])
            cot_rows = cot[at, :].astype(F32)
            d_mid = cot_rows + d_in
            low = d_mid.astype(BF16)
            mid[at, :] = d_mid
            d_branch[at, :] = low
            sums_ref[0] += fold_rows(weighted)
            sums_ref[1] += fold_rows(grad)
            sums_ref[2] += fold_rows(low.astype(F32))
            sums_ref[3] += fold_rows(cot_rows)
            return carry

        lax.fori_loop(0, BLOCK // 2 // STRIP, strip, 0)

    def mixed_step(c):
        def cols(n, carry):
            there = rows_at(n * COLS, COLS)
            d_mixed[:, there] = dot_t(d_branch[...], w_out[there, :]).astype(BF16)
            return carry

        lax.fori_loop(0, width // COLS, cols, 0)
        keys = pl.ds(pl.multiple_of(c * BLOCK, BLOCK), count)
        bias_ref[...] = mask_bias(
            code_ref[keys, :], doc_ref[:, rows_at(c * BLOCK, BLOCK)],
            (c - REACH + 1) * BLOCK, count, c * BLOCK, BLOCK,
        )

    def heads_step(c, g):
        keys = pl.ds(pl.multiple_of(c * BLOCK, BLOCK), count)
        queries = rows_at(c * BLOCK, BLOCK)
        dk = jnp.zeros((count, hd), F32)
        dv = jnp.zeros((count, hd), F32)
        for u in range(GROUP):
            h = g * GROUP + u
            cols = rows_at(h * hd, hd)
            qh = q[:, cols]
            dm = d_mixed[:, cols]
            s = dot_t(kv_ref[keys, pl.ds(0, hd)], qh) * scale + bias_ref[...]
            probs = jnp.exp(s - lse_ref[pl.ds(h, 1), queries])
            d_probs = dot_t(kv_ref[keys, pl.ds(hd, hd)], dm)
            t = probs * d_probs
            inner = jnp.sum(t, axis=0, keepdims=True)
            ds = (t - probs * inner).astype(BF16)
            dqh = project(kt_ref[:, keys], ds) * scale
            dq[:, cols] = dqh.T.astype(BF16)
            dk = dk + project(ds, qh)
            dv = dv + project(probs.astype(BF16), dm)
        dkv_ref[keys, pl.ds(0, hd)] += dk * scale
        dkv_ref[keys, pl.ds(hd, hd)] += dv

    load(0, w_up_hbm, w_up).wait()
    produce(0)
    line.meet()
    for k in range(3):
        line.slot(k)
    load(1, w_out_hbm, w_out).wait()

    def cycle(u, carry):
        c = u - 1
        base = u * slots + 3

        @pl.when(u >= 2)
        def _():
            for i in stores(u - 2):
                i.wait()

        @pl.when(u >= 1)
        def _():
            for i in load_chunk(c):
                i.start()

        line.slot(base)

        @pl.when(u + 1 < chunks)
        def _():
            produce(u + 1)

        @pl.when(u + 1 == chunks)
        def _():
            produce_feed()

        line.slot(base + 1)

        @pl.when(u >= 1)
        def _():
            for i in load_chunk(c):
                i.wait()
            norm_step(c, 0)

        line.slot(base + 2)

        @pl.when(u >= 1)
        def _():
            norm_step(c, 1)
            for i in stores(c, (0, 1)):
                i.start()

        line.slot(base + 3)

        @pl.when(u >= 1)
        def _():
            mixed_step(c)

        def some_heads(g, carry):
            line.slot(base + 4 + g)

            @pl.when(u >= 1)
            def _():
                heads_step(c, g)

            return carry

        lax.fori_loop(0, heads // GROUP, some_heads, 0)

        @pl.when(u >= 1)
        def _():
            stores(c, (2,))[0].start()

            def strip(i, carry):
                sums_ref[4] += fold_rows(dq[rows_at(i * STRIP, STRIP), :].astype(F32))
                return carry

            lax.fori_loop(0, BLOCK // STRIP, strip, 0)

        return carry

    lax.fori_loop(0, chunks + 1, cycle, 0)
    for k in range((chunks + 1) * slots + 3, (line.pieces + LATE) // SLOT):
        line.slot(k)
    keep_feed = pltpu.make_async_copy(line.total.at[pl.ds(0, BLOCK)], feed_hbm, out_sem.at[3])
    keep_feed.start()
    for i in stores(chunks - 1):
        i.wait()
    keep_feed.wait()
    line.finish(BLOCK // PIECE)


def mlp_attend_back(
    d_hidden, w_up, w_out, middle, cotangent, queries, acts, w_down,
    keyval, keys_t, code_col, doc_row, lse, gain,
):
    seq, width = queries.shape
    heads = width // keys_t.shape[0]
    vmem = pl.BlockSpec(memory_space=pltpu.VMEM)
    dma = pltpu.SemaphoreType.DMA
    block = lambda dtype: pltpu.VMEM((BLOCK, width), dtype)
    return pl.pallas_call(
        functools.partial(mlp_attend_back_kernel, heads),
        out_shape=(
            jax.ShapeDtypeStruct((seq, width), F32),
            jax.ShapeDtypeStruct((seq, width), BF16),
            jax.ShapeDtypeStruct((seq, width), BF16),
            jax.ShapeDtypeStruct((BLOCK, width), F32),
            jax.ShapeDtypeStruct(keyval.shape, F32),
            jax.ShapeDtypeStruct((5, 8, width), F32),
        ),
        in_specs=[HBM] * 8 + [vmem] * 6,
        out_specs=(HBM, HBM, HBM, HBM, vmem, vmem),
        scratch_shapes=[
            pltpu.VMEM(w_up.shape, BF16),
            pltpu.VMEM(w_out.shape, BF16),
            pltpu.VMEM((BLOCK, d_hidden.shape[1]), BF16),
            block(F32),
            block(BF16),
            block(BF16),
            block(BF16),
            block(BF16),
            block(BF16),
            pltpu.VMEM((REACH * BLOCK, BLOCK), F32),
            dma((6,)),
            dma((4,)),
        ]
        + LineSum.scratch(seq, (seq + BLOCK) // PIECE, width),
        compiler_params=pltpu.CompilerParams(
            collective_id=1, has_side_effects=True, vmem_limit_bytes=VMEM_LIMIT
        ),
        cost_estimate=pl.CostEstimate(
            flops=200 * 10**9, bytes_accessed=2**25, transcendentals=0
        ),
        name="mlp_attend_back",
    )(
        d_hidden, w_up, w_out, middle, cotangent, queries, acts, w_down,
        keyval, keys_t, code_col, doc_row, lse, gain.reshape(1, width),
    )


def feed_kernel(
    rounds,
    acts_hbm, w_down_hbm, mid_hbm, dq_hbm, w_q_hbm, in_hbm, d_mid_hbm, table_hbm,
    dkv_ref, w_kv_ref, gain_ref, bias_ref, sums_in, vectors_in,
    out_hbm, in_grad_hbm, table_out, vectors_out,
    w_down, w_q, acts, mid, dq, xs, d_mid, spread, low, in_grad, sums, trade, trade_in, table, table_in, table_all,
    load_sem, out_sem, t_send, t_recv, h_send, h_recv, d_send, d_recv, *line_refs,
):
    line = LineSum(line_refs)
    rows, width = line.part.shape
    seq = rows + BLOCK
    blocks = seq // BLOCK
    chunks = rows // BLOCK
    slots = BLOCK // (PIECE * SLOT)
    planes, _, cols_q = w_q.shape
    m = lax.axis_index("mp")
    d = lax.axis_index("dp")
    peers = [{"dp": flip_bit(d, 1 << r)} for r in range(rounds)]

    def load(i, src, dst):
        return pltpu.make_async_copy(src, dst, load_sem.at[i])

    def load_feed(c):
        at = rows_at((c + 1) * BLOCK, BLOCK)
        return [load(2, acts_hbm.at[at], acts), load(3, mid_hbm.at[at], mid)]

    def load_grad(c):
        at = rows_at(c * BLOCK, BLOCK)
        return [
            load(4, dq_hbm.at[at], dq),
            load(5, in_hbm.at[at], xs),
            load(6, d_mid_hbm.at[at], d_mid),
        ]

    def store(i, src, dst, c):
        return pltpu.make_async_copy(src, dst.at[rows_at(c * BLOCK, BLOCK)], out_sem.at[i])

    load_table = load(7, table_hbm, table)
    load(0, w_down_hbm, w_down).start()
    for i in load_feed(0):
        i.start()
    load_table.start()
    load(1, w_q_hbm, w_q).start()
    for i in load_grad(0):
        i.start()
    line.greet(peers)
    sums[...] = jnp.zeros_like(sums)

    def produce(c):
        at = rows_at(c * BLOCK, BLOCK)
        for i in load_feed(c):
            i.wait()

        def cols(n, carry):
            there = rows_at(n * COLS, COLS)
            line.part[at, there] = project(acts[...], w_down[:, there])
            return carry

        lax.fori_loop(0, width // COLS, cols, 0)

        @pl.when(m == 0)
        def _():
            line.part[at, :] += mid[...]

        @pl.when(c + 1 < chunks)
        def _():
            for i in load_feed(c + 1):
                i.start()

    def output_step(c):
        def strip(i, carry):
            at = rows_at(i * STRIP, STRIP)
            there = rows_at(c * BLOCK + i * STRIP, STRIP)
            low[at, :] = (line.total[there, :] + bias_ref[...]).astype(BF16)
            return carry

        lax.fori_loop(0, BLOCK // STRIP, strip, 0)

    def spread_step(c):
        here = rows_at(c * BLOCK, BLOCK)

        def cols(n, carry):
            there = rows_at(n * COLS, COLS)
            total = dot_t(dkv_ref[here, :], w_kv_ref[there, :])
            for i in range(planes):
                total = total + dot_t(dq[:, pl.ds(i * cols_q, cols_q)], w_q[i, there, :])
            spread[:, there] = total
            return carry

        lax.fori_loop(0, width // COLS, cols, 0)

    def norm_step(c, half):
        def strip(i, carry):
            at = rows_at(half * (BLOCK // 2) + i * STRIP, STRIP)
            grad = spread[at, :]
            d_in, weighted = norm_back_rows(xs[at, :].astype(F32), grad, gain_ref[...])
            in_grad[at, :] = (d_mid[at, :] + d_in).astype(BF16)
            sums[0] += fold_rows(weighted)
            sums[1] += fold_rows(grad)
            return carry

        lax.fori_loop(0, BLOCK // 2 // STRIP, strip, 0)

    def swap(r):
        return pltpu.make_async_remote_copy(
            trade.at[r], trade_in.at[r], t_send.at[r], t_recv.at[r],
            device_id=peers[r], device_id_type=MESH,
        )

    def vectors_first():
        trade[0] = jnp.zeros_like(trade.at[0])
        for i in range(2):
            trade[0, i : i + 1] = jnp.sum(sums[i], axis=0, keepdims=True)
        for i in range(sums_in.shape[0]):
            trade[0, 2 + i : 3 + i] = jnp.sum(sums_in[i], axis=0, keepdims=True)
        at = 2 + sums_in.shape[0]
        trade[0, at : at + vectors_in.shape[0]] = vectors_in[...]
        swap(0).start()

    def vectors_next(r):
        swap(r).wait()
        trade[r + 1] = trade[r] + trade_in[r]
        if r + 1 < rounds:
            swap(r + 1).start()
        else:
            vectors_out[...] = trade[r + 1]

    bits = [lax.rem(lax.div(d, 1 << r), 2) for r in range(rounds)]
    base = [0]
    size = [table.shape[0]]
    for r in range(rounds):
        size.append(size[r] // 2)
        base.append(base[r] + bits[r] * size[r + 1])

    def part_of(start, count):
        return pl.ds(pl.multiple_of(start, 8), count)

    def halve(r):
        away = part_of(base[r] + (1 - bits[r]) * size[r + 1], size[r + 1])
        into = pl.ds(size[0] - size[r], size[r + 1])
        return pltpu.make_async_remote_copy(
            table.at[away], table_in.at[into], h_send.at[r], h_recv.at[r],
            device_id=peers[r], device_id_type=MESH,
        )

    def double(r, mine):
        start = base[r] + (bits[r] if mine else 1 - bits[r]) * size[r + 1]
        at = part_of(start, size[r + 1])
        return pltpu.make_async_remote_copy(
            table_all.at[at], table_all.at[at], d_send.at[r], d_recv.at[r],
            device_id=peers[r], device_id_type=MESH,
        )

    store_table = pltpu.make_async_copy(table_all, table_out, out_sem.at[2])

    def table_step(i):
        if i == 0:
            load_table.wait()
        elif i <= rounds:
            r = i - 1
            halve(r).wait()
            at = part_of(base[r + 1], size[r + 1])
            whole = table_all if i == rounds else table
            whole[at, :] = table[at, :] + table_in[pl.ds(size[0] - size[r], size[r + 1]), :]
        else:
            r = 2 * rounds - i
            double(r, True).wait_send()
            double(r, False).wait_recv()
        if i < rounds:
            halve(i).start()
        elif i < 2 * rounds:
            double(2 * rounds - 1 - i, True).start()
        else:
            store_table.start()

    load(0, w_down_hbm, w_down).wait()
    produce(0)
    line.meet(peers)
    for k in range(3):
        line.slot(k)
    load(1, w_q_hbm, w_q).wait()

    def grads(u, first):
        v = 2 * u + (0 if first else 1)

        def one():
            @pl.when(v < blocks)
            def _():
                for i in load_grad(v):
                    i.wait()
                spread_step(v)

        def two():
            @pl.when(v < blocks)
            def _():
                @pl.when(v >= 1)
                def _():
                    store(1, in_grad, in_grad_hbm, v - 1).wait()

                norm_step(v, 0)

        def three():
            @pl.when(v < blocks)
            def _():
                norm_step(v, 1)
                store(1, in_grad, in_grad_hbm, v).start()

                @pl.when(v + 1 < blocks)
                def _():
                    for i in load_grad(v + 1):
                        i.start()

        return one, two, three

    def cycle(u, carry):
        c = u - 1
        base_tick = u * slots + 3

        def produce_step():
            @pl.when(u + 1 < chunks)
            def _():
                produce(u + 1)

        def out_step():
            @pl.when(u >= 1)
            def _():
                @pl.when(u >= 2)
                def _():
                    store(0, low, out_hbm, u - 2).wait()

                output_step(c)
                store(0, low, out_hbm, c).start()

        steps = [produce_step, out_step, *grads(u, True), *grads(u, False)]
        for i, step in enumerate(steps):
            line.slot(base_tick + i)
            for v in range(chunks + 1):
                at = v * slots + i
                extra = []
                if at % 2 == 0 and at // 2 <= 2 * rounds:
                    extra.append(functools.partial(table_step, at // 2))
                late = at - (blocks // 2) * slots
                if late == 0:
                    extra.append(vectors_first)
                elif 0 < late <= rounds:
                    extra.append(functools.partial(vectors_next, late - 1))
                if extra:

                    @pl.when(u == v)
                    def _(extra=extra):
                        for e in extra:
                            e()

            step()
        return carry

    lax.fori_loop(0, chunks + 1, cycle, 0)
    store(0, low, out_hbm, chunks - 1).wait()
    store(1, in_grad, in_grad_hbm, blocks - 1).wait()
    store_table.wait()
    line.finish()


def feed_and_input_grad(
    acts, w_down, middle, b_down, d_queries, all_query, d_keyval, w_keyval, inputs, d_middle, gain,
    table, sums, vectors,
):
    seq, width = inputs.shape
    rounds = (lax.axis_size("dp") - 1).bit_length()
    vmem = pl.BlockSpec(memory_space=pltpu.VMEM)
    dma = pltpu.SemaphoreType.DMA
    block = lambda dtype: pltpu.VMEM((BLOCK, width), dtype)
    rest = seq - BLOCK
    shape = jax.ShapeDtypeStruct
    return pl.pallas_call(
        functools.partial(feed_kernel, rounds),
        out_shape=(
            shape((rest, width), BF16),
            shape((seq, width), BF16),
            shape(table.shape, F32),
            shape((16, width), F32),
        ),
        in_specs=[HBM] * 8 + [vmem] * 6,
        out_specs=(HBM, HBM, HBM, vmem),
        scratch_shapes=[
            pltpu.VMEM(w_down.shape, BF16),
            pltpu.VMEM(all_query.shape, BF16),
            pltpu.VMEM((BLOCK, acts.shape[1]), BF16),
            block(F32),
            block(BF16),
            block(BF16),
            block(F32),
            block(F32),
            block(BF16),
            block(BF16),
            pltpu.VMEM((2, 8, width), F32),
            pltpu.VMEM((rounds + 1, 16, width), F32),
            pltpu.VMEM((rounds, 16, width), F32),
            pltpu.VMEM(table.shape, F32),
            pltpu.VMEM(table.shape, F32),
            pltpu.VMEM(table.shape, F32),
            dma((8,)),
            dma((3,)),
            dma((rounds,)),
            dma((rounds,)),
            dma((rounds,)),
            dma((rounds,)),
            dma((rounds,)),
            dma((rounds,)),
        ]
        + LineSum.scratch(rest, rest // PIECE, width),
        compiler_params=pltpu.CompilerParams(
            collective_id=2, has_side_effects=True, vmem_limit_bytes=VMEM_LIMIT
        ),
        cost_estimate=pl.CostEstimate(
            flops=200 * 10**9, bytes_accessed=2**25, transcendentals=0
        ),
        name="feed_and_input_grad",
    )(
        acts, w_down, middle, d_queries, all_query, inputs, d_middle, table,
        d_keyval, w_keyval, gain.reshape(1, width), b_down.reshape(1, width), sums, vectors,
    )


def shards(
    inputs,
    doc_ids,
    pad_mask,
    attn_gain,
    attn_shift,
    w_query,
    b_query,
    w_keyval,
    b_value,
    w_out,
    b_out,
    mlp_gain,
    mlp_shift,
    w_up,
    b_up,
    w_down,
    b_down,
    cotangent,
):
    seq = doc_ids.shape[1]
    hd = b_value.shape[0]
    width = inputs.shape[1]
    own_cols = w_query.shape[1]
    own = lax.axis_index("mp") * own_cols
    inputs_f = inputs.astype(F32)
    docs = doc_ids[0]
    codes = jnp.where(pad_mask[0] == 1, docs, -1)
    code_col = jnp.pad(codes, (FRONT, 0), constant_values=-2).reshape(-1, 1)
    doc_row = docs.reshape(1, seq)

    all_query, all_out, normed_attn, queries, mixed, d_acts, keyval, keys_t, lse = attention_front(
        inputs, w_query, b_query, w_keyval, b_value, w_out, attn_gain, attn_shift, code_col, doc_row,
        cotangent, w_down,
    )
    middle = inputs_f + project(mixed, all_out) + b_out
    normed_mlp = norm_rows(middle, mlp_gain, mlp_shift).astype(BF16)
    hidden = project(normed_mlp, w_up) + b_up
    acts = jax.nn.gelu(hidden, approximate=True).astype(BF16)
    grad_w_down = jnp.einsum("tf,td->fd", acts, cotangent, preferred_element_type=F32)
    _, gelu_pull = jax.vjp(functools.partial(jax.nn.gelu, approximate=True), hidden)
    d_hidden = gelu_pull(d_acts)[0].astype(BF16)
    grad_b_up = jnp.sum(d_hidden.astype(F32), axis=0)
    grad_w_up = jnp.einsum("td,tf->df", normed_mlp, d_hidden, preferred_element_type=F32)
    d_hidden, grad_w_up, grad_w_down = lax.optimization_barrier((d_hidden, grad_w_up, grad_w_down))
    grad_w_up = lax.psum_scatter(grad_w_up, "dp", scatter_dimension=0, tiled=True)
    grad_w_down = lax.psum_scatter(grad_w_down, "dp", scatter_dimension=1, tiled=True)

    d_middle, d_branch, d_queries, feed_first, d_keyval_sum, sums = mlp_attend_back(
        d_hidden, w_up, all_out, middle, cotangent, queries, acts, w_down,
        keyval, keys_t, code_col, doc_row, lse, mlp_gain,
    )
    d_keyval_sum, grad_w_down, grad_w_up = lax.optimization_barrier(
        (d_keyval_sum, grad_w_down, grad_w_up)
    )
    d_keyval_sum = d_keyval_sum[FRONT:]
    own_mixed = lax.dynamic_slice_in_dim(mixed, own, own_cols, 1)
    grad_w_out = jnp.einsum("tq,td->qd", own_mixed, d_branch, preferred_element_type=F32)
    grad_b_value = jnp.sum(d_keyval_sum[:, hd:], axis=0)
    d_keyval = d_keyval_sum.astype(BF16)
    own_d_queries = lax.dynamic_slice_in_dim(d_queries, own, own_cols, 1)
    grad_w_query = jnp.einsum("td,tq->dq", normed_attn, own_d_queries, preferred_element_type=F32)
    grad_w_keyval = jnp.einsum("tk,td->kd", d_keyval, normed_attn, preferred_element_type=F32)
    vectors = jnp.stack([grad_b_up, jnp.pad(grad_b_value, (0, width - hd))])
    vectors, grad_w_keyval, grad_w_out, grad_w_query = lax.optimization_barrier(
        (vectors, grad_w_keyval, grad_w_out, grad_w_query)
    )
    grad_w_out = lax.psum_scatter(grad_w_out, "dp", scatter_dimension=1, tiled=True)
    grad_w_query = lax.psum_scatter(grad_w_query, "dp", scatter_dimension=0, tiled=True)
    out_rest, input_grad, grad_w_keyval, totals = feed_and_input_grad(
        acts, w_down, middle, b_down, d_queries, all_query, d_keyval, w_keyval, inputs, d_middle, attn_gain,
        grad_w_keyval, sums, vectors,
    )
    out_first = (middle[:BLOCK] + feed_first + b_down).astype(BF16)
    outputs = jnp.concatenate([out_first, out_rest], 0)
    grad_w_keyval = grad_w_keyval.T
    grad_attn_gain, grad_attn_shift, grad_mlp_gain, grad_mlp_shift = (totals[i] for i in range(4))
    grad_b_out, grad_b_down, grad_b_query, grad_b_up = (totals[i] for i in range(4, 8))
    grad_b_query = lax.dynamic_slice_in_dim(grad_b_query, own, own_cols, 0)
    grad_b_value = totals[8, :hd]
    return (
        outputs,
        input_grad,
        grad_attn_gain,
        grad_attn_shift,
        grad_w_query,
        grad_b_query,
        grad_w_keyval,
        grad_b_value,
        grad_w_out,
        grad_b_out,
        grad_mlp_gain,
        grad_mlp_shift,
        grad_w_up,
        grad_b_up,
        grad_w_down,
        grad_b_down,
    )


def solution(mesh):
    return jax.shard_map(
        shards,
        mesh=mesh,
        in_specs=(
            P("dp", None),
            P("dp", None),
            P("dp", None),
            P(),
            P(),
            P(None, "mp"),
            P("mp"),
            P(),
            P(),
            P("mp", None),
            P(),
            P(),
            P(),
            P(None, "mp"),
            P("mp"),
            P("mp", None),
            P(),
            P("dp", None),
        ),
        out_specs=(
            P("dp", None),
            P("dp", None),
            P(),
            P(),
            P("dp", "mp"),
            P("mp"),
            P(),
            P(),
            P("mp", "dp"),
            P(),
            P(),
            P(),
            P("dp", "mp"),
            P("mp"),
            P("mp", "dp"),
            P(),
        ),
        check_vma=False,
    )
```

```python
import functools
import math

import jax
import jax.numpy as jnp
from jax import lax
from jax.experimental import pallas as pl
from jax.experimental.pallas import tpu as pltpu
from jax.sharding import PartitionSpec as P

EPS = 1e-05
MESH = pl.DeviceIdType.MESH
F32 = jnp.float32
BF16 = jnp.bfloat16
VMEM_LIMIT = 60 * 2**20
HBM = pl.BlockSpec(memory_space=pl.ANY)


def norm_rows(rows_in, gain, shift):
    center = rows_in - jnp.mean(rows_in, axis=-1, keepdims=True)
    spread = jnp.mean(center * center, axis=-1, keepdims=True)
    return center * lax.rsqrt(spread + EPS) * gain + shift


def project(left, right):
    return jnp.dot(left, right, preferred_element_type=F32)


STRIP = 16
COLS = 512
BLOCK = 256
REACH = 3
GROUP = 4
NEG = -1e30
FRONT = (REACH - 1) * BLOCK


def key_window(c):
    first = max(0, c - REACH + 1) * BLOCK
    return first, (c + 1) * BLOCK - first


def mask_bias(code_col, doc_row, first_key, keys, first_query, queries):
    j = first_key + lax.broadcasted_iota(jnp.int32, (keys, queries), 0)
    i = first_query + lax.broadcasted_iota(jnp.int32, (keys, queries), 1)
    ok = ((j < i) & (code_col == doc_row)) | (j == i)
    return jnp.where(ok, 0.0, NEG)


def dot_t(a, b):
    return lax.dot_general(a, b, (((1,), (1,)), ((), ())), preferred_element_type=F32)


def rows_at(start, count):
    return pl.ds(pl.multiple_of(start, count), count)


def mp_partner(m, r):
    if r == 1:
        return m + 1 - 2 * lax.rem(m, 2)
    if r == 2:
        return m + 2 - 4 * lax.div(m, 2)
    return 3 - m


def flip_bit(d, bit):
    on = lax.rem(lax.div(d, bit), 2)
    return d + bit * (1 - 2 * on)


def front_kernel(
    heads,
    wq, wo, in_hbm, cot_hbm, w_down_hbm, bq, w_kv, gain_ref, shift_ref, bv_ref, code_ref, doc_ref,
    wq_out, wo_out, normed_hbm, q_hbm, mixed_hbm, d_acts_hbm, kv_ref, kt_ref, lse_ref,
    own_q, own_o, gq, go, sq, so, normed, q_ring, mixed_ring, vt, bias_ref, bq_all, cot, down, d_acts,
    load_sem, cot_sem, down_sem, d_acts_sem, ship_sem, o_sem, ring_sem, z_send, z_recv, b_send, b_recv, n_send, n_recv,
):
    m = lax.axis_index("mp")
    d = lax.axis_index("dp")
    dc, dx, dy = flip_bit(d, 1), flip_bit(d, 2), flip_bit(d, 4)
    dxy = flip_bit(dx, 4)
    is_mid = (m == 1) | (m == 2)
    buddy, across = {"mp": mp_partner(m, 1)}, {"mp": 3 - m}
    upper = lax.div(m, 2)
    inner = lax.rem(m + upper, 2)

    def plane_at(s):
        q = (1 - inner, 2, 3)[s]
        return q + upper * (3 - 2 * q)

    g = (gq, go)
    half = (gq.shape[2] // 2, go.shape[2] // 2)
    seq, width = normed.shape
    cols_q = q_ring.shape[2]
    hd = vt.shape[0]
    blocks = seq // BLOCK
    scale = 1.0 / math.sqrt(hd)
    planes = 4

    loads = [
        pltpu.make_async_copy(wq.at[d], own_q, load_sem.at[0]),
        pltpu.make_async_copy(wo.at[d], own_o, load_sem.at[1]),
        pltpu.make_async_copy(in_hbm, normed, load_sem.at[2]),
        pltpu.make_async_copy(wq, sq.at[m], load_sem.at[3]),
        pltpu.make_async_copy(wq, wq_out.at[m], load_sem.at[4]),
        pltpu.make_async_copy(wo, wo_out.at[m], load_sem.at[5]),
    ]
    for c in loads:
        c.start()
    bar = pltpu.get_barrier_semaphore()
    for r in (1, 2, 3):
        pl.semaphore_signal(bar, inc=1, device_id={"mp": mp_partner(m, r)}, device_id_type=MESH)
    for n in (dc, dx, dy):
        pl.semaphore_signal(bar, inc=1, device_id={"dp": n}, device_id_type=MESH)
    loads[0].wait()
    gq[m, d] = own_q[...].astype(F32)
    loads[1].wait()
    go[m, d] = own_o[...].astype(F32)
    bq_all[m] = bq[...]
    pl.semaphore_wait(bar, 6)

    def z_copy(w, plane, to, i):
        ref = g[w].at[plane, d]
        return pltpu.make_async_remote_copy(
            ref, ref, z_send.at[w, i], z_recv.at[w, plane], device_id=to, device_id_type=MESH
        )

    def z_own(w, wait=False):
        def go_or_wait(c):
            if wait:
                c.wait_send()
            else:
                c.start()

        go_or_wait(z_copy(w, m, buddy, 0))

        @pl.when(is_mid)
        def _():
            go_or_wait(z_copy(w, m, across, 1))

    def z_forward(w, s, wait=False):
        @pl.when(is_mid)
        def _():
            c = z_copy(w, plane_at(s), across if s == 0 else buddy, 2 + s)
            if wait:
                c.wait_send()
            else:
                c.start()

    def z_land(w, s):
        z_copy(w, plane_at(s), buddy, 0).wait_recv()

    def bias_copy(r, plane):
        return pltpu.make_async_remote_copy(
            bq_all.at[plane], bq_all.at[plane], b_send.at[r - 1], b_recv.at[r - 1],
            device_id={"mp": mp_partner(m, r)}, device_id_type=MESH,
        )

    sent_eighth = (d, d, d, dx, dy, dx, dy, dxy)
    landed_eighth = (dx, dy, dc, flip_bit(dx, 1), flip_bit(dy, 1), dxy, dxy, flip_bit(dxy, 1))
    sent_to = (dx, dy, dc, dc, dc, dy, dx, dc)

    def near(kind, w, r, eighths):
        q = plane_at(r)
        ref = g[w].at[q, eighths[kind]]
        if kind == 5:
            ref = g[w].at[q, eighths[kind], pl.ds(0, half[w])]
        if kind == 6:
            ref = g[w].at[q, eighths[kind], pl.ds(half[w], half[w])]
        return pltpu.make_async_remote_copy(
            ref, ref, n_send.at[kind, w, r], n_recv.at[kind, w, r],
            device_id={"dp": sent_to[kind]}, device_id_type=MESH,
        )

    def go_near(kind, w, r):
        near(kind, w, r, sent_eighth).start()

    def landed(kind, w, r):
        near(kind, w, r, landed_eighth).wait_recv()

    shipped = []
    ring = so.shape[0]

    def ship(w, r, eighth):
        q = plane_at(r)
        n = sum(1 for v, _ in shipped if v == w)
        if w == 0:
            sq[q, eighth] = gq[q, eighth].astype(BF16)
            c = pltpu.make_async_copy(sq.at[q, eighth], wq_out.at[q, eighth], ship_sem.at[n])
        else:
            slot = n % ring
            if n >= ring:
                [c for v, c in shipped if v == 1][n - ring].wait()
            so[slot] = go[q, eighth].astype(BF16)
            c = pltpu.make_async_copy(so.at[slot], wo_out.at[q, eighth], o_sem.at[slot])
        c.start()
        shipped.append((w, c))

    def store_q(q, c, slot):
        at = pl.ds(c * BLOCK, BLOCK)
        return pltpu.make_async_copy(
            q_ring.at[slot], q_hbm.at[at, rows_at(q * cols_q, cols_q)], ring_sem.at[0, slot]
        )

    def store_mixed(q, c, slot):
        at = pl.ds(c * BLOCK, BLOCK)
        return pltpu.make_async_copy(
            mixed_ring.at[slot], mixed_hbm.at[at, rows_at(q * cols_q, cols_q)], ring_sem.at[1, slot]
        )

    def set_bias(c):
        first, count = key_window(c)
        bias_ref[pl.ds(0, count), :] = mask_bias(
            code_ref[pl.ds(FRONT + first, count), :], doc_ref[:, pl.ds(c * BLOCK, BLOCK)],
            first, count, c * BLOCK, BLOCK,
        )

    def attend_block(q, c, n):
        slot = lax.rem(n, 2) if not isinstance(n, int) else n % 2
        first, count = key_window(c)
        keys, at = pl.ds(FRONT + first, count), pl.ds(c * BLOCK, BLOCK)

        def free():
            store_q(q, c, slot).wait()
            store_mixed(q, c, slot).wait()

        if not isinstance(n, int) or n >= 2:
            free()
        w = sq[q].reshape(width, cols_q)
        q_ring[slot] = (project(normed[at, :], w) + bq_all[q]).astype(BF16)
        store_q(q, c, slot).start()
        for u in range(cols_q // hd):
            head = pl.ds(u * hd, hd)
            s = dot_t(kv_ref[keys, pl.ds(0, hd)], q_ring[slot, :, head]) * scale
            s = s + bias_ref[pl.ds(0, count), :]
            top = jnp.max(s, axis=0, keepdims=True)
            e = jnp.exp(s - top)
            total = jnp.sum(e, axis=0, keepdims=True)
            probs = (e * (1.0 / total)).astype(BF16)
            mixed_ring[slot, :, head] = project(vt[:, pl.ds(first, count)], probs).T.astype(BF16)
            lse_ref[pl.ds(q * (cols_q // hd) + u, 1), at] = top + jnp.log(total)
        store_mixed(q, c, slot).start()

    bands = w_down_hbm.shape[0] // down.shape[1]

    def load_cot(i):
        at = rows_at(lax.rem(i, blocks) * BLOCK, BLOCK)
        slot = lax.rem(i, 2)
        return pltpu.make_async_copy(cot_hbm.at[at], cot.at[slot], cot_sem.at[slot])

    def load_down(n):
        at = pl.ds(n * down.shape[1], down.shape[1])
        return pltpu.make_async_copy(w_down_hbm.at[at], down.at[n % 2], down_sem.at[n % 2])

    def store_d_acts(n, i):
        slot = lax.rem(i, 2)
        rows = rows_at(lax.rem(i, blocks) * BLOCK, BLOCK)
        cols = pl.ds(n * down.shape[1], down.shape[1])
        return pltpu.make_async_copy(
            d_acts.at[slot], d_acts_hbm.at[rows, cols], d_acts_sem.at[slot]
        )

    def d_acts_band(n):
        load_down(n).wait()
        if n + 1 < bands:
            load_down(n + 1).start()

        def one(i, carry):
            slot = lax.rem(i, 2)
            load_cot(i).wait()

            @pl.when(i + 1 < bands * blocks)
            def _():
                load_cot(i + 1).start()

            @pl.when(i >= 2)
            def _():
                store_d_acts(n, i).wait()

            d_acts[slot] = dot_t(cot[slot], down[n % 2])
            store_d_acts(n, i).start()
            return carry

        lax.fori_loop(n * blocks, (n + 1) * blocks, one, 0)

    def own_plane(c):
        set_bias(c)
        attend_block(m, c, c)

    def other_planes(c, first, end):
        if first == 1:
            set_bias(c)

        def one(r, carry):
            attend_block(lax.rem(m + r, planes), c, blocks + c * (planes - 1) + r - 1)
            return carry

        lax.fori_loop(first, end, one, 0)

    stream = [(w, r) for w in (0, 1) for r in range(3)]

    def pass_on(i):
        w, s = stream[i]

        @pl.when(is_mid)
        def _():
            z_land(w, s)
            z_forward(w, s)

        if i == 2:
            z_own(1)

    def from_line(i):
        w, s = stream[i]

        @pl.when(jnp.logical_not(is_mid))
        def _():
            z_land(w, s)

        for kind in (0, 1, 2):
            go_near(kind, w, s)
        ship(w, s, d)

    def from_near(i):
        w, s = stream[i]
        landed(0, w, s)
        go_near(5, w, s)
        go_near(3, w, s)
        ship(w, s, dx)
        landed(1, w, s)
        go_near(6, w, s)
        go_near(4, w, s)
        ship(w, s, dy)
        landed(2, w, s)
        ship(w, s, dc)

    def from_far(i):
        w, s = stream[i]
        landed(5, w, s)
        landed(6, w, s)
        go_near(7, w, s)
        ship(w, s, dxy)
        for kind in (3, 4):
            landed(kind, w, s)
            ship(w, s, landed_eighth[kind])
        landed(7, w, s)
        ship(w, s, landed_eighth[7])

    z_own(0)
    for r in (1, 2, 3):
        bias_copy(r, m).start()

    load_down(0).start()
    load_cot(0).start()
    loads[2].wait()

    def norm_strip(i, carry):
        at = rows_at(i * STRIP, STRIP)
        normed[at, :] = norm_rows(normed[at, :].astype(F32), gain_ref[...], shift_ref[...]).astype(BF16)
        return carry

    lax.fori_loop(0, seq // STRIP, norm_strip, 0)
    keep_normed = pltpu.make_async_copy(normed, normed_hbm, load_sem.at[2])
    keep_normed.start()
    kv_ref[pl.ds(0, FRONT), :] = jnp.zeros((FRONT, 2 * hd), BF16)
    kt_ref[:, pl.ds(0, FRONT)] = jnp.zeros((hd, FRONT), BF16)
    for c in range(blocks):
        at, put = pl.ds(c * BLOCK, BLOCK), pl.ds(FRONT + c * BLOCK, BLOCK)
        kv = project(normed[at, :], w_kv[...])
        keys, values = kv[:, :hd], kv[:, hd:] + bv_ref[...]
        kv_ref[put, pl.ds(0, hd)] = keys.astype(BF16)
        kv_ref[put, pl.ds(hd, hd)] = values.astype(BF16)
        kt_ref[:, put] = keys.T.astype(BF16)
        vt[:, at] = values.T.astype(BF16)
    loads[3].wait()

    def stage(s):
        if s == 0:
            pass_on(0)
        if s + 1 < len(stream):
            pass_on(s + 1)
        if s < len(stream):
            from_line(s)
        if 1 <= s <= len(stream):
            from_near(s - 1)
        if s >= 2:
            from_far(s - 2)

    stage(0)
    own_plane(0)
    own_plane(1)
    stage(1)
    own_plane(2)
    own_plane(3)
    stage(2)
    for n in range(bands // 2):
        d_acts_band(n)
    stage(3)
    for n in range(bands // 2, bands):
        d_acts_band(n)
    for r in (1, 2, 3):
        bias_copy(r, mp_partner(m, r)).wait_recv()
    stage(4)
    other_planes(0, 1, planes)
    other_planes(1, 1, planes)
    from_line(5)
    other_planes(2, 1, 2)
    from_near(4)
    other_planes(2, 2, planes)
    from_far(3)
    other_planes(3, 1, 2)
    from_near(5)
    other_planes(3, 2, planes)
    from_far(4)
    from_far(5)

    for i in (0, 1):
        store_d_acts(0, i).wait()
    for slot in (0, 1):
        store_q(m, 0, slot).wait()
        store_mixed(m, 0, slot).wait()
    for w in (0, 1):
        z_own(w, wait=True)
    for w, r in stream:
        z_forward(w, r, wait=True)
        for kind in range(8):
            near(kind, w, r, sent_eighth).wait_send()
    for r in (1, 2, 3):
        bias_copy(r, m).wait_send()
    rows_o = [c for v, c in shipped if v == 1]
    for c in [c for v, c in shipped if v == 0] + rows_o[-ring:]:
        c.wait()
    keep_normed.wait()
    loads[4].wait()
    loads[5].wait()


def gather_by_sum(shard):
    blank = jnp.zeros((lax.axis_size("mp"),) + shard.shape, F32)
    half = shard.astype(F32) * 0.5
    own = lax.dynamic_update_index_in_dim(blank, half, lax.axis_index("mp"), 0)
    return lax.psum(own, "mp") * 2.0


def attention_front(
    inputs, w_query, b_query, w_keyval, b_value, w_out, gain, shift, code_col, doc_row, cotangent, w_down
):
    dp, mp = lax.axis_size("dp"), lax.axis_size("mp")
    width, cols = w_query.shape
    rows = w_out.shape[0]
    seq = inputs.shape[0]
    hd = w_keyval.shape[1] // 2
    if (dp, mp) != (8, 4):
        all_query, all_out, all_bias = (
            gather_by_sum(a).astype(a.dtype) for a in (w_query, w_out, b_query)
        )
        normed = norm_rows(inputs.astype(F32), gain, shift).astype(BF16)
        kv_bias = jnp.concatenate([jnp.zeros((hd,), F32), b_value])
        keyval = (project(normed, w_keyval) + kv_bias).astype(BF16)
        queries = jnp.concatenate(
            [project(normed, all_query[i]) + all_bias[i] for i in range(mp)], 1
        ).astype(BF16)
        mixed, lse = attend(queries, keyval, code_col[FRONT:], doc_row)
        keyval = jnp.pad(keyval, ((FRONT, 0), (0, 0)))
        keys_t = keyval[:, :hd].T
        d_acts = jnp.einsum("td,fd->tf", cotangent, w_down, preferred_element_type=F32)
        return all_query, all_out.reshape(-1, width), normed, queries, mixed, d_acts, keyval, keys_t, lse
    wq = w_query.reshape(dp, width // dp, cols)
    wo = w_out.reshape(dp, rows // dp, width)
    dma = pltpu.SemaphoreType.DMA
    vmem = pl.BlockSpec(memory_space=pltpu.VMEM)
    full_q, full_o = (mp,) + wq.shape, (mp,) + wo.shape
    heads = mp * cols // hd
    shape = jax.ShapeDtypeStruct
    out_q, out_o, normed, queries, mixed, d_acts, keyval, keys_t, lse = pl.pallas_call(
        functools.partial(front_kernel, heads),
        out_shape=(
            shape(full_q, BF16),
            shape(full_o, BF16),
            shape((seq, width), BF16),
            shape((seq, mp * cols), BF16),
            shape((seq, mp * cols), BF16),
            shape((seq, w_down.shape[0]), F32),
            shape((FRONT + seq, 2 * hd), BF16),
            shape((hd, FRONT + seq), BF16),
            shape((heads, seq), F32),
        ),
        in_specs=[HBM] * 5 + [vmem] * 7,
        out_specs=(HBM,) * 6 + (vmem,) * 3,
        scratch_shapes=[
            pltpu.VMEM(wq.shape[1:], BF16),
            pltpu.VMEM(wo.shape[1:], BF16),
            pltpu.VMEM(full_q, F32),
            pltpu.VMEM(full_o, F32),
            pltpu.VMEM(full_q, BF16),
            pltpu.VMEM((4,) + wo.shape[1:], BF16),
            pltpu.VMEM((seq, width), BF16),
            pltpu.VMEM((2, BLOCK, cols), BF16),
            pltpu.VMEM((2, BLOCK, cols), BF16),
            pltpu.VMEM((hd, seq), BF16),
            pltpu.VMEM((REACH * BLOCK, BLOCK), F32),
            pltpu.VMEM((mp, 1, cols), F32),
            pltpu.VMEM((2, BLOCK, width), BF16),
            pltpu.VMEM((2, COLS, width), BF16),
            pltpu.VMEM((2, BLOCK, COLS), F32),
            dma((6,)),
            dma((2,)),
            dma((2,)),
            dma((2,)),
            dma((3 * dp,)),
            dma((4,)),
            dma((2, 2)),
            dma((2, 5)),
            dma((2, mp)),
            dma((3,)),
            dma((3,)),
            dma((8, 2, 3)),
            dma((8, 2, 3)),
        ],
        compiler_params=pltpu.CompilerParams(
            collective_id=0, has_side_effects=True, vmem_limit_bytes=VMEM_LIMIT
        ),
        name="attention_front",
    )(
        wq, wo, inputs, cotangent, w_down, b_query.reshape(1, cols), w_keyval, gain.reshape(1, width),
        shift.reshape(1, width), b_value.reshape(1, hd), code_col, doc_row,
    )
    return (
        out_q.reshape(mp, width, cols), out_o.reshape(mp * rows, width),
        normed, queries, mixed, d_acts, keyval, keys_t, lse,
    )


PIECE = 32
SLOT = 1
CROSS_LATE = 2 * SLOT
LATE = 5 * SLOT
AHEAD = 3 * SLOT


class LineSum:
    scratch = staticmethod(
        lambda rows, pieces, width: [pltpu.VMEM((rows, width), F32)] * 3
        + [pltpu.SemaphoreType.DMA((pieces,))] * 5
    )

    def __init__(self, refs):
        self.part, self.total, self.cross, *sems = refs
        self.in_send, self.in_recv, self.over_send, self.over_recv, self.out_send = sems
        self.slots = self.part.shape[0] // PIECE
        self.pieces = self.in_send.shape[0]
        m = lax.axis_index("mp")
        self.is_end = (m == 0) | (m == 3)
        self.is_mid = (m == 1) | (m == 2)
        self.buddy = {"mp": mp_partner(m, 1)}
        self.across = {"mp": 3 - m}

    def greet(self, others=()):
        bar = pltpu.get_barrier_semaphore()
        pl.semaphore_signal(bar, inc=1, device_id=self.buddy, device_id_type=MESH)
        for other in others:
            pl.semaphore_signal(bar, inc=1, device_id=other, device_id_type=MESH)

        @pl.when(self.is_mid)
        def _():
            pl.semaphore_signal(bar, inc=1, device_id=self.across, device_id_type=MESH)

    def meet(self, others=()):
        bar = pltpu.get_barrier_semaphore()

        @pl.when(self.is_end)
        def _():
            pl.semaphore_wait(bar, 1 + len(others))

        @pl.when(self.is_mid)
        def _():
            pl.semaphore_wait(bar, 2 + len(others))

    def at(self, k):
        slot = k if self.slots == self.pieces else k % self.slots
        return rows_at(slot * PIECE, PIECE)

    def inward(self, k):
        at = self.at(k)
        return pltpu.make_async_remote_copy(
            self.part.at[at], self.total.at[at], self.in_send.at[k], self.in_recv.at[k],
            device_id=self.buddy, device_id_type=MESH,
        )

    def over(self, k):
        at = self.at(k)
        return pltpu.make_async_remote_copy(
            self.part.at[at], self.cross.at[at], self.over_send.at[k], self.over_recv.at[k],
            device_id=self.across, device_id_type=MESH,
        )

    def outward(self, k):
        at = self.at(k)
        return pltpu.make_async_remote_copy(
            self.total.at[at], self.total.at[at], self.out_send.at[k], self.in_recv.at[k],
            device_id=self.buddy, device_id_type=MESH,
        )

    def slot(self, i):
        for j in range(SLOT):
            self.tick(i * SLOT + j)

    def tick(self, k):
        n = self.pieces

        @pl.when(self.is_end)
        def _():
            @pl.when(k < n)
            def _():
                @pl.when(k >= AHEAD)
                def _():
                    self.inward(k - AHEAD).wait_send()

                self.inward(k).start()

            @pl.when((k >= LATE) & (k < n + LATE))
            def _():
                self.outward(k - LATE).wait_recv()

        @pl.when(self.is_mid)
        def _():
            @pl.when(k < n)
            def _():
                at = self.at(k)
                self.inward(k).wait_recv()
                self.part[at, :] += self.total[at, :]
                self.over(k).start()

            @pl.when((k >= CROSS_LATE) & (k < n + CROSS_LATE))
            def _():
                j = k - CROSS_LATE
                at = self.at(j)
                self.over(j).wait_recv()
                self.total[at, :] = self.part[at, :] + self.cross[at, :]
                self.outward(j).start()

    def free(self, first, count):
        @pl.when(self.is_mid)
        def _():
            def sent(k, c):
                self.over(k).wait_send()
                self.outward(k).wait_send()
                return c

            lax.fori_loop(first, first + count, sent, 0)

    def finish(self, freed=0):
        n = self.pieces

        @pl.when(self.is_end)
        def _():
            for k in range(n - AHEAD, n):
                self.inward(k).wait_send()

        self.free(freed, n - freed)


def attend_kernel(seq, heads, q_ref, kv_ref, vt_ref, code_ref, doc_ref, mixed_ref, lse_ref, bias_ref):
    hd = vt_ref.shape[0]
    scale = 1.0 / math.sqrt(hd)
    for c in range(seq // BLOCK):

        @pl.when(pl.program_id(0) == c)
        def _(c=c):
            first, count = key_window(c)
            keys = pl.ds(first, count)
            bias_ref[pl.ds(0, count), :] = mask_bias(
                code_ref[keys, :], doc_ref[...], first, count, c * BLOCK, BLOCK
            )

            def some_heads(g, carry):
                for u in range(GROUP):
                    h = g * GROUP + u
                    cols = pl.ds(pl.multiple_of(h * hd, hd), hd)
                    s = dot_t(kv_ref[keys, pl.ds(0, hd)], q_ref[:, cols]) * scale
                    s = s + bias_ref[pl.ds(0, count), :]
                    top = jnp.max(s, axis=0, keepdims=True)
                    e = jnp.exp(s - top)
                    total = jnp.sum(e, axis=0, keepdims=True)
                    probs = (e * (1.0 / total)).astype(BF16)
                    mixed = project(vt_ref[:, keys], probs)
                    mixed_ref[:, cols] = mixed.T.astype(BF16)
                    lse_ref[pl.ds(h, 1), :] = top + jnp.log(total)
                return carry

            lax.fori_loop(0, heads // GROUP, some_heads, 0)


def attend(queries, keyval, code_col, doc_row):
    seq, width = queries.shape
    hd = keyval.shape[1] // 2
    heads = width // hd
    values_t = keyval[:, hd:].T
    whole = lambda *shape: pl.BlockSpec(shape, lambda c: (0,) * len(shape))
    return pl.pallas_call(
        functools.partial(attend_kernel, seq, heads),
        grid=(seq // BLOCK,),
        out_shape=(
            jax.ShapeDtypeStruct((seq, width), BF16),
            jax.ShapeDtypeStruct((heads, seq), F32),
        ),
        in_specs=[
            pl.BlockSpec((BLOCK, width), lambda c: (c, 0)),
            whole(seq, 2 * hd),
            whole(hd, seq),
            whole(seq, 1),
            pl.BlockSpec((1, BLOCK), lambda c: (0, c)),
        ],
        out_specs=(
            pl.BlockSpec((BLOCK, width), lambda c: (c, 0)),
            pl.BlockSpec((heads, BLOCK), lambda c: (0, c)),
        ),
        scratch_shapes=[pltpu.VMEM((REACH * BLOCK, BLOCK), F32)],
        compiler_params=pltpu.CompilerParams(vmem_limit_bytes=VMEM_LIMIT),
        name="attend",
    )(queries, keyval, values_t, code_col, doc_row)


def norm_back_rows(x, grad, gain):
    mean = jnp.mean(x, axis=-1, keepdims=True)
    center = x - mean
    scale = lax.rsqrt(jnp.mean(center * center, axis=-1, keepdims=True) + EPS)
    xhat = center * scale
    e = grad * gain
    weighted = grad * xhat
    d_in = scale * (
        e - jnp.mean(e, axis=-1, keepdims=True) - xhat * jnp.mean(e * xhat, axis=-1, keepdims=True)
    )
    return d_in, weighted


def dot_down(a, b):
    return lax.dot_general(a, b, (((0,), (0,)), ((), ())), preferred_element_type=F32)


def fold_rows(x):
    return jnp.sum(x.reshape(-1, 8, x.shape[-1]), axis=0)


def mlp_attend_back_kernel(
    heads,
    dh_hbm, w_up_hbm, w_out_hbm, mid_hbm, cot_hbm, q_hbm, acts_hbm, w_down_hbm, normed_hbm, mixed_hbm,
    kv_ref, kt_ref, code_ref, doc_ref, lse_ref, gain_ref,
    d_mid_hbm, dq_hbm, feed_hbm, grads_hbm, dkv_ref, sums_ref,
    w_up, w_out, dh, mid, cot, q, normed, mixed, d_branch, d_mixed, dq, grads, bias_ref,
    load_sem, out_sem, *line_refs,
):
    line = LineSum(line_refs)
    seq, width = q_hbm.shape
    m = lax.axis_index("mp")
    own_cols = mixed.shape[1]
    own = rows_at(m * own_cols, own_cols)
    ring = line.part.shape[0] // BLOCK
    hd = kt_ref.shape[0]
    chunks = seq // BLOCK
    slots = BLOCK // (PIECE * SLOT)
    count = REACH * BLOCK
    scale = 1.0 / math.sqrt(hd)

    def load(i, src, dst):
        return pltpu.make_async_copy(src, dst, load_sem.at[i])

    def load_dh(c):
        return load(2, dh_hbm.at[rows_at(c * BLOCK, BLOCK)], dh)

    def load_chunk(c):
        at = rows_at(c * BLOCK, BLOCK)
        return [
            load(3, mid_hbm.at[at], mid),
            load(4, cot_hbm.at[at], cot),
            load(5, q_hbm.at[at], q),
            load(6, normed_hbm.at[at], normed),
            load(7, mixed_hbm.at[at, own], mixed),
        ]

    def block_at(c):
        return rows_at((c % ring) * BLOCK, BLOCK)

    def store(i, src, dst, c):
        return pltpu.make_async_copy(src, dst.at[rows_at(c * BLOCK, BLOCK)], out_sem.at[i])

    def stores(c, which=(0, 1)):
        pairs = ((mid, d_mid_hbm), (dq, dq_hbm))
        return [store(i, *pairs[i], c) for i in which]

    load(0, w_up_hbm, w_up).start()
    load_dh(0).start()
    load(1, w_out_hbm, w_out).start()
    load_acts = load(2, acts_hbm.at[pl.ds(0, BLOCK)], dh)
    load_down = load(0, w_down_hbm, w_up)
    load_mid = load(3, mid_hbm.at[pl.ds(0, BLOCK)], mid)
    line.greet()
    dkv_ref[...] = jnp.zeros_like(dkv_ref)
    sums_ref[...] = jnp.zeros_like(sums_ref)
    grads[...] = jnp.zeros_like(grads)

    def produce(c):
        at = block_at(c)
        load_dh(c).wait()

        def cols(n, carry):
            there = rows_at(n * COLS, COLS)
            line.part[at, there] = dot_t(dh[...], w_up[there, :])
            return carry

        lax.fori_loop(0, width // COLS, cols, 0)

        @pl.when(c + 1 < chunks)
        def _():
            load_dh(c + 1).start()

        @pl.when(c + 1 == chunks)
        def _():
            load_acts.start()
            load_down.start()

    def produce_feed():
        at = block_at(chunks)
        load_acts.wait()
        load_down.wait()
        load_mid.wait()

        def cols(n, carry):
            there = rows_at(n * COLS, COLS)
            line.part[at, there] = project(dh[...], w_up[:, there])
            return carry

        lax.fori_loop(0, width // COLS, cols, 0)

        @pl.when(m == 0)
        def _():
            line.part[at, :] += mid[...]

    def add_grads(first, left, right):
        at = pl.ds(first, own_cols)

        def cols(n, carry):
            there = rows_at(n * COLS, COLS)
            grads[at, there] += dot_down(left, right[:, there])
            return carry

        lax.fori_loop(0, width // COLS, cols, 0)

    def norm_step(c, half):
        def strip(i, carry):
            row = half * (BLOCK // 2) + i * STRIP
            at = rows_at(row, STRIP)
            grad = line.total[rows_at((c % ring) * BLOCK + row, STRIP), :]
            d_in, weighted = norm_back_rows(mid[at, :], grad, gain_ref[...])
            cot_rows = cot[at, :].astype(F32)
            d_mid = cot_rows + d_in
            low = d_mid.astype(BF16)
            mid[at, :] = d_mid
            d_branch[at, :] = low
            sums_ref[0] += fold_rows(weighted)
            sums_ref[1] += fold_rows(grad)
            sums_ref[2] += fold_rows(low.astype(F32))
            sums_ref[3] += fold_rows(cot_rows)
            return carry

        lax.fori_loop(0, BLOCK // 2 // STRIP, strip, 0)

    def mixed_step(c):
        def cols(n, carry):
            there = rows_at(n * COLS, COLS)
            d_mixed[:, there] = dot_t(d_branch[...], w_out[there, :]).astype(BF16)
            return carry

        lax.fori_loop(0, width // COLS, cols, 0)
        keys = pl.ds(pl.multiple_of(c * BLOCK, BLOCK), count)
        bias_ref[...] = mask_bias(
            code_ref[keys, :], doc_ref[:, rows_at(c * BLOCK, BLOCK)],
            (c - REACH + 1) * BLOCK, count, c * BLOCK, BLOCK,
        )

    def heads_step(c, g):
        keys = pl.ds(pl.multiple_of(c * BLOCK, BLOCK), count)
        queries = rows_at(c * BLOCK, BLOCK)
        dk = jnp.zeros((count, hd), F32)
        dv = jnp.zeros((count, hd), F32)
        for u in range(GROUP):
            h = g * GROUP + u
            cols = rows_at(h * hd, hd)
            qh = q[:, cols]
            dm = d_mixed[:, cols]
            s = dot_t(kv_ref[keys, pl.ds(0, hd)], qh) * scale + bias_ref[...]
            probs = jnp.exp(s - lse_ref[pl.ds(h, 1), queries])
            d_probs = dot_t(kv_ref[keys, pl.ds(hd, hd)], dm)
            t = probs * d_probs
            inner = jnp.sum(t, axis=0, keepdims=True)
            ds = (t - probs * inner).astype(BF16)
            dqh = project(kt_ref[:, keys], ds) * scale
            dq[:, cols] = dqh.T.astype(BF16)
            dk = dk + project(ds, qh)
            dv = dv + project(probs.astype(BF16), dm)
        dkv_ref[keys, pl.ds(0, hd)] += dk * scale
        dkv_ref[keys, pl.ds(hd, hd)] += dv

    load(0, w_up_hbm, w_up).wait()
    produce(0)
    line.meet()
    for k in range(3):
        line.slot(k)
    load(1, w_out_hbm, w_out).wait()

    def cycle(u, carry):
        c = u - 1
        base = u * slots + 3

        @pl.when(u >= 2)
        def _():
            for i in stores(u - 2):
                i.wait()

        @pl.when(u + 1 == chunks)
        def _():
            load_mid.start()

        line.slot(base)

        @pl.when(u >= 2)
        def _():
            line.free((u - 2) * (BLOCK // PIECE), BLOCK // PIECE)

        @pl.when(u + 1 < chunks)
        def _():
            produce(u + 1)

        @pl.when(u + 1 == chunks)
        def _():
            produce_feed()

        @pl.when(u >= 1)
        def _():
            for i in load_chunk(c):
                i.start()

        line.slot(base + 1)

        @pl.when(u >= 1)
        def _():
            for i in load_chunk(c):
                i.wait()
            norm_step(c, 0)

        line.slot(base + 2)

        @pl.when(u >= 1)
        def _():
            norm_step(c, 1)
            stores(c, (0,))[0].start()

        line.slot(base + 3)

        @pl.when(u >= 1)
        def _():
            mixed_step(c)
            add_grads(own_cols, mixed[...], d_branch)

        def some_heads(g, carry):
            line.slot(base + 4 + g)

            @pl.when(u >= 1)
            def _():
                heads_step(c, g)

            return carry

        lax.fori_loop(0, heads // GROUP, some_heads, 0)

        @pl.when(u >= 1)
        def _():
            stores(c, (1,))[0].start()
            add_grads(0, dq[:, own], normed)

            def strip(i, carry):
                sums_ref[4] += fold_rows(dq[rows_at(i * STRIP, STRIP), :].astype(F32))
                return carry

            lax.fori_loop(0, BLOCK // STRIP, strip, 0)

        return carry

    lax.fori_loop(0, chunks + 1, cycle, 0)
    for k in range((chunks + 1) * slots + 3, (line.pieces + LATE) // SLOT):
        line.slot(k)
    keep_grads = pltpu.make_async_copy(grads, grads_hbm, out_sem.at[3])
    keep_grads.start()
    keep_feed = pltpu.make_async_copy(line.total.at[block_at(chunks)], feed_hbm, out_sem.at[2])
    keep_feed.start()
    for i in stores(chunks - 1):
        i.wait()
    keep_feed.wait()
    keep_grads.wait()
    line.finish((chunks - 1) * (BLOCK // PIECE))


def mlp_attend_back(
    d_hidden, w_up, w_out, middle, cotangent, queries, acts, w_down, normed, mixed, own_cols,
    keyval, keys_t, code_col, doc_row, lse, gain,
):
    seq, width = queries.shape
    heads = width // keys_t.shape[0]
    vmem = pl.BlockSpec(memory_space=pltpu.VMEM)
    dma = pltpu.SemaphoreType.DMA
    block = lambda dtype: pltpu.VMEM((BLOCK, width), dtype)
    return pl.pallas_call(
        functools.partial(mlp_attend_back_kernel, heads),
        out_shape=(
            jax.ShapeDtypeStruct((seq, width), F32),
            jax.ShapeDtypeStruct((seq, width), BF16),
            jax.ShapeDtypeStruct((BLOCK, width), F32),
            jax.ShapeDtypeStruct((2 * own_cols, width), F32),
            jax.ShapeDtypeStruct(keyval.shape, F32),
            jax.ShapeDtypeStruct((5, 8, width), F32),
        ),
        in_specs=[HBM] * 10 + [vmem] * 6,
        out_specs=(HBM, HBM, HBM, HBM, vmem, vmem),
        scratch_shapes=[
            pltpu.VMEM(w_up.shape, BF16),
            pltpu.VMEM(w_out.shape, BF16),
            pltpu.VMEM((BLOCK, d_hidden.shape[1]), BF16),
            block(F32),
            block(BF16),
            block(BF16),
            block(BF16),
            pltpu.VMEM((BLOCK, own_cols), BF16),
            block(BF16),
            block(BF16),
            block(BF16),
            pltpu.VMEM((2 * own_cols, width), F32),
            pltpu.VMEM((REACH * BLOCK, BLOCK), F32),
            dma((8,)),
            dma((4,)),
        ]
        + LineSum.scratch(min(3 * BLOCK, seq), (seq + BLOCK) // PIECE, width),
        compiler_params=pltpu.CompilerParams(
            collective_id=1, has_side_effects=True, vmem_limit_bytes=VMEM_LIMIT
        ),
        cost_estimate=pl.CostEstimate(
            flops=200 * 10**9, bytes_accessed=2**25, transcendentals=0
        ),
        name="mlp_attend_back",
    )(
        d_hidden, w_up, w_out, middle, cotangent, queries, acts, w_down, normed, mixed,
        keyval, keys_t, code_col, doc_row, lse, gain.reshape(1, width),
    )


def feed_kernel(
    rounds,
    acts_hbm, w_down_hbm, mid_hbm, dq_hbm, w_q_hbm, in_hbm, d_mid_hbm, normed_hbm, first_hbm,
    dkv_f_ref, w_kv_ref, gain_ref, bias_ref, sums_in, b_up_in,
    out_hbm, in_grad_hbm, table_out, vectors_out,
    w_down, w_q, acts, mid, dq, xs, d_mid, spread, low, in_grad, normed, dkv_ref, sums, trade, trade_in, table, table_in, table_all,
    load_sem, out_sem, t_send, t_recv, h_send, h_recv, d_send, d_recv, *line_refs,
):
    line = LineSum(line_refs)
    rows, width = line.part.shape
    seq = rows + BLOCK
    blocks = seq // BLOCK
    chunks = rows // BLOCK
    slots = BLOCK // (PIECE * SLOT)
    planes, _, cols_q = w_q.shape
    m = lax.axis_index("mp")
    d = lax.axis_index("dp")
    peers = [{"dp": flip_bit(d, 1 << r)} for r in range(rounds)]

    def load(i, src, dst):
        return pltpu.make_async_copy(src, dst, load_sem.at[i])

    def load_feed(c):
        at = rows_at((c + 1) * BLOCK, BLOCK)
        return [load(2, acts_hbm.at[at], acts), load(3, mid_hbm.at[at], mid)]

    def load_grad(c):
        at = rows_at(c * BLOCK, BLOCK)
        return [
            load(4, dq_hbm.at[at], dq),
            load(5, in_hbm.at[at], xs),
            load(6, d_mid_hbm.at[at], d_mid),
        ]

    def store(i, src, dst, c):
        return pltpu.make_async_copy(src, dst.at[rows_at(c * BLOCK, BLOCK)], out_sem.at[i])

    def load_normed(c):
        return load(7, normed_hbm.at[rows_at(c * BLOCK, BLOCK)], normed)

    load_first = load(8, first_hbm, spread)
    load(0, w_down_hbm, w_down).start()
    for i in load_feed(0):
        i.start()
    load_first.start()
    load_normed(0).start()
    load(1, w_q_hbm, w_q).start()
    for i in load_grad(0):
        i.start()
    line.greet(peers)
    sums[...] = jnp.zeros_like(sums)
    dkv_ref[...] = dkv_f_ref[pl.ds(FRONT, seq), :].astype(BF16)
    hd = dkv_ref.shape[1] // 2

    def produce(c):
        at = rows_at(c * BLOCK, BLOCK)
        for i in load_feed(c):
            i.wait()

        def cols(n, carry):
            there = rows_at(n * COLS, COLS)
            line.part[at, there] = project(acts[...], w_down[:, there])
            return carry

        lax.fori_loop(0, width // COLS, cols, 0)

        @pl.when(m == 0)
        def _():
            line.part[at, :] += mid[...]

        @pl.when(c + 1 < chunks)
        def _():
            for i in load_feed(c + 1):
                i.start()

    def output_step(source, c):
        def strip(i, carry):
            at = rows_at(i * STRIP, STRIP)
            there = rows_at(c * BLOCK + i * STRIP, STRIP)
            low[at, :] = (source[there, :] + bias_ref[...]).astype(BF16)
            return carry

        lax.fori_loop(0, BLOCK // STRIP, strip, 0)

    def spread_step(c):
        here = rows_at(c * BLOCK, BLOCK)

        def cols(n, carry):
            there = rows_at(n * COLS, COLS)
            total = dot_t(dkv_ref[here, :], w_kv_ref[there, :])
            for i in range(planes):
                total = total + dot_t(dq[:, pl.ds(i * cols_q, cols_q)], w_q[i, there, :])
            spread[:, there] = total
            return carry

        lax.fori_loop(0, width // COLS, cols, 0)

    def norm_step(c, half):
        def strip(i, carry):
            at = rows_at(half * (BLOCK // 2) + i * STRIP, STRIP)
            grad = spread[at, :]
            d_in, weighted = norm_back_rows(xs[at, :].astype(F32), grad, gain_ref[...])
            in_grad[at, :] = (d_mid[at, :] + d_in).astype(BF16)
            sums[0] += fold_rows(weighted)
            sums[1] += fold_rows(grad)
            return carry

        lax.fori_loop(0, BLOCK // 2 // STRIP, strip, 0)

    def swap(r):
        return pltpu.make_async_remote_copy(
            trade.at[r], trade_in.at[r], t_send.at[r], t_recv.at[r],
            device_id=peers[r], device_id_type=MESH,
        )

    def vectors_first():
        trade[0] = jnp.zeros_like(trade.at[0])
        for i in range(2):
            trade[0, i : i + 1] = jnp.sum(sums[i], axis=0, keepdims=True)
        for i in range(sums_in.shape[0]):
            trade[0, 2 + i : 3 + i] = jnp.sum(sums_in[i], axis=0, keepdims=True)
        at = 2 + sums_in.shape[0]
        trade[0, at : at + 1] = b_up_in[...]
        d_values = dkv_f_ref[pl.ds(FRONT, seq), pl.ds(hd, hd)]
        trade[0, at + 1 : at + 2, 0:hd] = jnp.sum(d_values, axis=0, keepdims=True)
        swap(0).start()

    def vectors_next(r):
        swap(r).wait()
        trade[r + 1] = trade[r] + trade_in[r]
        if r + 1 < rounds:
            swap(r + 1).start()
        else:
            vectors_out[...] = trade[r + 1]

    def table_block(c):
        load_normed(c).wait()

        def cols(n, carry):
            there = rows_at(n * COLS, COLS)
            part = dot_down(dkv_ref[pl.ds(c * BLOCK, BLOCK), :], normed[:, there])
            table[:, there] = part if c == 0 else table[:, there] + part
            return carry

        lax.fori_loop(0, width // COLS, cols, 0)
        if c + 1 < blocks:
            load_normed(c + 1).start()

    bits = [lax.rem(lax.div(d, 1 << r), 2) for r in range(rounds)]
    base = [0]
    size = [table.shape[0]]
    for r in range(rounds):
        size.append(size[r] // 2)
        base.append(base[r] + bits[r] * size[r + 1])

    def part_of(start, count):
        return pl.ds(pl.multiple_of(start, 8), count)

    def halve(r):
        away = part_of(base[r] + (1 - bits[r]) * size[r + 1], size[r + 1])
        into = pl.ds(size[0] - size[r], size[r + 1])
        return pltpu.make_async_remote_copy(
            table.at[away], table_in.at[into], h_send.at[r], h_recv.at[r],
            device_id=peers[r], device_id_type=MESH,
        )

    def double(r, mine):
        start = base[r] + (bits[r] if mine else 1 - bits[r]) * size[r + 1]
        at = part_of(start, size[r + 1])
        return pltpu.make_async_remote_copy(
            table_all.at[at], table_all.at[at], d_send.at[r], d_recv.at[r],
            device_id=peers[r], device_id_type=MESH,
        )

    store_table = pltpu.make_async_copy(table_all, table_out, out_sem.at[2])

    def table_step(i):
        if 1 <= i <= rounds:
            r = i - 1
            halve(r).wait()
            at = part_of(base[r + 1], size[r + 1])
            whole = table_all if i == rounds else table
            whole[at, :] = table[at, :] + table_in[pl.ds(size[0] - size[r], size[r + 1]), :]
        elif i > rounds:
            r = 2 * rounds - i
            double(r, True).wait_send()
            double(r, False).wait_recv()
        if i < rounds:
            halve(i).start()
        elif i < 2 * rounds:
            double(2 * rounds - 1 - i, True).start()
        else:
            store_table.start()

    load(0, w_down_hbm, w_down).wait()
    produce(0)
    line.meet(peers)
    for k in range(3):
        line.slot(k)
    load(1, w_q_hbm, w_q).wait()

    def grads(u, first):
        v = 2 * u + (0 if first else 1)

        def one():
            @pl.when(v < blocks)
            def _():
                for i in load_grad(v):
                    i.wait()
                spread_step(v)

        def two():
            @pl.when(v < blocks)
            def _():
                @pl.when(v >= 1)
                def _():
                    store(1, in_grad, in_grad_hbm, v - 1).wait()

                norm_step(v, 0)

        def three():
            @pl.when(v < blocks)
            def _():
                norm_step(v, 1)
                store(1, in_grad, in_grad_hbm, v).start()

                @pl.when(v + 1 < blocks)
                def _():
                    for i in load_grad(v + 1):
                        i.start()

        return one, two, three

    def cycle(u, carry):
        c = u - 1
        base_tick = u * slots + 3

        def produce_step():
            @pl.when(u + 1 < chunks)
            def _():
                produce(u + 1)

        def out_step():
            @pl.when(u == 0)
            def _():
                load_first.wait()
                output_step(spread, 0)
                store(0, low, out_hbm, 0).start()

            @pl.when(u >= 1)
            def _():
                store(0, low, out_hbm, u - 1).wait()
                output_step(line.total, c)
                store(0, low, out_hbm, u).start()

        steps = [produce_step, out_step, *grads(u, True), *grads(u, False)]
        for i, step in enumerate(steps):
            line.slot(base_tick + i)
            for v in range(chunks + 1):
                at = v * slots + i
                extra = []
                if at % 2 == 0 and at // 2 < blocks:
                    extra.append(functools.partial(table_block, at // 2))
                if at % 2 == 0 and 0 <= at // 2 - blocks <= 2 * rounds:
                    extra.append(functools.partial(table_step, at // 2 - blocks))
                late = at - (blocks // 2) * slots
                if late == 0:
                    extra.append(vectors_first)
                elif 0 < late <= rounds:
                    extra.append(functools.partial(vectors_next, late - 1))
                if extra:

                    @pl.when(u == v)
                    def _(extra=extra):
                        for e in extra:
                            e()

            step()
        return carry

    lax.fori_loop(0, chunks + 1, cycle, 0)
    store(0, low, out_hbm, chunks).wait()
    store(1, in_grad, in_grad_hbm, blocks - 1).wait()
    store_table.wait()
    line.finish()


def feed_and_input_grad(
    acts, w_down, middle, b_down, d_queries, all_query, d_keyval_sum, w_keyval, inputs, d_middle, gain,
    normed, feed_first, sums, b_up,
):
    seq, width = inputs.shape
    rounds = (lax.axis_size("dp") - 1).bit_length()
    vmem = pl.BlockSpec(memory_space=pltpu.VMEM)
    dma = pltpu.SemaphoreType.DMA
    block = lambda dtype: pltpu.VMEM((BLOCK, width), dtype)
    rest = seq - BLOCK
    shape = jax.ShapeDtypeStruct
    table = (w_keyval.shape[1], width)
    return pl.pallas_call(
        functools.partial(feed_kernel, rounds),
        out_shape=(
            shape((seq, width), BF16),
            shape((seq, width), BF16),
            shape(table, F32),
            shape((16, width), F32),
        ),
        in_specs=[HBM] * 9 + [vmem] * 6,
        out_specs=(HBM, HBM, HBM, vmem),
        scratch_shapes=[
            pltpu.VMEM(w_down.shape, BF16),
            pltpu.VMEM(all_query.shape, BF16),
            pltpu.VMEM((BLOCK, acts.shape[1]), BF16),
            block(F32),
            block(BF16),
            block(BF16),
            block(F32),
            block(F32),
            block(BF16),
            block(BF16),
            block(BF16),
            pltpu.VMEM((seq, w_keyval.shape[1]), BF16),
            pltpu.VMEM((2, 8, width), F32),
            pltpu.VMEM((rounds + 1, 16, width), F32),
            pltpu.VMEM((rounds, 16, width), F32),
            pltpu.VMEM(table, F32),
            pltpu.VMEM(table, F32),
            pltpu.VMEM(table, F32),
            dma((9,)),
            dma((3,)),
            dma((rounds,)),
            dma((rounds,)),
            dma((rounds,)),
            dma((rounds,)),
            dma((rounds,)),
            dma((rounds,)),
        ]
        + LineSum.scratch(rest, rest // PIECE, width),
        compiler_params=pltpu.CompilerParams(
            collective_id=2, has_side_effects=True, vmem_limit_bytes=VMEM_LIMIT
        ),
        cost_estimate=pl.CostEstimate(
            flops=200 * 10**9, bytes_accessed=2**25, transcendentals=0
        ),
        name="feed_and_input_grad",
    )(
        acts, w_down, middle, d_queries, all_query, inputs, d_middle, normed, feed_first,
        d_keyval_sum, w_keyval, gain.reshape(1, width), b_down.reshape(1, width), sums,
        b_up.reshape(1, width),
    )


def shards(
    inputs,
    doc_ids,
    pad_mask,
    attn_gain,
    attn_shift,
    w_query,
    b_query,
    w_keyval,
    b_value,
    w_out,
    b_out,
    mlp_gain,
    mlp_shift,
    w_up,
    b_up,
    w_down,
    b_down,
    cotangent,
):
    seq = doc_ids.shape[1]
    hd = b_value.shape[0]
    width = inputs.shape[1]
    own_cols = w_query.shape[1]
    own = lax.axis_index("mp") * own_cols
    inputs_f = inputs.astype(F32)
    docs = doc_ids[0]
    codes = jnp.where(pad_mask[0] == 1, docs, -1)
    code_col = jnp.pad(codes, (FRONT, 0), constant_values=-2).reshape(-1, 1)
    doc_row = docs.reshape(1, seq)

    all_query, all_out, normed_attn, queries, mixed, d_acts, keyval, keys_t, lse = attention_front(
        inputs, w_query, b_query, w_keyval, b_value, w_out, attn_gain, attn_shift, code_col, doc_row,
        cotangent, w_down,
    )
    middle = inputs_f + project(mixed, all_out) + b_out
    normed_mlp = norm_rows(middle, mlp_gain, mlp_shift).astype(BF16)
    hidden = project(normed_mlp, w_up) + b_up
    acts = jax.nn.gelu(hidden, approximate=True).astype(BF16)
    grad_w_down = jnp.einsum("tf,td->fd", acts, cotangent, preferred_element_type=F32)
    _, gelu_pull = jax.vjp(functools.partial(jax.nn.gelu, approximate=True), hidden)
    d_hidden = gelu_pull(d_acts)[0].astype(BF16)
    grad_b_up = jnp.sum(d_hidden.astype(F32), axis=0)
    grad_w_up = jnp.einsum("td,tf->df", normed_mlp, d_hidden, preferred_element_type=F32)
    d_hidden, grad_w_up, grad_w_down = lax.optimization_barrier((d_hidden, grad_w_up, grad_w_down))
    grad_w_up = lax.psum_scatter(grad_w_up, "dp", scatter_dimension=0, tiled=True)
    grad_w_down = lax.psum_scatter(grad_w_down, "dp", scatter_dimension=1, tiled=True)

    d_middle, d_queries, feed_first, grads, d_keyval_sum, sums = mlp_attend_back(
        d_hidden, w_up, all_out, middle, cotangent, queries, acts, w_down, normed_attn, mixed, own_cols,
        keyval, keys_t, code_col, doc_row, lse, mlp_gain,
    )
    grads, grad_w_down, grad_w_up = lax.optimization_barrier((grads, grad_w_down, grad_w_up))
    grads = lax.psum_scatter(grads, "dp", scatter_dimension=1, tiled=True)
    outputs, input_grad, grad_w_keyval, totals = feed_and_input_grad(
        acts, w_down, middle, b_down, d_queries, all_query, d_keyval_sum, w_keyval, inputs, d_middle,
        attn_gain, normed_attn, feed_first, sums, grad_b_up,
    )
    grad_w_query, grad_w_out = grads[:own_cols].T, grads[own_cols:]
    grad_w_keyval = grad_w_keyval.T
    grad_attn_gain, grad_attn_shift, grad_mlp_gain, grad_mlp_shift = (totals[i] for i in range(4))
    grad_b_out, grad_b_down, grad_b_query, grad_b_up = (totals[i] for i in range(4, 8))
    grad_b_query = lax.dynamic_slice_in_dim(grad_b_query, own, own_cols, 0)
    grad_b_value = totals[8, :hd]
    return (
        outputs,
        input_grad,
        grad_attn_gain,
        grad_attn_shift,
        grad_w_query,
        grad_b_query,
        grad_w_keyval,
        grad_b_value,
        grad_w_out,
        grad_b_out,
        grad_mlp_gain,
        grad_mlp_shift,
        grad_w_up,
        grad_b_up,
        grad_w_down,
        grad_b_down,
    )


def solution(mesh):
    return jax.shard_map(
        shards,
        mesh=mesh,
        in_specs=(
            P("dp", None),
            P("dp", None),
            P("dp", None),
            P(),
            P(),
            P(None, "mp"),
            P("mp"),
            P(),
            P(),
            P("mp", None),
            P(),
            P(),
            P(),
            P(None, "mp"),
            P("mp"),
            P("mp", None),
            P(),
            P("dp", None),
        ),
        out_specs=(
            P("dp", None),
            P("dp", None),
            P(),
            P(),
            P("dp", "mp"),
            P("mp"),
            P(),
            P(),
            P("mp", "dp"),
            P(),
            P(),
            P(),
            P("dp", "mp"),
            P("mp"),
            P("mp", "dp"),
            P(),
        ),
        check_vma=False,
    )
```

```python
import functools
import math

import jax
import jax.numpy as jnp
from jax import lax
from jax.experimental import pallas as pl
from jax.experimental.pallas import tpu as pltpu
from jax.sharding import PartitionSpec as P

EPS = 1e-05
MESH = pl.DeviceIdType.MESH
F32 = jnp.float32
BF16 = jnp.bfloat16
VMEM_LIMIT = 60 * 2**20
HBM = pl.BlockSpec(memory_space=pl.ANY)


def norm_rows(rows_in, gain, shift):
    center = rows_in - jnp.mean(rows_in, axis=-1, keepdims=True)
    spread = jnp.mean(center * center, axis=-1, keepdims=True)
    return center * lax.rsqrt(spread + EPS) * gain + shift


def project(left, right):
    return jnp.dot(left, right, preferred_element_type=F32)


STRIP = 16
COLS = 512
BLOCK = 256
REACH = 3
GROUP = 4
NEG = -1e30
FRONT = (REACH - 1) * BLOCK


def key_window(c):
    first = max(0, c - REACH + 1) * BLOCK
    return first, (c + 1) * BLOCK - first


def mask_bias(code_col, doc_row, first_key, keys, first_query, queries):
    j = first_key + lax.broadcasted_iota(jnp.int32, (keys, queries), 0)
    i = first_query + lax.broadcasted_iota(jnp.int32, (keys, queries), 1)
    ok = ((j < i) & (code_col == doc_row)) | (j == i)
    return jnp.where(ok, 0.0, NEG)


def dot_t(a, b):
    return lax.dot_general(a, b, (((1,), (1,)), ((), ())), preferred_element_type=F32)


def rows_at(start, count):
    return pl.ds(pl.multiple_of(start, count), count)


def mp_partner(m, r):
    if r == 1:
        return m + 1 - 2 * lax.rem(m, 2)
    if r == 2:
        return m + 2 - 4 * lax.div(m, 2)
    return 3 - m


def flip_bit(d, bit):
    on = lax.rem(lax.div(d, bit), 2)
    return d + bit * (1 - 2 * on)


def front_kernel(
    heads,
    wq, wo, in_hbm, cot_hbm, w_down_hbm, bq, w_kv, gain_ref, shift_ref, bv_ref, code_ref, doc_ref,
    wq_out, wo_out, normed_hbm, q_hbm, mixed_hbm, d_acts_hbm, kv_ref, kt_ref, lse_ref,
    own_q, own_o, gq, go, sq, so, normed, q_ring, mixed_ring, vt, bias_ref, bq_all, cot, down, d_acts,
    load_sem, cot_sem, down_sem, d_acts_sem, ship_sem, o_sem, ring_sem, z_send, z_recv, b_send, b_recv, n_send, n_recv,
):
    m = lax.axis_index("mp")
    d = lax.axis_index("dp")
    dc, dx, dy = flip_bit(d, 1), flip_bit(d, 2), flip_bit(d, 4)
    dxy = flip_bit(dx, 4)
    is_mid = (m == 1) | (m == 2)
    buddy, across = {"mp": mp_partner(m, 1)}, {"mp": 3 - m}
    upper = lax.div(m, 2)
    inner = lax.rem(m + upper, 2)

    def plane_at(s):
        q = (1 - inner, 2, 3)[s]
        return q + upper * (3 - 2 * q)

    g = (gq, go)
    half = (gq.shape[2] // 2, go.shape[2] // 2)
    seq, width = normed.shape
    cols_q = q_ring.shape[2]
    hd = vt.shape[0]
    blocks = seq // BLOCK
    scale = 1.0 / math.sqrt(hd)
    planes = 4

    loads = [
        pltpu.make_async_copy(wq.at[d], own_q, load_sem.at[0]),
        pltpu.make_async_copy(wo.at[d], own_o, load_sem.at[1]),
        pltpu.make_async_copy(in_hbm, normed, load_sem.at[2]),
        pltpu.make_async_copy(wq, sq.at[m], load_sem.at[3]),
        pltpu.make_async_copy(wq, wq_out.at[m], load_sem.at[4]),
        pltpu.make_async_copy(wo, wo_out.at[m], load_sem.at[5]),
    ]
    for c in loads:
        c.start()
    bar = pltpu.get_barrier_semaphore()
    for r in (1, 2, 3):
        pl.semaphore_signal(bar, inc=1, device_id={"mp": mp_partner(m, r)}, device_id_type=MESH)
    for n in (dc, dx, dy):
        pl.semaphore_signal(bar, inc=1, device_id={"dp": n}, device_id_type=MESH)
    loads[0].wait()
    gq[m, d] = own_q[...].astype(F32)
    loads[1].wait()
    go[m, d] = own_o[...].astype(F32)
    bq_all[m] = bq[...]
    pl.semaphore_wait(bar, 6)

    def z_copy(w, plane, to, i):
        ref = g[w].at[plane, d]
        return pltpu.make_async_remote_copy(
            ref, ref, z_send.at[w, i], z_recv.at[w, plane], device_id=to, device_id_type=MESH
        )

    def z_own(w, wait=False):
        def go_or_wait(c):
            if wait:
                c.wait_send()
            else:
                c.start()

        go_or_wait(z_copy(w, m, buddy, 0))

        @pl.when(is_mid)
        def _():
            go_or_wait(z_copy(w, m, across, 1))

    def z_forward(w, s, wait=False):
        @pl.when(is_mid)
        def _():
            c = z_copy(w, plane_at(s), across if s == 0 else buddy, 2 + s)
            if wait:
                c.wait_send()
            else:
                c.start()

    def z_land(w, s):
        z_copy(w, plane_at(s), buddy, 0).wait_recv()

    def bias_copy(r, plane):
        return pltpu.make_async_remote_copy(
            bq_all.at[plane], bq_all.at[plane], b_send.at[r - 1], b_recv.at[r - 1],
            device_id={"mp": mp_partner(m, r)}, device_id_type=MESH,
        )

    sent_eighth = (d, d, d, dx, dy, dx, dy, dxy)
    landed_eighth = (dx, dy, dc, flip_bit(dx, 1), flip_bit(dy, 1), dxy, dxy, flip_bit(dxy, 1))
    sent_to = (dx, dy, dc, dc, dc, dy, dx, dc)

    def near(kind, w, r, eighths):
        q = plane_at(r)
        ref = g[w].at[q, eighths[kind]]
        if kind == 5:
            ref = g[w].at[q, eighths[kind], pl.ds(0, half[w])]
        if kind == 6:
            ref = g[w].at[q, eighths[kind], pl.ds(half[w], half[w])]
        return pltpu.make_async_remote_copy(
            ref, ref, n_send.at[kind, w, r], n_recv.at[kind, w, r],
            device_id={"dp": sent_to[kind]}, device_id_type=MESH,
        )

    def go_near(kind, w, r):
        near(kind, w, r, sent_eighth).start()

    def landed(kind, w, r):
        near(kind, w, r, landed_eighth).wait_recv()

    shipped = []
    ring = so.shape[0]

    def ship(w, r, eighth):
        q = plane_at(r)
        n = sum(1 for v, _ in shipped if v == w)
        if w == 0:
            sq[q, eighth] = gq[q, eighth].astype(BF16)
            c = pltpu.make_async_copy(sq.at[q, eighth], wq_out.at[q, eighth], ship_sem.at[n])
        else:
            slot = n % ring
            if n >= ring:
                [c for v, c in shipped if v == 1][n - ring].wait()
            so[slot] = go[q, eighth].astype(BF16)
            c = pltpu.make_async_copy(so.at[slot], wo_out.at[q, eighth], o_sem.at[slot])
        c.start()
        shipped.append((w, c))

    def store_q(q, c, slot):
        at = pl.ds(c * BLOCK, BLOCK)
        return pltpu.make_async_copy(
            q_ring.at[slot], q_hbm.at[at, rows_at(q * cols_q, cols_q)], ring_sem.at[0, slot]
        )

    def store_mixed(q, c, slot):
        at = pl.ds(c * BLOCK, BLOCK)
        return pltpu.make_async_copy(
            mixed_ring.at[slot], mixed_hbm.at[at, rows_at(q * cols_q, cols_q)], ring_sem.at[1, slot]
        )

    def set_bias(c):
        first, count = key_window(c)
        bias_ref[pl.ds(0, count), :] = mask_bias(
            code_ref[pl.ds(FRONT + first, count), :], doc_ref[:, pl.ds(c * BLOCK, BLOCK)],
            first, count, c * BLOCK, BLOCK,
        )

    def attend_block(q, c, n):
        slot = lax.rem(n, 2) if not isinstance(n, int) else n % 2
        first, count = key_window(c)
        keys, at = pl.ds(FRONT + first, count), pl.ds(c * BLOCK, BLOCK)

        def free():
            store_q(q, c, slot).wait()
            store_mixed(q, c, slot).wait()

        if not isinstance(n, int) or n >= 2:
            free()
        w = sq[q].reshape(width, cols_q)
        q_ring[slot] = (project(normed[at, :], w) + bq_all[q]).astype(BF16)
        store_q(q, c, slot).start()
        for u in range(cols_q // hd):
            head = pl.ds(u * hd, hd)
            s = dot_t(kv_ref[keys, pl.ds(0, hd)], q_ring[slot, :, head]) * scale
            s = s + bias_ref[pl.ds(0, count), :]
            top = jnp.max(s, axis=0, keepdims=True)
            e = jnp.exp(s - top)
            total = jnp.sum(e, axis=0, keepdims=True)
            probs = (e * (1.0 / total)).astype(BF16)
            mixed_ring[slot, :, head] = project(vt[:, pl.ds(first, count)], probs).T.astype(BF16)
            lse_ref[pl.ds(q * (cols_q // hd) + u, 1), at] = top + jnp.log(total)
        store_mixed(q, c, slot).start()

    bands = w_down_hbm.shape[0] // down.shape[1]

    def load_cot(i):
        at = rows_at(lax.rem(i, blocks) * BLOCK, BLOCK)
        slot = lax.rem(i, 2)
        return pltpu.make_async_copy(cot_hbm.at[at], cot.at[slot], cot_sem.at[slot])

    def load_down(n):
        at = pl.ds(n * down.shape[1], down.shape[1])
        return pltpu.make_async_copy(w_down_hbm.at[at], down.at[n % 2], down_sem.at[n % 2])

    def store_d_acts(n, i):
        slot = lax.rem(i, 2)
        rows = rows_at(lax.rem(i, blocks) * BLOCK, BLOCK)
        cols = pl.ds(n * down.shape[1], down.shape[1])
        return pltpu.make_async_copy(
            d_acts.at[slot], d_acts_hbm.at[rows, cols], d_acts_sem.at[slot]
        )

    def d_acts_band(n):
        load_down(n).wait()
        if n + 1 < bands:
            load_down(n + 1).start()

        def one(i, carry):
            slot = lax.rem(i, 2)
            load_cot(i).wait()

            @pl.when(i + 1 < bands * blocks)
            def _():
                load_cot(i + 1).start()

            @pl.when(i >= 2)
            def _():
                store_d_acts(n, i).wait()

            d_acts[slot] = dot_t(cot[slot], down[n % 2])
            store_d_acts(n, i).start()
            return carry

        lax.fori_loop(n * blocks, (n + 1) * blocks, one, 0)

    def own_plane(c):
        set_bias(c)
        attend_block(m, c, c)

    def other_planes(c, first, end):
        if first == 1:
            set_bias(c)

        def one(r, carry):
            attend_block(lax.rem(m + r, planes), c, blocks + c * (planes - 1) + r - 1)
            return carry

        lax.fori_loop(first, end, one, 0)

    stream = [(w, r) for w in (0, 1) for r in range(3)]

    def pass_on(i):
        w, s = stream[i]

        @pl.when(is_mid)
        def _():
            z_land(w, s)
            z_forward(w, s)

        if i == 2:
            z_own(1)

    def from_line(i):
        w, s = stream[i]

        @pl.when(jnp.logical_not(is_mid))
        def _():
            z_land(w, s)

        for kind in (0, 1, 2):
            go_near(kind, w, s)
        ship(w, s, d)

    def from_near(i):
        w, s = stream[i]
        landed(0, w, s)
        go_near(5, w, s)
        go_near(3, w, s)
        ship(w, s, dx)
        landed(1, w, s)
        go_near(6, w, s)
        go_near(4, w, s)
        ship(w, s, dy)
        landed(2, w, s)
        ship(w, s, dc)

    def from_far(i):
        w, s = stream[i]
        landed(5, w, s)
        landed(6, w, s)
        go_near(7, w, s)
        ship(w, s, dxy)
        for kind in (3, 4):
            landed(kind, w, s)
            ship(w, s, landed_eighth[kind])
        landed(7, w, s)
        ship(w, s, landed_eighth[7])

    z_own(0)
    for r in (1, 2, 3):
        bias_copy(r, m).start()

    load_down(0).start()
    load_cot(0).start()
    loads[2].wait()

    def norm_strip(i, carry):
        at = rows_at(i * STRIP, STRIP)
        normed[at, :] = norm_rows(normed[at, :].astype(F32), gain_ref[...], shift_ref[...]).astype(BF16)
        return carry

    lax.fori_loop(0, seq // STRIP, norm_strip, 0)
    keep_normed = pltpu.make_async_copy(normed, normed_hbm, load_sem.at[2])
    keep_normed.start()
    kv_ref[pl.ds(0, FRONT), :] = jnp.zeros((FRONT, 2 * hd), BF16)
    kt_ref[:, pl.ds(0, FRONT)] = jnp.zeros((hd, FRONT), BF16)
    for c in range(blocks):
        at, put = pl.ds(c * BLOCK, BLOCK), pl.ds(FRONT + c * BLOCK, BLOCK)
        kv = project(normed[at, :], w_kv[...])
        keys, values = kv[:, :hd], kv[:, hd:] + bv_ref[...]
        kv_ref[put, pl.ds(0, hd)] = keys.astype(BF16)
        kv_ref[put, pl.ds(hd, hd)] = values.astype(BF16)
        kt_ref[:, put] = keys.T.astype(BF16)
        vt[:, at] = values.T.astype(BF16)
    loads[3].wait()

    def stage(s):
        if s == 0:
            pass_on(0)
        if s + 1 < len(stream):
            pass_on(s + 1)
        if s < len(stream):
            from_line(s)
        if 1 <= s <= len(stream):
            from_near(s - 1)
        if s >= 2:
            from_far(s - 2)

    stage(0)
    own_plane(0)
    own_plane(1)
    stage(1)
    own_plane(2)
    own_plane(3)
    stage(2)
    for n in range(bands // 2):
        d_acts_band(n)
    stage(3)
    for n in range(bands // 2, bands):
        d_acts_band(n)
    for r in (1, 2, 3):
        bias_copy(r, mp_partner(m, r)).wait_recv()
    stage(4)
    other_planes(0, 1, planes)
    other_planes(1, 1, planes)
    from_line(5)
    other_planes(2, 1, 2)
    from_near(4)
    other_planes(2, 2, planes)
    from_far(3)
    other_planes(3, 1, 2)
    from_near(5)
    other_planes(3, 2, planes)
    from_far(4)
    from_far(5)

    for i in (0, 1):
        store_d_acts(0, i).wait()
    for slot in (0, 1):
        store_q(m, 0, slot).wait()
        store_mixed(m, 0, slot).wait()
    for w in (0, 1):
        z_own(w, wait=True)
    for w, r in stream:
        z_forward(w, r, wait=True)
        for kind in range(8):
            near(kind, w, r, sent_eighth).wait_send()
    for r in (1, 2, 3):
        bias_copy(r, m).wait_send()
    rows_o = [c for v, c in shipped if v == 1]
    for c in [c for v, c in shipped if v == 0] + rows_o[-ring:]:
        c.wait()
    keep_normed.wait()
    loads[4].wait()
    loads[5].wait()


def gather_by_sum(shard):
    blank = jnp.zeros((lax.axis_size("mp"),) + shard.shape, F32)
    half = shard.astype(F32) * 0.5
    own = lax.dynamic_update_index_in_dim(blank, half, lax.axis_index("mp"), 0)
    return lax.psum(own, "mp") * 2.0


def attention_front(
    inputs, w_query, b_query, w_keyval, b_value, w_out, gain, shift, code_col, doc_row, cotangent, w_down
):
    dp, mp = lax.axis_size("dp"), lax.axis_size("mp")
    width, cols = w_query.shape
    rows = w_out.shape[0]
    seq = inputs.shape[0]
    hd = w_keyval.shape[1] // 2
    if (dp, mp) != (8, 4):
        all_query, all_out, all_bias = (
            gather_by_sum(a).astype(a.dtype) for a in (w_query, w_out, b_query)
        )
        normed = norm_rows(inputs.astype(F32), gain, shift).astype(BF16)
        kv_bias = jnp.concatenate([jnp.zeros((hd,), F32), b_value])
        keyval = (project(normed, w_keyval) + kv_bias).astype(BF16)
        queries = jnp.concatenate(
            [project(normed, all_query[i]) + all_bias[i] for i in range(mp)], 1
        ).astype(BF16)
        mixed, lse = attend(queries, keyval, code_col[FRONT:], doc_row)
        keyval = jnp.pad(keyval, ((FRONT, 0), (0, 0)))
        keys_t = keyval[:, :hd].T
        d_acts = jnp.einsum("td,fd->tf", cotangent, w_down, preferred_element_type=F32)
        return all_query, all_out.reshape(-1, width), normed, queries, mixed, d_acts, keyval, keys_t, lse
    wq = w_query.reshape(dp, width // dp, cols)
    wo = w_out.reshape(dp, rows // dp, width)
    dma = pltpu.SemaphoreType.DMA
    vmem = pl.BlockSpec(memory_space=pltpu.VMEM)
    full_q, full_o = (mp,) + wq.shape, (mp,) + wo.shape
    heads = mp * cols // hd
    shape = jax.ShapeDtypeStruct
    out_q, out_o, normed, queries, mixed, d_acts, keyval, keys_t, lse = pl.pallas_call(
        functools.partial(front_kernel, heads),
        out_shape=(
            shape(full_q, BF16),
            shape(full_o, BF16),
            shape((seq, width), BF16),
            shape((seq, mp * cols), BF16),
            shape((seq, mp * cols), BF16),
            shape((seq, w_down.shape[0]), F32),
            shape((FRONT + seq, 2 * hd), BF16),
            shape((hd, FRONT + seq), BF16),
            shape((heads, seq), F32),
        ),
        in_specs=[HBM] * 5 + [vmem] * 7,
        out_specs=(HBM,) * 6 + (vmem,) * 3,
        scratch_shapes=[
            pltpu.VMEM(wq.shape[1:], BF16),
            pltpu.VMEM(wo.shape[1:], BF16),
            pltpu.VMEM(full_q, F32),
            pltpu.VMEM(full_o, F32),
            pltpu.VMEM(full_q, BF16),
            pltpu.VMEM((4,) + wo.shape[1:], BF16),
            pltpu.VMEM((seq, width), BF16),
            pltpu.VMEM((2, BLOCK, cols), BF16),
            pltpu.VMEM((2, BLOCK, cols), BF16),
            pltpu.VMEM((hd, seq), BF16),
            pltpu.VMEM((REACH * BLOCK, BLOCK), F32),
            pltpu.VMEM((mp, 1, cols), F32),
            pltpu.VMEM((2, BLOCK, width), BF16),
            pltpu.VMEM((2, COLS, width), BF16),
            pltpu.VMEM((2, BLOCK, COLS), F32),
            dma((6,)),
            dma((2,)),
            dma((2,)),
            dma((2,)),
            dma((3 * dp,)),
            dma((4,)),
            dma((2, 2)),
            dma((2, 5)),
            dma((2, mp)),
            dma((3,)),
            dma((3,)),
            dma((8, 2, 3)),
            dma((8, 2, 3)),
        ],
        compiler_params=pltpu.CompilerParams(
            collective_id=0, has_side_effects=True, vmem_limit_bytes=VMEM_LIMIT
        ),
        name="attention_front",
    )(
        wq, wo, inputs, cotangent, w_down, b_query.reshape(1, cols), w_keyval, gain.reshape(1, width),
        shift.reshape(1, width), b_value.reshape(1, hd), code_col, doc_row,
    )
    return (
        out_q.reshape(mp, width, cols), out_o.reshape(mp * rows, width),
        normed, queries, mixed, d_acts, keyval, keys_t, lse,
    )


PIECE = 32
SLOT = 1
CROSS_LATE = 2 * SLOT
LATE = 5 * SLOT
AHEAD = 3 * SLOT


class LineSum:
    scratch = staticmethod(
        lambda rows, pieces, width: [pltpu.VMEM((rows, width), F32)] * 3
        + [pltpu.SemaphoreType.DMA((pieces,))] * 5
    )

    def __init__(self, refs):
        self.part, self.total, self.cross, *sems = refs
        self.in_send, self.in_recv, self.over_send, self.over_recv, self.out_send = sems
        self.slots = self.part.shape[0] // PIECE
        self.pieces = self.in_send.shape[0]
        m = lax.axis_index("mp")
        self.is_end = (m == 0) | (m == 3)
        self.is_mid = (m == 1) | (m == 2)
        self.buddy = {"mp": mp_partner(m, 1)}
        self.across = {"mp": 3 - m}

    def greet(self, others=()):
        bar = pltpu.get_barrier_semaphore()
        pl.semaphore_signal(bar, inc=1, device_id=self.buddy, device_id_type=MESH)
        for other in others:
            pl.semaphore_signal(bar, inc=1, device_id=other, device_id_type=MESH)

        @pl.when(self.is_mid)
        def _():
            pl.semaphore_signal(bar, inc=1, device_id=self.across, device_id_type=MESH)

    def meet(self, others=()):
        bar = pltpu.get_barrier_semaphore()

        @pl.when(self.is_end)
        def _():
            pl.semaphore_wait(bar, 1 + len(others))

        @pl.when(self.is_mid)
        def _():
            pl.semaphore_wait(bar, 2 + len(others))

    def at(self, k):
        slot = k if self.slots == self.pieces else k % self.slots
        return rows_at(slot * PIECE, PIECE)

    def inward(self, k):
        at = self.at(k)
        return pltpu.make_async_remote_copy(
            self.part.at[at], self.total.at[at], self.in_send.at[k], self.in_recv.at[k],
            device_id=self.buddy, device_id_type=MESH,
        )

    def over(self, k):
        at = self.at(k)
        return pltpu.make_async_remote_copy(
            self.part.at[at], self.cross.at[at], self.over_send.at[k], self.over_recv.at[k],
            device_id=self.across, device_id_type=MESH,
        )

    def outward(self, k):
        at = self.at(k)
        return pltpu.make_async_remote_copy(
            self.total.at[at], self.total.at[at], self.out_send.at[k], self.in_recv.at[k],
            device_id=self.buddy, device_id_type=MESH,
        )

    def slot(self, i):
        for j in range(SLOT):
            self.tick(i * SLOT + j)

    def tick(self, k):
        n = self.pieces

        @pl.when(self.is_end)
        def _():
            @pl.when(k < n)
            def _():
                @pl.when(k >= AHEAD)
                def _():
                    self.inward(k - AHEAD).wait_send()

                self.inward(k).start()

            @pl.when((k >= LATE) & (k < n + LATE))
            def _():
                self.outward(k - LATE).wait_recv()

        @pl.when(self.is_mid)
        def _():
            @pl.when(k < n)
            def _():
                at = self.at(k)
                self.inward(k).wait_recv()
                self.part[at, :] += self.total[at, :]
                self.over(k).start()

            @pl.when((k >= CROSS_LATE) & (k < n + CROSS_LATE))
            def _():
                j = k - CROSS_LATE
                at = self.at(j)
                self.over(j).wait_recv()
                self.total[at, :] = self.part[at, :] + self.cross[at, :]
                self.outward(j).start()

    def free(self, first, count):
        @pl.when(self.is_mid)
        def _():
            def sent(k, c):
                self.over(k).wait_send()
                self.outward(k).wait_send()
                return c

            lax.fori_loop(first, first + count, sent, 0)

    def finish(self, freed=0):
        n = self.pieces

        @pl.when(self.is_end)
        def _():
            for k in range(n - AHEAD, n):
                self.inward(k).wait_send()

        self.free(freed, n - freed)


def attend_kernel(seq, heads, q_ref, kv_ref, vt_ref, code_ref, doc_ref, mixed_ref, lse_ref, bias_ref):
    hd = vt_ref.shape[0]
    scale = 1.0 / math.sqrt(hd)
    for c in range(seq // BLOCK):

        @pl.when(pl.program_id(0) == c)
        def _(c=c):
            first, count = key_window(c)
            keys = pl.ds(first, count)
            bias_ref[pl.ds(0, count), :] = mask_bias(
                code_ref[keys, :], doc_ref[...], first, count, c * BLOCK, BLOCK
            )

            def some_heads(g, carry):
                for u in range(GROUP):
                    h = g * GROUP + u
                    cols = pl.ds(pl.multiple_of(h * hd, hd), hd)
                    s = dot_t(kv_ref[keys, pl.ds(0, hd)], q_ref[:, cols]) * scale
                    s = s + bias_ref[pl.ds(0, count), :]
                    top = jnp.max(s, axis=0, keepdims=True)
                    e = jnp.exp(s - top)
                    total = jnp.sum(e, axis=0, keepdims=True)
                    probs = (e * (1.0 / total)).astype(BF16)
                    mixed = project(vt_ref[:, keys], probs)
                    mixed_ref[:, cols] = mixed.T.astype(BF16)
                    lse_ref[pl.ds(h, 1), :] = top + jnp.log(total)
                return carry

            lax.fori_loop(0, heads // GROUP, some_heads, 0)


def attend(queries, keyval, code_col, doc_row):
    seq, width = queries.shape
    hd = keyval.shape[1] // 2
    heads = width // hd
    values_t = keyval[:, hd:].T
    whole = lambda *shape: pl.BlockSpec(shape, lambda c: (0,) * len(shape))
    return pl.pallas_call(
        functools.partial(attend_kernel, seq, heads),
        grid=(seq // BLOCK,),
        out_shape=(
            jax.ShapeDtypeStruct((seq, width), BF16),
            jax.ShapeDtypeStruct((heads, seq), F32),
        ),
        in_specs=[
            pl.BlockSpec((BLOCK, width), lambda c: (c, 0)),
            whole(seq, 2 * hd),
            whole(hd, seq),
            whole(seq, 1),
            pl.BlockSpec((1, BLOCK), lambda c: (0, c)),
        ],
        out_specs=(
            pl.BlockSpec((BLOCK, width), lambda c: (c, 0)),
            pl.BlockSpec((heads, BLOCK), lambda c: (0, c)),
        ),
        scratch_shapes=[pltpu.VMEM((REACH * BLOCK, BLOCK), F32)],
        compiler_params=pltpu.CompilerParams(vmem_limit_bytes=VMEM_LIMIT),
        name="attend",
    )(queries, keyval, values_t, code_col, doc_row)


def norm_back_rows(x, grad, gain):
    mean = jnp.mean(x, axis=-1, keepdims=True)
    center = x - mean
    scale = lax.rsqrt(jnp.mean(center * center, axis=-1, keepdims=True) + EPS)
    xhat = center * scale
    e = grad * gain
    weighted = grad * xhat
    d_in = scale * (
        e - jnp.mean(e, axis=-1, keepdims=True) - xhat * jnp.mean(e * xhat, axis=-1, keepdims=True)
    )
    return d_in, weighted


def dot_down(a, b):
    return lax.dot_general(a, b, (((0,), (0,)), ((), ())), preferred_element_type=F32)


def fold_rows(x):
    return jnp.sum(x.reshape(-1, 8, x.shape[-1]), axis=0)


FEED_EARLY = 2

GELU_A = math.sqrt(2.0 / math.pi)
GELU_B = 0.044715


def gelu_pair(u):
    square = u * u
    t = jnp.tanh(u * (GELU_A + GELU_A * GELU_B * square))
    cdf = 0.5 * (1.0 + t)
    slope = cdf + 0.5 * u * (1.0 - t * t) * (GELU_A + 3.0 * GELU_A * GELU_B * square)
    return u * cdf, slope


def mlp_kernel(
    mixed_hbm, w_out_hbm, in_hbm, w_up_hbm, d_acts_hbm, cot_hbm,
    b_out_ref, gain_ref, shift_ref, b_up_ref,
    mid_hbm, acts_hbm, dh_hbm, down_hbm, up_hbm, first_hbm, b_up_sum,
    w_out, w_up, normed, acts, dh, cot, mixed, xs, mid, d_acts, turned, tiles,
    load_sem, out_sem, tile_sem, *line_refs,
):
    line = LineSum(line_refs)
    seq, width = normed.shape
    blocks = seq // BLOCK
    hidden = w_up.shape[1]

    def load(i, src, dst):
        return pltpu.make_async_copy(src, dst, load_sem.at[i])

    def load_block(c):
        at = pl.ds(c * BLOCK, BLOCK)
        return [
            load(2, mixed_hbm.at[at], mixed),
            load(3, in_hbm.at[at], xs),
        ]

    def load_d_acts(c):
        return load(4, d_acts_hbm.at[pl.ds(c * BLOCK, BLOCK)], d_acts)

    def store_mid(c):
        return pltpu.make_async_copy(mid, mid_hbm.at[pl.ds(c * BLOCK, BLOCK)], out_sem.at[0])

    store_acts = pltpu.make_async_copy(acts, acts_hbm, out_sem.at[1])
    store_dh = pltpu.make_async_copy(dh, dh_hbm, out_sem.at[2])

    load(0, w_out_hbm, w_out).start()
    for i in load_block(0):
        i.start()
    load(1, w_up_hbm, w_up).start()
    load_d_acts(0).start()
    load(5, cot_hbm, cot).start()
    line.greet()
    b_up_sum[...] = jnp.zeros_like(b_up_sum)

    def middle_step(c):
        for i in load_block(c):
            i.wait()
        if c >= 1:
            store_mid(c - 1).wait()

        def cols(n, carry):
            there = rows_at(n * COLS, COLS)
            mid[:, there] = (
                project(mixed[...], w_out[:, there]) + xs[:, there].astype(F32) + b_out_ref[:, there]
            )
            return carry

        lax.fori_loop(0, width // COLS, cols, 0)
        store_mid(c).start()
        if c + 1 < blocks:
            for i in load_block(c + 1):
                i.start()

    def norm_step(c):
        def strip(i, carry):
            at = rows_at(i * STRIP, STRIP)
            put = rows_at(c * BLOCK + i * STRIP, STRIP)
            normed[put, :] = norm_rows(mid[at, :], gain_ref[...], shift_ref[...]).astype(BF16)
            return carry

        lax.fori_loop(0, BLOCK // STRIP, strip, 0)

    def hidden_step(c):
        at = pl.ds(c * BLOCK, BLOCK)
        load_d_acts(c).wait()

        def cols(n, carry):
            there = rows_at(n * COLS, COLS)
            u = project(normed[at, :], w_up[:, there]) + b_up_ref[:, there]
            value, slope = gelu_pair(u)
            acts[at, there] = value.astype(BF16)
            low = (d_acts[:, there] * slope).astype(BF16)
            dh[at, there] = low
            b_up_sum[:, there] += fold_rows(low.astype(F32))
            return carry

        lax.fori_loop(0, hidden // COLS, cols, 0)
        if c + 1 < blocks:
            load_d_acts(c + 1).start()
        else:
            store_acts.start()
            store_dh.start()

    def produce():
        def cols(n, carry):
            there = rows_at(n * COLS, COLS)
            line.part[:, there] = dot_t(dh[pl.ds(0, BLOCK), :], w_up[there, :])
            return carry

        lax.fori_loop(0, width // COLS, cols, 0)

    tile_rows, tile_cols = tiles.shape[1:]
    tile_list = []
    for left, right, out in ((acts, cot, down_hbm), (normed, dh, up_hbm)):
        for row in range(0, left.shape[1], tile_rows):
            for col in range(0, right.shape[1], tile_cols):
                tile_list.append((left, right, out, row, col))

    def store_tile(i):
        _, _, out, row, col = tile_list[i]
        return pltpu.make_async_copy(
            tiles.at[i % 2], out.at[pl.ds(row, tile_rows), pl.ds(col, tile_cols)], tile_sem.at[i % 2]
        )

    def tile_step(i):
        left, right, _, row, col = tile_list[i]
        if col == 0:
            turned[...] = left[:, pl.ds(row, tile_rows)].T
        if i >= 2:
            store_tile(i - 2).wait()

        def cols(n, carry):
            there, put = rows_at(col + n * COLS, COLS), rows_at(n * COLS, COLS)
            tiles[i % 2, :, put] = project(turned[...], right[:, there])
            return carry

        lax.fori_loop(0, tile_cols // COLS, cols, 0)
        store_tile(i).start()

    load(0, w_out_hbm, w_out).wait()
    middle_step(0)
    norm_step(0)
    load(1, w_up_hbm, w_up).wait()
    hidden_step(0)
    produce()
    line.meet()
    load(5, cot_hbm, cot).wait()
    steps = []
    for c in range(1, blocks):
        steps.append([functools.partial(f, c) for f in (middle_step, norm_step)])
        steps.append([functools.partial(hidden_step, c)])
    slots = (line.pieces + LATE) // SLOT
    count = len(tile_list)
    per = -(-count // max(slots - len(steps), 1))
    for i in range(0, count, per):
        steps.append([functools.partial(tile_step, j) for j in range(i, min(i + per, count))])
    for i in range(max(slots, len(steps))):
        if i < slots:
            line.slot(i)
        if i < len(steps):
            for step in steps[i]:
                step()
    store_first = pltpu.make_async_copy(line.total, first_hbm, out_sem.at[3])
    store_first.start()
    store_tile(count - 2).wait()
    store_tile(count - 1).wait()
    store_mid(blocks - 1).wait()
    store_acts.wait()
    store_dh.wait()
    store_first.wait()
    line.finish()


def mlp(mixed, w_out, inputs, w_up, d_acts, cotangent, b_out, gain, shift, b_up):
    seq, width = inputs.shape
    hidden = w_up.shape[1]
    vmem = pl.BlockSpec(memory_space=pltpu.VMEM)
    dma = pltpu.SemaphoreType.DMA
    shape = jax.ShapeDtypeStruct
    block = lambda cols, dtype: pltpu.VMEM((BLOCK, cols), dtype)
    return pl.pallas_call(
        mlp_kernel,
        out_shape=(
            shape((seq, width), F32),
            shape((seq, hidden), BF16),
            shape((seq, hidden), BF16),
            shape((hidden, width), F32),
            shape((width, hidden), F32),
            shape((BLOCK, width), F32),
            shape((8, hidden), F32),
        ),
        in_specs=[HBM] * 6 + [vmem] * 4,
        out_specs=(HBM,) * 6 + (vmem,),
        scratch_shapes=[
            pltpu.VMEM(w_out.shape, BF16),
            pltpu.VMEM(w_up.shape, BF16),
            pltpu.VMEM((seq, width), BF16),
            pltpu.VMEM((seq, hidden), BF16),
            pltpu.VMEM((seq, hidden), BF16),
            pltpu.VMEM((seq, width), BF16),
            block(w_out.shape[0], BF16),
            block(width, BF16),
            block(width, F32),
            block(hidden, F32),
            pltpu.VMEM((2 * BLOCK, seq), BF16),
            pltpu.VMEM((2, 2 * BLOCK, width // 2), F32),
            dma((6,)),
            dma((4,)),
            dma((2,)),
        ]
        + LineSum.scratch(BLOCK, BLOCK // PIECE, width),
        compiler_params=pltpu.CompilerParams(
            collective_id=3, has_side_effects=True, vmem_limit_bytes=VMEM_LIMIT
        ),
        cost_estimate=pl.CostEstimate(flops=60 * 10**9, bytes_accessed=2**26, transcendentals=0),
        name="mlp",
    )(
        mixed, w_out, inputs, w_up, d_acts, cotangent, b_out.reshape(1, width),
        gain.reshape(1, width), shift.reshape(1, width), b_up.reshape(1, hidden),
    )


def mlp_attend_back_kernel(
    heads,
    dh_hbm, w_up_hbm, w_out_hbm, mid_hbm, cot_hbm, q_hbm, acts_hbm, w_down_hbm, normed_hbm, mixed_hbm,
    first_hbm,
    kv_ref, kt_ref, code_ref, doc_ref, lse_ref, gain_ref, b_down_ref,
    d_mid_hbm, dq_hbm, feed_out, grads_hbm, dkv_ref, sums_ref,
    w_up, w_out, dh, mid, cot, q, normed, mixed, d_branch, d_mixed, dq, grads, bias_ref,
    load_sem, out_sem, *line_refs,
):
    line = LineSum(line_refs)
    seq, width = q_hbm.shape
    m = lax.axis_index("mp")
    own_cols = mixed.shape[1]
    own = rows_at(m * own_cols, own_cols)
    ring = line.part.shape[0] // BLOCK
    hd = kt_ref.shape[0]
    chunks = seq // BLOCK
    slots = BLOCK // (PIECE * SLOT)
    count = REACH * BLOCK
    scale = 1.0 / math.sqrt(hd)

    def load(i, src, dst):
        return pltpu.make_async_copy(src, dst, load_sem.at[i])

    def load_dh(b):
        return load(2, dh_hbm.at[rows_at((b + 1) * BLOCK, BLOCK)], dh)

    def load_chunk(c):
        at = rows_at(c * BLOCK, BLOCK)
        return [
            load(3, mid_hbm.at[at], mid),
            load(4, cot_hbm.at[at], cot),
            load(5, q_hbm.at[at], q),
            load(6, normed_hbm.at[at], normed),
            load(7, mixed_hbm.at[at, own], mixed),
        ]

    def block_at(b):
        return rows_at((b % ring) * BLOCK, BLOCK)

    load_first = load(8, first_hbm, line.total.at[block_at(ring - 1)])

    def store(i, src, dst, c):
        return pltpu.make_async_copy(src, dst.at[rows_at(c * BLOCK, BLOCK)], out_sem.at[i])

    def stores(c, which=(0, 1)):
        pairs = ((mid, d_mid_hbm), (dq, dq_hbm))
        return [store(i, *pairs[i], c) for i in which]

    load(0, w_up_hbm, w_up).start()
    load_dh(0).start()
    load(1, w_out_hbm, w_out).start()
    load_first.start()
    load_down = load(0, w_down_hbm, w_up)

    def load_acts(j):
        return load(2, acts_hbm.at[rows_at(j * BLOCK, BLOCK)], dh)

    def load_mid(j):
        return load(3, mid_hbm.at[rows_at(j * BLOCK, BLOCK)], mid)

    line.greet()
    dkv_ref[...] = jnp.zeros_like(dkv_ref)
    sums_ref[...] = jnp.zeros_like(sums_ref)
    grads[...] = jnp.zeros_like(grads)

    lines = chunks - 1

    def produce(b):
        at = block_at(b)
        load_dh(b).wait()

        def cols(n, carry):
            there = rows_at(n * COLS, COLS)
            line.part[at, there] = dot_t(dh[...], w_up[there, :])
            return carry

        lax.fori_loop(0, width // COLS, cols, 0)

        @pl.when(b + 1 < lines)
        def _():
            load_dh(b + 1).start()

        @pl.when(b + 1 == lines)
        def _():
            load_acts(0).start()
            load_down.start()

    def produce_feed(j):
        at = block_at(lines + j)
        load_acts(j).wait()
        load_mid(j).wait()

        @pl.when(j == 0)
        def _():
            load_down.wait()

        def cols(n, carry):
            there = rows_at(n * COLS, COLS)
            line.part[at, there] = project(dh[...], w_up[:, there])
            return carry

        lax.fori_loop(0, width // COLS, cols, 0)

        @pl.when(m == 0)
        def _():
            line.part[at, :] += mid[...]

        @pl.when(j + 1 < FEED_EARLY)
        def _():
            load_acts(j + 1).start()

    def add_grads(first, left, right):
        at = pl.ds(first, own_cols)

        def cols(n, carry):
            there = rows_at(n * COLS, COLS)
            grads[at, there] += dot_down(left, right[:, there])
            return carry

        lax.fori_loop(0, width // COLS, cols, 0)

    def norm_step(c, half):
        def strip(i, carry):
            row = half * (BLOCK // 2) + i * STRIP
            at = rows_at(row, STRIP)
            grad = line.total[rows_at(((c + ring - 1) % ring) * BLOCK + row, STRIP), :]
            d_in, weighted = norm_back_rows(mid[at, :], grad, gain_ref[...])
            cot_rows = cot[at, :].astype(F32)
            d_mid = cot_rows + d_in
            low = d_mid.astype(BF16)
            mid[at, :] = d_mid
            d_branch[at, :] = low
            sums_ref[0] += fold_rows(weighted)
            sums_ref[1] += fold_rows(grad)
            sums_ref[2] += fold_rows(low.astype(F32))
            sums_ref[3] += fold_rows(cot_rows)
            return carry

        lax.fori_loop(0, BLOCK // 2 // STRIP, strip, 0)

    def mixed_step(c):
        def cols(n, carry):
            there = rows_at(n * COLS, COLS)
            d_mixed[:, there] = dot_t(d_branch[...], w_out[there, :]).astype(BF16)
            return carry

        lax.fori_loop(0, width // COLS, cols, 0)
        keys = pl.ds(pl.multiple_of(c * BLOCK, BLOCK), count)
        bias_ref[...] = mask_bias(
            code_ref[keys, :], doc_ref[:, rows_at(c * BLOCK, BLOCK)],
            (c - REACH + 1) * BLOCK, count, c * BLOCK, BLOCK,
        )

    def heads_step(c, g):
        keys = pl.ds(pl.multiple_of(c * BLOCK, BLOCK), count)
        queries = rows_at(c * BLOCK, BLOCK)
        dk = jnp.zeros((count, hd), F32)
        dv = jnp.zeros((count, hd), F32)
        for u in range(GROUP):
            h = g * GROUP + u
            cols = rows_at(h * hd, hd)
            qh = q[:, cols]
            dm = d_mixed[:, cols]
            s = dot_t(kv_ref[keys, pl.ds(0, hd)], qh) * scale + bias_ref[...]
            probs = jnp.exp(s - lse_ref[pl.ds(h, 1), queries])
            d_probs = dot_t(kv_ref[keys, pl.ds(hd, hd)], dm)
            t = probs * d_probs
            inner = jnp.sum(t, axis=0, keepdims=True)
            ds = (t - probs * inner).astype(BF16)
            dqh = project(kt_ref[:, keys], ds) * scale
            dq[:, cols] = dqh.T.astype(BF16)
            dk = dk + project(ds, qh)
            dv = dv + project(probs.astype(BF16), dm)
        dkv_ref[keys, pl.ds(0, hd)] += dk * scale
        dkv_ref[keys, pl.ds(hd, hd)] += dv

    load(0, w_up_hbm, w_up).wait()
    produce(0)
    line.meet()
    for k in range(3):
        line.slot(k)
    load(1, w_out_hbm, w_out).wait()
    load_first.wait()

    def cycle(c, carry):
        base = c * slots + 3

        @pl.when(c >= 1)
        def _():
            for i in stores(c - 1):
                i.wait()

        @pl.when(c + 1 >= lines)
        def _():
            load_mid(c + 1 - lines).start()

        line.slot(base)

        @pl.when(c >= 2)
        def _():
            line.free((c - 2) * (BLOCK // PIECE), BLOCK // PIECE)

        @pl.when(c + 1 < lines)
        def _():
            produce(c + 1)

        @pl.when(c + 1 >= lines)
        def _():
            produce_feed(c + 1 - lines)

        for i in load_chunk(c):
            i.start()
        line.slot(base + 1)
        for i in load_chunk(c):
            i.wait()
        norm_step(c, 0)
        line.slot(base + 2)
        norm_step(c, 1)
        stores(c, (0,))[0].start()
        line.slot(base + 3)
        mixed_step(c)
        add_grads(own_cols, mixed[...], d_branch)

        def some_heads(g, carry):
            line.slot(base + 4 + g)
            heads_step(c, g)
            return carry

        lax.fori_loop(0, heads // GROUP, some_heads, 0)
        stores(c, (1,))[0].start()
        add_grads(0, dq[:, own], normed)

        def strip(i, carry):
            sums_ref[4] += fold_rows(dq[rows_at(i * STRIP, STRIP), :].astype(F32))
            return carry

        lax.fori_loop(0, BLOCK // STRIP, strip, 0)
        return carry

    lax.fori_loop(0, chunks, cycle, 0)
    keep_grads = pltpu.make_async_copy(grads, grads_hbm, out_sem.at[3])
    keep_grads.start()
    for k in range(chunks * slots + 3, (line.pieces + LATE) // SLOT):
        line.slot(k)
    for i in stores(chunks - 1):
        i.wait()
    keep_feed = []
    for j, low in enumerate((d_branch, d_mixed)):

        def strip(i, carry, j=j, low=low):
            total = line.total[rows_at((lines + j) % ring * BLOCK + i * STRIP, STRIP), :]
            low[rows_at(i * STRIP, STRIP), :] = (total + b_down_ref[...]).astype(BF16)
            return carry

        lax.fori_loop(0, BLOCK // STRIP, strip, 0)
        keep_feed.append(
            pltpu.make_async_copy(low, feed_out.at[pl.ds(j * BLOCK, BLOCK)], out_sem.at[j])
        )
        keep_feed[j].start()
    for i in keep_feed:
        i.wait()
    keep_grads.wait()
    line.finish((lines - 1) * (BLOCK // PIECE))


def mlp_attend_back(
    d_hidden, w_up, w_out, middle, cotangent, queries, acts, w_down, normed, mixed, first, own_cols,
    keyval, keys_t, code_col, doc_row, lse, gain, b_down,
):
    seq, width = queries.shape
    heads = width // keys_t.shape[0]
    vmem = pl.BlockSpec(memory_space=pltpu.VMEM)
    dma = pltpu.SemaphoreType.DMA
    block = lambda dtype: pltpu.VMEM((BLOCK, width), dtype)
    return pl.pallas_call(
        functools.partial(mlp_attend_back_kernel, heads),
        out_shape=(
            jax.ShapeDtypeStruct((seq, width), F32),
            jax.ShapeDtypeStruct((seq, width), BF16),
            jax.ShapeDtypeStruct((FEED_EARLY * BLOCK, width), BF16),
            jax.ShapeDtypeStruct((2 * own_cols, width), F32),
            jax.ShapeDtypeStruct(keyval.shape, F32),
            jax.ShapeDtypeStruct((5, 8, width), F32),
        ),
        in_specs=[HBM] * 11 + [vmem] * 7,
        out_specs=(HBM, HBM, HBM, HBM, vmem, vmem),
        scratch_shapes=[
            pltpu.VMEM(w_up.shape, BF16),
            pltpu.VMEM(w_out.shape, BF16),
            pltpu.VMEM((BLOCK, d_hidden.shape[1]), BF16),
            block(F32),
            block(BF16),
            block(BF16),
            block(BF16),
            pltpu.VMEM((BLOCK, own_cols), BF16),
            block(BF16),
            block(BF16),
            block(BF16),
            pltpu.VMEM((2 * own_cols, width), F32),
            pltpu.VMEM((REACH * BLOCK, BLOCK), F32),
            dma((9,)),
            dma((4,)),
        ]
        + LineSum.scratch(seq - BLOCK, (seq + (FEED_EARLY - 1) * BLOCK) // PIECE, width),
        compiler_params=pltpu.CompilerParams(
            collective_id=1, has_side_effects=True, vmem_limit_bytes=VMEM_LIMIT
        ),
        cost_estimate=pl.CostEstimate(
            flops=200 * 10**9, bytes_accessed=2**25, transcendentals=0
        ),
        name="mlp_attend_back",
    )(
        d_hidden, w_up, w_out, middle, cotangent, queries, acts, w_down, normed, mixed, first,
        keyval, keys_t, code_col, doc_row, lse, gain.reshape(1, width), b_down.reshape(1, width),
    )


def feed_kernel(
    rounds,
    acts_hbm, w_down_hbm, mid_hbm, dq_hbm, w_q_hbm, in_hbm, d_mid_hbm, normed_hbm,
    dkv_f_ref, w_kv_ref, gain_ref, bias_ref, sums_in, b_up_in,
    out_hbm, in_grad_hbm, table_out, vectors_out,
    w_down, w_q, acts, mid, dq, xs, d_mid, spread, low, in_grad, normed, dkv_ref, sums, trade, trade_in, table, table_in, table_all,
    load_sem, out_sem, t_send, t_recv, h_send, h_recv, d_send, d_recv, *line_refs,
):
    line = LineSum(line_refs)
    rows, width = line.part.shape
    seq = rows + FEED_EARLY * BLOCK
    blocks = seq // BLOCK
    chunks = rows // BLOCK
    slots = BLOCK // (PIECE * SLOT)
    planes, _, cols_q = w_q.shape
    m = lax.axis_index("mp")
    d = lax.axis_index("dp")
    peers = [{"dp": flip_bit(d, 1 << r)} for r in range(rounds)]

    def load(i, src, dst):
        return pltpu.make_async_copy(src, dst, load_sem.at[i])

    def load_feed(c):
        at = rows_at((c + FEED_EARLY) * BLOCK, BLOCK)
        return [load(2, acts_hbm.at[at], acts), load(3, mid_hbm.at[at], mid)]

    def load_grad(c):
        at = rows_at(c * BLOCK, BLOCK)
        return [
            load(4, dq_hbm.at[at], dq),
            load(5, in_hbm.at[at], xs),
            load(6, d_mid_hbm.at[at], d_mid),
        ]

    def store(i, src, dst, c):
        return pltpu.make_async_copy(src, dst.at[rows_at(c * BLOCK, BLOCK)], out_sem.at[i])

    def load_normed(c):
        return load(7, normed_hbm.at[rows_at(c * BLOCK, BLOCK)], normed)

    load(0, w_down_hbm, w_down).start()
    for i in load_feed(0):
        i.start()
    load_normed(0).start()
    load(1, w_q_hbm, w_q).start()
    for i in load_grad(0):
        i.start()
    line.greet(peers)
    sums[...] = jnp.zeros_like(sums)
    dkv_ref[...] = dkv_f_ref[pl.ds(FRONT, seq), :].astype(BF16)
    hd = dkv_ref.shape[1] // 2

    def produce(c):
        at = rows_at(c * BLOCK, BLOCK)
        for i in load_feed(c):
            i.wait()

        def cols(n, carry):
            there = rows_at(n * COLS, COLS)
            line.part[at, there] = project(acts[...], w_down[:, there])
            return carry

        lax.fori_loop(0, width // COLS, cols, 0)

        @pl.when(m == 0)
        def _():
            line.part[at, :] += mid[...]

        if c + 1 < chunks:
            for i in load_feed(c + 1):
                i.start()

    def output_step(c):
        def strip(i, carry):
            at = rows_at(i * STRIP, STRIP)
            there = rows_at(c * BLOCK + i * STRIP, STRIP)
            low[at, :] = (line.total[there, :] + bias_ref[...]).astype(BF16)
            return carry

        lax.fori_loop(0, BLOCK // STRIP, strip, 0)

    def spread_step(c):
        here = rows_at(c * BLOCK, BLOCK)

        def cols(n, carry):
            there = rows_at(n * COLS, COLS)
            total = dot_t(dkv_ref[here, :], w_kv_ref[there, :])
            for i in range(planes):
                total = total + dot_t(dq[:, pl.ds(i * cols_q, cols_q)], w_q[i, there, :])
            spread[:, there] = total
            return carry

        lax.fori_loop(0, width // COLS, cols, 0)

    def norm_step(c):
        def strip(i, carry):
            at = rows_at(i * STRIP, STRIP)
            grad = spread[at, :]
            d_in, weighted = norm_back_rows(xs[at, :].astype(F32), grad, gain_ref[...])
            in_grad[at, :] = (d_mid[at, :] + d_in).astype(BF16)
            sums[0] += fold_rows(weighted)
            sums[1] += fold_rows(grad)
            return carry

        lax.fori_loop(0, BLOCK // STRIP, strip, 0)

    def swap(r):
        return pltpu.make_async_remote_copy(
            trade.at[r], trade_in.at[r], t_send.at[r], t_recv.at[r],
            device_id=peers[r], device_id_type=MESH,
        )

    def vectors_first():
        trade[0] = jnp.zeros_like(trade.at[0])
        for i in range(2):
            trade[0, i : i + 1] = jnp.sum(sums[i], axis=0, keepdims=True)
        for i in range(sums_in.shape[0]):
            trade[0, 2 + i : 3 + i] = jnp.sum(sums_in[i], axis=0, keepdims=True)
        at = 2 + sums_in.shape[0]
        trade[0, at : at + 1] = b_up_in[...]
        d_values = dkv_f_ref[pl.ds(FRONT, seq), pl.ds(hd, hd)]
        trade[0, at + 1 : at + 2, 0:hd] = jnp.sum(d_values, axis=0, keepdims=True)
        swap(0).start()

    def vectors_next(r):
        swap(r).wait()
        trade[r + 1] = trade[r] + trade_in[r]
        if r + 1 < rounds:
            swap(r + 1).start()
        else:
            vectors_out[...] = trade[r + 1]

    def table_block(c):
        load_normed(c).wait()

        def cols(n, carry):
            there = rows_at(n * COLS, COLS)
            part = dot_down(dkv_ref[pl.ds(c * BLOCK, BLOCK), :], normed[:, there])
            table[:, there] = part if c == 0 else table[:, there] + part
            return carry

        lax.fori_loop(0, width // COLS, cols, 0)
        if c + 1 < blocks:
            load_normed(c + 1).start()

    bits = [lax.rem(lax.div(d, 1 << r), 2) for r in range(rounds)]
    base = [0]
    size = [table.shape[0]]
    for r in range(rounds):
        size.append(size[r] // 2)
        base.append(base[r] + bits[r] * size[r + 1])

    def part_of(start, count):
        return pl.ds(pl.multiple_of(start, 8), count)

    def halve(r):
        away = part_of(base[r] + (1 - bits[r]) * size[r + 1], size[r + 1])
        into = pl.ds(size[0] - size[r], size[r + 1])
        return pltpu.make_async_remote_copy(
            table.at[away], table_in.at[into], h_send.at[r], h_recv.at[r],
            device_id=peers[r], device_id_type=MESH,
        )

    def double(r, mine):
        start = base[r] + (bits[r] if mine else 1 - bits[r]) * size[r + 1]
        at = part_of(start, size[r + 1])
        return pltpu.make_async_remote_copy(
            table_all.at[at], table_all.at[at], d_send.at[r], d_recv.at[r],
            device_id=peers[r], device_id_type=MESH,
        )

    store_table = pltpu.make_async_copy(table_all, table_out, out_sem.at[2])

    def table_step(i):
        if 1 <= i <= rounds:
            r = i - 1
            halve(r).wait()
            at = part_of(base[r + 1], size[r + 1])
            whole = table_all if i == rounds else table
            whole[at, :] = table[at, :] + table_in[pl.ds(size[0] - size[r], size[r + 1]), :]
        elif i > rounds:
            r = 2 * rounds - i
            double(r, True).wait_send()
            double(r, False).wait_recv()
        if i < rounds:
            halve(i).start()
        elif i < 2 * rounds:
            double(2 * rounds - 1 - i, True).start()
        else:
            store_table.start()

    load(0, w_down_hbm, w_down).wait()
    produce(0)
    line.meet(peers)
    for k in range(3):
        line.slot(k)
    load(1, w_q_hbm, w_q).wait()

    def spread_block(v):
        for i in load_grad(v):
            i.wait()
        spread_step(v)

    def norm_block(v):
        if v >= 1:
            store(1, in_grad, in_grad_hbm, v - 1).wait()
        norm_step(v)
        store(1, in_grad, in_grad_hbm, v).start()
        if v + 1 < blocks:
            for i in load_grad(v + 1):
                i.start()

    def output_block(c):
        if c >= 1:
            store(0, low, out_hbm, c - 1).wait()
        output_step(c)
        store(0, low, out_hbm, c).start()

    slot_count = (line.pieces + LATE) // SLOT
    steps = [[] for _ in range(max(slot_count, 4 * blocks + 8))]
    for c in range(1, chunks):
        steps[(c - 1) * slots + 3].append(functools.partial(produce, c))
    for c in range(chunks):
        steps[(c + 1) * slots - 1 + LATE // SLOT].append(functools.partial(output_block, c))
    for v in range(blocks):
        steps[3 + 2 * v].append(functools.partial(spread_block, v))
        steps[4 + 2 * v].append(functools.partial(norm_block, v))
        steps[2 + 2 * v].append(functools.partial(table_block, v))
    done = 4 + 2 * blocks
    for i in range(rounds + 1):
        steps[done + i].append(vectors_first if i == 0 else functools.partial(vectors_next, i - 1))
    first = 1 + 2 * blocks
    apart = max(1, min(2, (len(steps) - 1 - first) // (2 * rounds)))
    for i in range(2 * rounds + 1):
        steps[first + i * apart].append(functools.partial(table_step, i))
    for i, todo in enumerate(steps):
        if i >= 3 and i < slot_count:
            line.slot(i)
        for step in todo:
            step()
    store(0, low, out_hbm, chunks - 1).wait()
    store(1, in_grad, in_grad_hbm, blocks - 1).wait()
    store_table.wait()
    line.finish()


def feed_and_input_grad(
    acts, w_down, middle, b_down, d_queries, all_query, d_keyval_sum, w_keyval, inputs, d_middle, gain,
    normed, sums, b_up,
):
    seq, width = inputs.shape
    rounds = (lax.axis_size("dp") - 1).bit_length()
    vmem = pl.BlockSpec(memory_space=pltpu.VMEM)
    dma = pltpu.SemaphoreType.DMA
    block = lambda dtype: pltpu.VMEM((BLOCK, width), dtype)
    rest = seq - FEED_EARLY * BLOCK
    shape = jax.ShapeDtypeStruct
    table = (w_keyval.shape[1], width)
    return pl.pallas_call(
        functools.partial(feed_kernel, rounds),
        out_shape=(
            shape((rest, width), BF16),
            shape((seq, width), BF16),
            shape(table, F32),
            shape((16, width), F32),
        ),
        in_specs=[HBM] * 8 + [vmem] * 6,
        out_specs=(HBM, HBM, HBM, vmem),
        scratch_shapes=[
            pltpu.VMEM(w_down.shape, BF16),
            pltpu.VMEM(all_query.shape, BF16),
            pltpu.VMEM((BLOCK, acts.shape[1]), BF16),
            block(F32),
            block(BF16),
            block(BF16),
            block(F32),
            block(F32),
            block(BF16),
            block(BF16),
            block(BF16),
            pltpu.VMEM((seq, w_keyval.shape[1]), BF16),
            pltpu.VMEM((2, 8, width), F32),
            pltpu.VMEM((rounds + 1, 16, width), F32),
            pltpu.VMEM((rounds, 16, width), F32),
            pltpu.VMEM(table, F32),
            pltpu.VMEM(table, F32),
            pltpu.VMEM(table, F32),
            dma((8,)),
            dma((3,)),
            dma((rounds,)),
            dma((rounds,)),
            dma((rounds,)),
            dma((rounds,)),
            dma((rounds,)),
            dma((rounds,)),
        ]
        + LineSum.scratch(rest, rest // PIECE, width),
        compiler_params=pltpu.CompilerParams(
            collective_id=2, has_side_effects=True, vmem_limit_bytes=VMEM_LIMIT
        ),
        cost_estimate=pl.CostEstimate(
            flops=150 * 10**9, bytes_accessed=2**25, transcendentals=0
        ),
        name="feed_and_input_grad",
    )(
        acts, w_down, middle, d_queries, all_query, inputs, d_middle, normed,
        d_keyval_sum, w_keyval, gain.reshape(1, width), b_down.reshape(1, width), sums,
        b_up.reshape(1, width),
    )


def shards(
    inputs,
    doc_ids,
    pad_mask,
    attn_gain,
    attn_shift,
    w_query,
    b_query,
    w_keyval,
    b_value,
    w_out,
    b_out,
    mlp_gain,
    mlp_shift,
    w_up,
    b_up,
    w_down,
    b_down,
    cotangent,
):
    seq = doc_ids.shape[1]
    hd = b_value.shape[0]
    width = inputs.shape[1]
    own_cols = w_query.shape[1]
    own = lax.axis_index("mp") * own_cols
    docs = doc_ids[0]
    codes = jnp.where(pad_mask[0] == 1, docs, -1)
    code_col = jnp.pad(codes, (FRONT, 0), constant_values=-2).reshape(-1, 1)
    doc_row = docs.reshape(1, seq)

    all_query, all_out, normed_attn, queries, mixed, d_acts, keyval, keys_t, lse = attention_front(
        inputs, w_query, b_query, w_keyval, b_value, w_out, attn_gain, attn_shift, code_col, doc_row,
        cotangent, w_down,
    )
    middle, acts, d_hidden, grad_w_down, grad_w_up, first, grad_b_up = mlp(
        mixed, all_out, inputs, w_up, d_acts, cotangent, b_out, mlp_gain, mlp_shift, b_up
    )
    grad_b_up = jnp.sum(grad_b_up, axis=0)
    grad_w_up = lax.psum_scatter(grad_w_up, "dp", scatter_dimension=0, tiled=True)
    grad_w_down = lax.psum_scatter(grad_w_down, "dp", scatter_dimension=1, tiled=True)

    d_middle, d_queries, out_first, grads, d_keyval_sum, sums = mlp_attend_back(
        d_hidden, w_up, all_out, middle, cotangent, queries, acts, w_down, normed_attn, mixed, first, own_cols,
        keyval, keys_t, code_col, doc_row, lse, mlp_gain, b_down,
    )
    grads, grad_w_down, grad_w_up = lax.optimization_barrier((grads, grad_w_down, grad_w_up))
    grads = lax.psum_scatter(grads, "dp", scatter_dimension=1, tiled=True)
    out_rest, input_grad, grad_w_keyval, totals = feed_and_input_grad(
        acts, w_down, middle, b_down, d_queries, all_query, d_keyval_sum, w_keyval, inputs, d_middle,
        attn_gain, normed_attn, sums, grad_b_up,
    )
    outputs = jnp.concatenate([out_first, out_rest], 0)
    grad_w_query, grad_w_out = grads[:own_cols].T, grads[own_cols:]
    grad_w_keyval = grad_w_keyval.T
    grad_attn_gain, grad_attn_shift, grad_mlp_gain, grad_mlp_shift = (totals[i] for i in range(4))
    grad_b_out, grad_b_down, grad_b_query, grad_b_up = (totals[i] for i in range(4, 8))
    grad_b_query = lax.dynamic_slice_in_dim(grad_b_query, own, own_cols, 0)
    grad_b_value = totals[8, :hd]
    return (
        outputs,
        input_grad,
        grad_attn_gain,
        grad_attn_shift,
        grad_w_query,
        grad_b_query,
        grad_w_keyval,
        grad_b_value,
        grad_w_out,
        grad_b_out,
        grad_mlp_gain,
        grad_mlp_shift,
        grad_w_up,
        grad_b_up,
        grad_w_down,
        grad_b_down,
    )


def solution(mesh):
    return jax.shard_map(
        shards,
        mesh=mesh,
        in_specs=(
            P("dp", None),
            P("dp", None),
            P("dp", None),
            P(),
            P(),
            P(None, "mp"),
            P("mp"),
            P(),
            P(),
            P("mp", None),
            P(),
            P(),
            P(),
            P(None, "mp"),
            P("mp"),
            P("mp", None),
            P(),
            P("dp", None),
        ),
        out_specs=(
            P("dp", None),
            P("dp", None),
            P(),
            P(),
            P("dp", "mp"),
            P("mp"),
            P(),
            P(),
            P("mp", "dp"),
            P(),
            P(),
            P(),
            P("dp", "mp"),
            P("mp"),
            P("mp", "dp"),
            P(),
        ),
        check_vma=False,
    )
```

```python
import functools
import math

import jax
import jax.numpy as jnp
from jax import lax
from jax.experimental import pallas as pl
from jax.experimental.pallas import tpu as pltpu
from jax.sharding import PartitionSpec as P

EPS = 1e-05
MESH = pl.DeviceIdType.MESH
F32 = jnp.float32
BF16 = jnp.bfloat16
VMEM_LIMIT = 60 * 2**20
HBM = pl.BlockSpec(memory_space=pl.ANY)


def norm_rows(rows_in, gain, shift):
    center = rows_in - jnp.mean(rows_in, axis=-1, keepdims=True)
    spread = jnp.mean(center * center, axis=-1, keepdims=True)
    return center * lax.rsqrt(spread + EPS) * gain + shift


def project(left, right):
    return jnp.dot(left, right, preferred_element_type=F32)


STRIP = 16
COLS = 512
BLOCK = 256
REACH = 3
GROUP = 4
NEG = -1e30
FRONT = (REACH - 1) * BLOCK


def key_window(c):
    first = max(0, c - REACH + 1) * BLOCK
    return first, (c + 1) * BLOCK - first


def mask_bias(code_col, doc_row, first_key, keys, first_query, queries):
    j = first_key + lax.broadcasted_iota(jnp.int32, (keys, queries), 0)
    i = first_query + lax.broadcasted_iota(jnp.int32, (keys, queries), 1)
    ok = ((j < i) & (code_col == doc_row)) | (j == i)
    return jnp.where(ok, 0.0, NEG)


def dot_t(a, b):
    return lax.dot_general(a, b, (((1,), (1,)), ((), ())), preferred_element_type=F32)


def rows_at(start, count):
    return pl.ds(pl.multiple_of(start, count), count)


def mp_partner(m, r):
    if r == 1:
        return m + 1 - 2 * lax.rem(m, 2)
    if r == 2:
        return m + 2 - 4 * lax.div(m, 2)
    return 3 - m


def flip_bit(d, bit):
    on = lax.rem(lax.div(d, bit), 2)
    return d + bit * (1 - 2 * on)


def front_kernel(
    heads,
    wq, wo, in_hbm, cot_hbm, w_down_hbm, bq, w_kv, gain_ref, shift_ref, bv_ref, code_ref, doc_ref,
    wq_out, wo_out, normed_hbm, q_hbm, mixed_hbm, d_acts_hbm, kv_ref, kt_ref, lse_ref,
    own_q, own_o, gq, go, sq, so, normed, q_ring, mixed_ring, vt, bias_ref, bq_all, cot, down, d_acts,
    load_sem, cot_sem, down_sem, d_acts_sem, ship_sem, o_sem, ring_sem, z_send, z_recv, b_send, b_recv, n_send, n_recv,
):
    m = lax.axis_index("mp")
    d = lax.axis_index("dp")
    dc, dx, dy = flip_bit(d, 1), flip_bit(d, 2), flip_bit(d, 4)
    dxy = flip_bit(dx, 4)
    is_mid = (m == 1) | (m == 2)
    buddy, across = {"mp": mp_partner(m, 1)}, {"mp": 3 - m}
    upper = lax.div(m, 2)
    inner = lax.rem(m + upper, 2)

    def plane_at(s):
        q = (1 - inner, 2, 3)[s]
        return q + upper * (3 - 2 * q)

    g = (gq, go)
    half = (gq.shape[2] // 2, go.shape[2] // 2)
    seq, width = normed.shape
    cols_q = q_ring.shape[2]
    hd = vt.shape[0]
    blocks = seq // BLOCK
    scale = 1.0 / math.sqrt(hd)
    planes = 4

    loads = [
        pltpu.make_async_copy(wq.at[d], own_q, load_sem.at[0]),
        pltpu.make_async_copy(wo.at[d], own_o, load_sem.at[1]),
        pltpu.make_async_copy(in_hbm, normed, load_sem.at[2]),
        pltpu.make_async_copy(wq, sq.at[m], load_sem.at[3]),
        pltpu.make_async_copy(wq, wq_out.at[m], load_sem.at[4]),
        pltpu.make_async_copy(wo, wo_out.at[m], load_sem.at[5]),
    ]
    for c in loads:
        c.start()
    bar = pltpu.get_barrier_semaphore()
    for r in (1, 2, 3):
        pl.semaphore_signal(bar, inc=1, device_id={"mp": mp_partner(m, r)}, device_id_type=MESH)
    for n in (dc, dx, dy):
        pl.semaphore_signal(bar, inc=1, device_id={"dp": n}, device_id_type=MESH)
    loads[0].wait()
    gq[m, d] = own_q[...].astype(F32)
    loads[1].wait()
    go[m, d] = own_o[...].astype(F32)
    bq_all[m] = bq[...]
    pl.semaphore_wait(bar, 6)

    def z_copy(w, plane, to, i):
        ref = g[w].at[plane, d]
        return pltpu.make_async_remote_copy(
            ref, ref, z_send.at[w, i], z_recv.at[w, plane], device_id=to, device_id_type=MESH
        )

    def z_own(w, wait=False):
        def go_or_wait(c):
            if wait:
                c.wait_send()
            else:
                c.start()

        go_or_wait(z_copy(w, m, buddy, 0))

        @pl.when(is_mid)
        def _():
            go_or_wait(z_copy(w, m, across, 1))

    def z_forward(w, s, wait=False):
        @pl.when(is_mid)
        def _():
            c = z_copy(w, plane_at(s), across if s == 0 else buddy, 2 + s)
            if wait:
                c.wait_send()
            else:
                c.start()

    def z_land(w, s):
        z_copy(w, plane_at(s), buddy, 0).wait_recv()

    def bias_copy(r, plane):
        return pltpu.make_async_remote_copy(
            bq_all.at[plane], bq_all.at[plane], b_send.at[r - 1], b_recv.at[r - 1],
            device_id={"mp": mp_partner(m, r)}, device_id_type=MESH,
        )

    sent_eighth = (d, d, d, dx, dy, dx, dy, dxy)
    landed_eighth = (dx, dy, dc, flip_bit(dx, 1), flip_bit(dy, 1), dxy, dxy, flip_bit(dxy, 1))
    sent_to = (dx, dy, dc, dc, dc, dy, dx, dc)

    def near(kind, w, r, eighths):
        q = plane_at(r)
        ref = g[w].at[q, eighths[kind]]
        if kind == 5:
            ref = g[w].at[q, eighths[kind], pl.ds(0, half[w])]
        if kind == 6:
            ref = g[w].at[q, eighths[kind], pl.ds(half[w], half[w])]
        return pltpu.make_async_remote_copy(
            ref, ref, n_send.at[kind, w, r], n_recv.at[kind, w, r],
            device_id={"dp": sent_to[kind]}, device_id_type=MESH,
        )

    def go_near(kind, w, r):
        near(kind, w, r, sent_eighth).start()

    def landed(kind, w, r):
        near(kind, w, r, landed_eighth).wait_recv()

    shipped = []
    ring = so.shape[0]

    def ship(w, r, eighth):
        q = plane_at(r)
        n = sum(1 for v, _ in shipped if v == w)
        if w == 0:
            sq[q, eighth] = gq[q, eighth].astype(BF16)
            c = pltpu.make_async_copy(sq.at[q, eighth], wq_out.at[q, eighth], ship_sem.at[n])
        else:
            slot = n % ring
            if n >= ring:
                [c for v, c in shipped if v == 1][n - ring].wait()
            so[slot] = go[q, eighth].astype(BF16)
            c = pltpu.make_async_copy(so.at[slot], wo_out.at[q, eighth], o_sem.at[slot])
        c.start()
        shipped.append((w, c))

    def store_q(q, c, slot):
        at = pl.ds(c * BLOCK, BLOCK)
        return pltpu.make_async_copy(
            q_ring.at[slot], q_hbm.at[at, rows_at(q * cols_q, cols_q)], ring_sem.at[0, slot]
        )

    def store_mixed(q, c, slot):
        at = pl.ds(c * BLOCK, BLOCK)
        return pltpu.make_async_copy(
            mixed_ring.at[slot], mixed_hbm.at[at, rows_at(q * cols_q, cols_q)], ring_sem.at[1, slot]
        )

    def set_bias(c):
        first, count = key_window(c)
        bias_ref[pl.ds(0, count), :] = mask_bias(
            code_ref[pl.ds(FRONT + first, count), :], doc_ref[:, pl.ds(c * BLOCK, BLOCK)],
            first, count, c * BLOCK, BLOCK,
        )

    def attend_block(q, c, n):
        slot = lax.rem(n, 2) if not isinstance(n, int) else n % 2
        first, count = key_window(c)
        keys, at = pl.ds(FRONT + first, count), pl.ds(c * BLOCK, BLOCK)

        def free():
            store_q(q, c, slot).wait()
            store_mixed(q, c, slot).wait()

        if not isinstance(n, int) or n >= 2:
            free()
        w = sq[q].reshape(width, cols_q)
        q_ring[slot] = (project(normed[at, :], w) + bq_all[q]).astype(BF16)
        store_q(q, c, slot).start()
        for u in range(cols_q // hd):
            head = pl.ds(u * hd, hd)
            s = dot_t(kv_ref[keys, pl.ds(0, hd)], q_ring[slot, :, head]) * scale
            s = s + bias_ref[pl.ds(0, count), :]
            top = jnp.max(s, axis=0, keepdims=True)
            e = jnp.exp(s - top)
            total = jnp.sum(e, axis=0, keepdims=True)
            probs = (e * (1.0 / total)).astype(BF16)
            mixed_ring[slot, :, head] = project(vt[:, pl.ds(first, count)], probs).T.astype(BF16)
            lse_ref[pl.ds(q * (cols_q // hd) + u, 1), at] = top + jnp.log(total)
        store_mixed(q, c, slot).start()

    bands = w_down_hbm.shape[0] // down.shape[1]

    def load_cot(i):
        at = rows_at(lax.rem(i, blocks) * BLOCK, BLOCK)
        slot = lax.rem(i, 2)
        return pltpu.make_async_copy(cot_hbm.at[at], cot.at[slot], cot_sem.at[slot])

    def load_down(n):
        at = pl.ds(n * down.shape[1], down.shape[1])
        return pltpu.make_async_copy(w_down_hbm.at[at], down.at[n % 2], down_sem.at[n % 2])

    def store_d_acts(n, i):
        slot = lax.rem(i, 2)
        rows = rows_at(lax.rem(i, blocks) * BLOCK, BLOCK)
        cols = pl.ds(n * down.shape[1], down.shape[1])
        return pltpu.make_async_copy(
            d_acts.at[slot], d_acts_hbm.at[rows, cols], d_acts_sem.at[slot]
        )

    def d_acts_band(n):
        load_down(n).wait()
        if n + 1 < bands:
            load_down(n + 1).start()

        def one(i, carry):
            slot = lax.rem(i, 2)
            load_cot(i).wait()

            @pl.when(i + 1 < bands * blocks)
            def _():
                load_cot(i + 1).start()

            @pl.when(i >= 2)
            def _():
                store_d_acts(n, i).wait()

            d_acts[slot] = dot_t(cot[slot], down[n % 2])
            store_d_acts(n, i).start()
            return carry

        lax.fori_loop(n * blocks, (n + 1) * blocks, one, 0)

    def own_plane(c):
        set_bias(c)
        attend_block(m, c, c)

    def other_planes(c, first, end):
        if first == 1:
            set_bias(c)

        def one(r, carry):
            attend_block(lax.rem(m + r, planes), c, blocks + c * (planes - 1) + r - 1)
            return carry

        lax.fori_loop(first, end, one, 0)

    stream = [(w, r) for w in (0, 1) for r in range(3)]

    def pass_on(i):
        w, s = stream[i]

        @pl.when(is_mid)
        def _():
            z_land(w, s)
            z_forward(w, s)

        if i == 2:
            z_own(1)

    def from_line(i):
        w, s = stream[i]

        @pl.when(jnp.logical_not(is_mid))
        def _():
            z_land(w, s)

        for kind in (0, 1, 2):
            go_near(kind, w, s)
        ship(w, s, d)

    def from_near(i):
        w, s = stream[i]
        landed(0, w, s)
        go_near(5, w, s)
        go_near(3, w, s)
        ship(w, s, dx)
        landed(1, w, s)
        go_near(6, w, s)
        go_near(4, w, s)
        ship(w, s, dy)
        landed(2, w, s)
        ship(w, s, dc)

    def from_far(i):
        w, s = stream[i]
        landed(5, w, s)
        landed(6, w, s)
        go_near(7, w, s)
        ship(w, s, dxy)
        for kind in (3, 4):
            landed(kind, w, s)
            ship(w, s, landed_eighth[kind])
        landed(7, w, s)
        ship(w, s, landed_eighth[7])

    z_own(0)
    for r in (1, 2, 3):
        bias_copy(r, m).start()

    load_down(0).start()
    load_cot(0).start()
    loads[2].wait()

    def norm_strip(i, carry):
        at = rows_at(i * STRIP, STRIP)
        normed[at, :] = norm_rows(normed[at, :].astype(F32), gain_ref[...], shift_ref[...]).astype(BF16)
        return carry

    lax.fori_loop(0, seq // STRIP, norm_strip, 0)
    keep_normed = pltpu.make_async_copy(normed, normed_hbm, load_sem.at[2])
    keep_normed.start()
    kv_ref[pl.ds(0, FRONT), :] = jnp.zeros((FRONT, 2 * hd), BF16)
    kt_ref[:, pl.ds(0, FRONT)] = jnp.zeros((hd, FRONT), BF16)
    for c in range(blocks):
        at, put = pl.ds(c * BLOCK, BLOCK), pl.ds(FRONT + c * BLOCK, BLOCK)
        kv = project(normed[at, :], w_kv[...])
        keys, values = kv[:, :hd], kv[:, hd:] + bv_ref[...]
        kv_ref[put, pl.ds(0, hd)] = keys.astype(BF16)
        kv_ref[put, pl.ds(hd, hd)] = values.astype(BF16)
        kt_ref[:, put] = keys.T.astype(BF16)
        vt[:, at] = values.T.astype(BF16)
    loads[3].wait()

    def stage(s):
        if s == 0:
            pass_on(0)
        if s + 1 < len(stream):
            pass_on(s + 1)
        if s < len(stream):
            from_line(s)
        if 1 <= s <= len(stream):
            from_near(s - 1)
        if s >= 2:
            from_far(s - 2)

    stage(0)
    own_plane(0)
    own_plane(1)
    stage(1)
    own_plane(2)
    own_plane(3)
    stage(2)
    for n in range(bands // 2):
        d_acts_band(n)
    stage(3)
    for n in range(bands // 2, bands):
        d_acts_band(n)
    for r in (1, 2, 3):
        bias_copy(r, mp_partner(m, r)).wait_recv()
    stage(4)
    other_planes(0, 1, planes)
    other_planes(1, 1, planes)
    from_line(5)
    other_planes(2, 1, 2)
    from_near(4)
    other_planes(2, 2, planes)
    from_far(3)
    other_planes(3, 1, 2)
    from_near(5)
    other_planes(3, 2, planes)
    from_far(4)
    from_far(5)

    for i in (0, 1):
        store_d_acts(0, i).wait()
    for slot in (0, 1):
        store_q(m, 0, slot).wait()
        store_mixed(m, 0, slot).wait()
    for w in (0, 1):
        z_own(w, wait=True)
    for w, r in stream:
        z_forward(w, r, wait=True)
        for kind in range(8):
            near(kind, w, r, sent_eighth).wait_send()
    for r in (1, 2, 3):
        bias_copy(r, m).wait_send()
    rows_o = [c for v, c in shipped if v == 1]
    for c in [c for v, c in shipped if v == 0] + rows_o[-ring:]:
        c.wait()
    keep_normed.wait()
    loads[4].wait()
    loads[5].wait()


def gather_by_sum(shard):
    blank = jnp.zeros((lax.axis_size("mp"),) + shard.shape, F32)
    half = shard.astype(F32) * 0.5
    own = lax.dynamic_update_index_in_dim(blank, half, lax.axis_index("mp"), 0)
    return lax.psum(own, "mp") * 2.0


def attention_front(
    inputs, w_query, b_query, w_keyval, b_value, w_out, gain, shift, code_col, doc_row, cotangent, w_down
):
    dp, mp = lax.axis_size("dp"), lax.axis_size("mp")
    width, cols = w_query.shape
    rows = w_out.shape[0]
    seq = inputs.shape[0]
    hd = w_keyval.shape[1] // 2
    if (dp, mp) != (8, 4):
        all_query, all_out, all_bias = (
            gather_by_sum(a).astype(a.dtype) for a in (w_query, w_out, b_query)
        )
        normed = norm_rows(inputs.astype(F32), gain, shift).astype(BF16)
        kv_bias = jnp.concatenate([jnp.zeros((hd,), F32), b_value])
        keyval = (project(normed, w_keyval) + kv_bias).astype(BF16)
        queries = jnp.concatenate(
            [project(normed, all_query[i]) + all_bias[i] for i in range(mp)], 1
        ).astype(BF16)
        mixed, lse = attend(queries, keyval, code_col[FRONT:], doc_row)
        keyval = jnp.pad(keyval, ((FRONT, 0), (0, 0)))
        keys_t = keyval[:, :hd].T
        d_acts = jnp.einsum("td,fd->tf", cotangent, w_down, preferred_element_type=F32)
        return all_query, all_out.reshape(-1, width), normed, queries, mixed, d_acts, keyval, keys_t, lse
    wq = w_query.reshape(dp, width // dp, cols)
    wo = w_out.reshape(dp, rows // dp, width)
    dma = pltpu.SemaphoreType.DMA
    vmem = pl.BlockSpec(memory_space=pltpu.VMEM)
    full_q, full_o = (mp,) + wq.shape, (mp,) + wo.shape
    heads = mp * cols // hd
    shape = jax.ShapeDtypeStruct
    out_q, out_o, normed, queries, mixed, d_acts, keyval, keys_t, lse = pl.pallas_call(
        functools.partial(front_kernel, heads),
        out_shape=(
            shape(full_q, BF16),
            shape(full_o, BF16),
            shape((seq, width), BF16),
            shape((seq, mp * cols), BF16),
            shape((seq, mp * cols), BF16),
            shape((seq, w_down.shape[0]), F32),
            shape((FRONT + seq, 2 * hd), BF16),
            shape((hd, FRONT + seq), BF16),
            shape((heads, seq), F32),
        ),
        in_specs=[HBM] * 5 + [vmem] * 7,
        out_specs=(HBM,) * 6 + (vmem,) * 3,
        scratch_shapes=[
            pltpu.VMEM(wq.shape[1:], BF16),
            pltpu.VMEM(wo.shape[1:], BF16),
            pltpu.VMEM(full_q, F32),
            pltpu.VMEM(full_o, F32),
            pltpu.VMEM(full_q, BF16),
            pltpu.VMEM((4,) + wo.shape[1:], BF16),
            pltpu.VMEM((seq, width), BF16),
            pltpu.VMEM((2, BLOCK, cols), BF16),
            pltpu.VMEM((2, BLOCK, cols), BF16),
            pltpu.VMEM((hd, seq), BF16),
            pltpu.VMEM((REACH * BLOCK, BLOCK), F32),
            pltpu.VMEM((mp, 1, cols), F32),
            pltpu.VMEM((2, BLOCK, width), BF16),
            pltpu.VMEM((2, COLS, width), BF16),
            pltpu.VMEM((2, BLOCK, COLS), F32),
            dma((6,)),
            dma((2,)),
            dma((2,)),
            dma((2,)),
            dma((3 * dp,)),
            dma((4,)),
            dma((2, 2)),
            dma((2, 5)),
            dma((2, mp)),
            dma((3,)),
            dma((3,)),
            dma((8, 2, 3)),
            dma((8, 2, 3)),
        ],
        compiler_params=pltpu.CompilerParams(
            collective_id=0, has_side_effects=True, vmem_limit_bytes=VMEM_LIMIT
        ),
        name="attention_front",
    )(
        wq, wo, inputs, cotangent, w_down, b_query.reshape(1, cols), w_keyval, gain.reshape(1, width),
        shift.reshape(1, width), b_value.reshape(1, hd), code_col, doc_row,
    )
    return (
        out_q.reshape(mp, width, cols), out_o.reshape(mp * rows, width),
        normed, queries, mixed, d_acts, keyval, keys_t, lse,
    )


PIECE = 32
SLOT = 1
CROSS_LATE = 2 * SLOT
LATE = 5 * SLOT
AHEAD = 3 * SLOT


class LineSum:
    scratch = staticmethod(
        lambda rows, pieces, width: [pltpu.VMEM((rows, width), F32)] * 3
        + [pltpu.SemaphoreType.DMA((pieces,))] * 5
    )

    def __init__(self, refs):
        self.part, self.total, self.cross, *sems = refs
        self.in_send, self.in_recv, self.over_send, self.over_recv, self.out_send = sems
        self.slots = self.part.shape[0] // PIECE
        self.pieces = self.in_send.shape[0]
        m = lax.axis_index("mp")
        self.is_end = (m == 0) | (m == 3)
        self.is_mid = (m == 1) | (m == 2)
        self.buddy = {"mp": mp_partner(m, 1)}
        self.across = {"mp": 3 - m}

    def greet(self, others=()):
        bar = pltpu.get_barrier_semaphore()
        pl.semaphore_signal(bar, inc=1, device_id=self.buddy, device_id_type=MESH)
        for other in others:
            pl.semaphore_signal(bar, inc=1, device_id=other, device_id_type=MESH)

        @pl.when(self.is_mid)
        def _():
            pl.semaphore_signal(bar, inc=1, device_id=self.across, device_id_type=MESH)

    def meet(self, others=()):
        bar = pltpu.get_barrier_semaphore()

        @pl.when(self.is_end)
        def _():
            pl.semaphore_wait(bar, 1 + len(others))

        @pl.when(self.is_mid)
        def _():
            pl.semaphore_wait(bar, 2 + len(others))

    def at(self, k):
        slot = k if self.slots == self.pieces else k % self.slots
        return rows_at(slot * PIECE, PIECE)

    def inward(self, k):
        at = self.at(k)
        return pltpu.make_async_remote_copy(
            self.part.at[at], self.total.at[at], self.in_send.at[k], self.in_recv.at[k],
            device_id=self.buddy, device_id_type=MESH,
        )

    def over(self, k):
        at = self.at(k)
        return pltpu.make_async_remote_copy(
            self.part.at[at], self.cross.at[at], self.over_send.at[k], self.over_recv.at[k],
            device_id=self.across, device_id_type=MESH,
        )

    def outward(self, k):
        at = self.at(k)
        return pltpu.make_async_remote_copy(
            self.total.at[at], self.total.at[at], self.out_send.at[k], self.in_recv.at[k],
            device_id=self.buddy, device_id_type=MESH,
        )

    def slot(self, i):
        for j in range(SLOT):
            self.tick(i * SLOT + j)

    def tick(self, k):
        n = self.pieces

        @pl.when(self.is_end)
        def _():
            @pl.when(k < n)
            def _():
                @pl.when(k >= AHEAD)
                def _():
                    self.inward(k - AHEAD).wait_send()

                self.inward(k).start()

            @pl.when((k >= LATE) & (k < n + LATE))
            def _():
                self.outward(k - LATE).wait_recv()

        @pl.when(self.is_mid)
        def _():
            @pl.when(k < n)
            def _():
                at = self.at(k)
                self.inward(k).wait_recv()
                self.part[at, :] += self.total[at, :]
                self.over(k).start()

            @pl.when((k >= CROSS_LATE) & (k < n + CROSS_LATE))
            def _():
                j = k - CROSS_LATE
                at = self.at(j)
                self.over(j).wait_recv()
                self.total[at, :] = self.part[at, :] + self.cross[at, :]
                self.outward(j).start()

    def free(self, first, count):
        @pl.when(self.is_mid)
        def _():
            def sent(k, c):
                self.over(k).wait_send()
                self.outward(k).wait_send()
                return c

            lax.fori_loop(first, first + count, sent, 0)

    def finish(self, freed=0):
        n = self.pieces

        @pl.when(self.is_end)
        def _():
            for k in range(n - AHEAD, n):
                self.inward(k).wait_send()

        self.free(freed, n - freed)


def attend_kernel(seq, heads, q_ref, kv_ref, vt_ref, code_ref, doc_ref, mixed_ref, lse_ref, bias_ref):
    hd = vt_ref.shape[0]
    scale = 1.0 / math.sqrt(hd)
    for c in range(seq // BLOCK):

        @pl.when(pl.program_id(0) == c)
        def _(c=c):
            first, count = key_window(c)
            keys = pl.ds(first, count)
            bias_ref[pl.ds(0, count), :] = mask_bias(
                code_ref[keys, :], doc_ref[...], first, count, c * BLOCK, BLOCK
            )

            def some_heads(g, carry):
                for u in range(GROUP):
                    h = g * GROUP + u
                    cols = pl.ds(pl.multiple_of(h * hd, hd), hd)
                    s = dot_t(kv_ref[keys, pl.ds(0, hd)], q_ref[:, cols]) * scale
                    s = s + bias_ref[pl.ds(0, count), :]
                    top = jnp.max(s, axis=0, keepdims=True)
                    e = jnp.exp(s - top)
                    total = jnp.sum(e, axis=0, keepdims=True)
                    probs = (e * (1.0 / total)).astype(BF16)
                    mixed = project(vt_ref[:, keys], probs)
                    mixed_ref[:, cols] = mixed.T.astype(BF16)
                    lse_ref[pl.ds(h, 1), :] = top + jnp.log(total)
                return carry

            lax.fori_loop(0, heads // GROUP, some_heads, 0)


def attend(queries, keyval, code_col, doc_row):
    seq, width = queries.shape
    hd = keyval.shape[1] // 2
    heads = width // hd
    values_t = keyval[:, hd:].T
    whole = lambda *shape: pl.BlockSpec(shape, lambda c: (0,) * len(shape))
    return pl.pallas_call(
        functools.partial(attend_kernel, seq, heads),
        grid=(seq // BLOCK,),
        out_shape=(
            jax.ShapeDtypeStruct((seq, width), BF16),
            jax.ShapeDtypeStruct((heads, seq), F32),
        ),
        in_specs=[
            pl.BlockSpec((BLOCK, width), lambda c: (c, 0)),
            whole(seq, 2 * hd),
            whole(hd, seq),
            whole(seq, 1),
            pl.BlockSpec((1, BLOCK), lambda c: (0, c)),
        ],
        out_specs=(
            pl.BlockSpec((BLOCK, width), lambda c: (c, 0)),
            pl.BlockSpec((heads, BLOCK), lambda c: (0, c)),
        ),
        scratch_shapes=[pltpu.VMEM((REACH * BLOCK, BLOCK), F32)],
        compiler_params=pltpu.CompilerParams(vmem_limit_bytes=VMEM_LIMIT),
        name="attend",
    )(queries, keyval, values_t, code_col, doc_row)


def norm_back_rows(x, grad, gain):
    mean = jnp.mean(x, axis=-1, keepdims=True)
    center = x - mean
    scale = lax.rsqrt(jnp.mean(center * center, axis=-1, keepdims=True) + EPS)
    xhat = center * scale
    e = grad * gain
    weighted = grad * xhat
    d_in = scale * (
        e - jnp.mean(e, axis=-1, keepdims=True) - xhat * jnp.mean(e * xhat, axis=-1, keepdims=True)
    )
    return d_in, weighted


def dot_down(a, b):
    return lax.dot_general(a, b, (((0,), (0,)), ((), ())), preferred_element_type=F32)


def fold_rows(x):
    return jnp.sum(x.reshape(-1, 8, x.shape[-1]), axis=0)


FEED_EARLY = 2

GELU_A = math.sqrt(2.0 / math.pi)
GELU_B = 0.044715


def gelu_pair(u):
    square = u * u
    t = jnp.tanh(u * (GELU_A + GELU_A * GELU_B * square))
    cdf = 0.5 * (1.0 + t)
    slope = cdf + 0.5 * u * (1.0 - t * t) * (GELU_A + 3.0 * GELU_A * GELU_B * square)
    return u * cdf, slope


def mlp_kernel(
    mixed_hbm, w_out_hbm, in_hbm, w_up_hbm, d_acts_hbm, cot_hbm,
    b_out_ref, gain_ref, shift_ref, b_up_ref,
    mid_hbm, acts_hbm, dh_hbm, down_hbm, up_hbm, first_hbm, next_hbm, b_up_sum,
    w_out, w_up, normed, acts, dh, cot, mixed, xs, mid, d_acts, turned, tiles,
    load_sem, out_sem, tile_sem, *line_refs,
):
    line = LineSum(line_refs)
    seq, width = normed.shape
    blocks = seq // BLOCK
    hidden = w_up.shape[1]

    def load(i, src, dst):
        return pltpu.make_async_copy(src, dst, load_sem.at[i])

    def load_block(c):
        at = pl.ds(c * BLOCK, BLOCK)
        return [
            load(2, mixed_hbm.at[at], mixed),
            load(3, in_hbm.at[at], xs),
        ]

    def load_d_acts(c):
        return load(4, d_acts_hbm.at[pl.ds(c * BLOCK, BLOCK)], d_acts)

    def store_mid(c):
        return pltpu.make_async_copy(mid, mid_hbm.at[pl.ds(c * BLOCK, BLOCK)], out_sem.at[0])

    store_acts = pltpu.make_async_copy(acts, acts_hbm, out_sem.at[1])
    store_dh = pltpu.make_async_copy(dh, dh_hbm, out_sem.at[2])

    load(0, w_out_hbm, w_out).start()
    for i in load_block(0):
        i.start()
    load(1, w_up_hbm, w_up).start()
    load_d_acts(0).start()
    load(5, cot_hbm, cot).start()
    line.greet()
    b_up_sum[...] = jnp.zeros_like(b_up_sum)

    def middle_step(c):
        for i in load_block(c):
            i.wait()
        if c >= 1:
            store_mid(c - 1).wait()

        def cols(n, carry):
            there = rows_at(n * COLS, COLS)
            mid[:, there] = (
                project(mixed[...], w_out[:, there]) + xs[:, there].astype(F32) + b_out_ref[:, there]
            )
            return carry

        lax.fori_loop(0, width // COLS, cols, 0)
        store_mid(c).start()
        if c + 1 < blocks:
            for i in load_block(c + 1):
                i.start()

    def norm_step(c):
        def strip(i, carry):
            at = rows_at(i * STRIP, STRIP)
            put = rows_at(c * BLOCK + i * STRIP, STRIP)
            normed[put, :] = norm_rows(mid[at, :], gain_ref[...], shift_ref[...]).astype(BF16)
            return carry

        lax.fori_loop(0, BLOCK // STRIP, strip, 0)

    def hidden_step(c):
        at = pl.ds(c * BLOCK, BLOCK)
        load_d_acts(c).wait()

        def cols(n, carry):
            there = rows_at(n * COLS, COLS)
            u = project(normed[at, :], w_up[:, there]) + b_up_ref[:, there]
            value, slope = gelu_pair(u)
            acts[at, there] = value.astype(BF16)
            low = (d_acts[:, there] * slope).astype(BF16)
            dh[at, there] = low
            b_up_sum[:, there] += fold_rows(low.astype(F32))
            return carry

        lax.fori_loop(0, hidden // COLS, cols, 0)
        if c + 1 < blocks:
            load_d_acts(c + 1).start()
        else:
            store_acts.start()
            store_dh.start()

    def produce(c, part):
        def cols(n, carry):
            there = rows_at(n * COLS, COLS)
            part[:, there] = dot_t(dh[pl.ds(c * BLOCK, BLOCK), :], w_up[there, :])
            return carry

        lax.fori_loop(0, width // COLS, cols, 0)

    store_next = pltpu.make_async_copy(mid, next_hbm, out_sem.at[0])

    def produce_next():
        store_mid(blocks - 1).wait()
        produce(1, mid)
        store_next.start()

    tile_rows, tile_cols = tiles.shape[1:]
    tile_list = []
    for left, right, out in ((acts, cot, down_hbm), (normed, dh, up_hbm)):
        for row in range(0, left.shape[1], tile_rows):
            for col in range(0, right.shape[1], tile_cols):
                tile_list.append((left, right, out, row, col))

    def store_tile(i):
        _, _, out, row, col = tile_list[i]
        return pltpu.make_async_copy(
            tiles.at[i % 2], out.at[pl.ds(row, tile_rows), pl.ds(col, tile_cols)], tile_sem.at[i % 2]
        )

    def tile_step(i):
        left, right, _, row, col = tile_list[i]
        if col == 0:
            turned[...] = left[:, pl.ds(row, tile_rows)].T
        if i >= 2:
            store_tile(i - 2).wait()

        def cols(n, carry):
            there, put = rows_at(col + n * COLS, COLS), rows_at(n * COLS, COLS)
            tiles[i % 2, :, put] = project(turned[...], right[:, there])
            return carry

        lax.fori_loop(0, tile_cols // COLS, cols, 0)
        store_tile(i).start()

    load(0, w_out_hbm, w_out).wait()
    middle_step(0)
    norm_step(0)
    load(1, w_up_hbm, w_up).wait()
    hidden_step(0)
    produce(0, line.part)
    line.meet()
    load(5, cot_hbm, cot).wait()
    steps = []
    for c in range(1, blocks):
        steps.append([functools.partial(f, c) for f in (middle_step, norm_step)])
        steps.append([functools.partial(hidden_step, c)])
    steps[-1].append(produce_next)
    slots = (line.pieces + LATE) // SLOT
    count = len(tile_list)
    per = -(-count // max(slots - len(steps), 1))
    for i in range(0, count, per):
        steps.append([functools.partial(tile_step, j) for j in range(i, min(i + per, count))])
    for i in range(max(slots, len(steps))):
        if i < slots:
            line.slot(i)
        if i < len(steps):
            for step in steps[i]:
                step()
    store_first = pltpu.make_async_copy(line.total, first_hbm, out_sem.at[3])
    store_first.start()
    store_tile(count - 2).wait()
    store_tile(count - 1).wait()
    store_next.wait()
    store_acts.wait()
    store_dh.wait()
    store_first.wait()
    line.finish()


def mlp(mixed, w_out, inputs, w_up, d_acts, cotangent, b_out, gain, shift, b_up):
    seq, width = inputs.shape
    hidden = w_up.shape[1]
    vmem = pl.BlockSpec(memory_space=pltpu.VMEM)
    dma = pltpu.SemaphoreType.DMA
    shape = jax.ShapeDtypeStruct
    block = lambda cols, dtype: pltpu.VMEM((BLOCK, cols), dtype)
    return pl.pallas_call(
        mlp_kernel,
        out_shape=(
            shape((seq, width), F32),
            shape((seq, hidden), BF16),
            shape((seq, hidden), BF16),
            shape((hidden, width), F32),
            shape((width, hidden), F32),
            shape((BLOCK, width), F32),
            shape((BLOCK, width), F32),
            shape((8, hidden), F32),
        ),
        in_specs=[HBM] * 6 + [vmem] * 4,
        out_specs=(HBM,) * 7 + (vmem,),
        scratch_shapes=[
            pltpu.VMEM(w_out.shape, BF16),
            pltpu.VMEM(w_up.shape, BF16),
            pltpu.VMEM((seq, width), BF16),
            pltpu.VMEM((seq, hidden), BF16),
            pltpu.VMEM((seq, hidden), BF16),
            pltpu.VMEM((seq, width), BF16),
            block(w_out.shape[0], BF16),
            block(width, BF16),
            block(width, F32),
            block(hidden, F32),
            pltpu.VMEM((2 * BLOCK, seq), BF16),
            pltpu.VMEM((2, 2 * BLOCK, width // 2), F32),
            dma((6,)),
            dma((4,)),
            dma((2,)),
        ]
        + LineSum.scratch(BLOCK, BLOCK // PIECE, width),
        compiler_params=pltpu.CompilerParams(
            collective_id=3, has_side_effects=True, vmem_limit_bytes=VMEM_LIMIT
        ),
        cost_estimate=pl.CostEstimate(flops=60 * 10**9, bytes_accessed=2**26, transcendentals=0),
        name="mlp",
    )(
        mixed, w_out, inputs, w_up, d_acts, cotangent, b_out.reshape(1, width),
        gain.reshape(1, width), shift.reshape(1, width), b_up.reshape(1, hidden),
    )


def mlp_attend_back_kernel(
    heads,
    dh_hbm, w_up_hbm, w_out_hbm, mid_hbm, cot_hbm, q_hbm, acts_hbm, w_down_hbm, normed_hbm, mixed_hbm,
    first_hbm, second_hbm,
    kv_ref, kt_ref, code_ref, doc_ref, lse_ref, gain_ref, b_down_ref,
    d_mid_hbm, dq_hbm, feed_out, feed_next, grads_hbm, dkv_ref, sums_ref,
    w_up, w_out, dh, mid, cot, q, normed, mixed, d_branch, d_mixed, dq, grads, bias_ref,
    load_sem, out_sem, *line_refs,
):
    line = LineSum(line_refs)
    seq, width = q_hbm.shape
    m = lax.axis_index("mp")
    own_cols = mixed.shape[1]
    own = rows_at(m * own_cols, own_cols)
    ring = line.part.shape[0] // BLOCK
    hd = kt_ref.shape[0]
    chunks = seq // BLOCK
    slots = BLOCK // (PIECE * SLOT)
    count = REACH * BLOCK
    scale = 1.0 / math.sqrt(hd)

    def load(i, src, dst):
        return pltpu.make_async_copy(src, dst, load_sem.at[i])

    def load_dh(b):
        return load(2, dh_hbm.at[rows_at((b + 1) * BLOCK, BLOCK)], dh)

    def load_chunk(c):
        at = rows_at(c * BLOCK, BLOCK)
        return [
            load(3, mid_hbm.at[at], mid),
            load(4, cot_hbm.at[at], cot),
            load(5, q_hbm.at[at], q),
            load(6, normed_hbm.at[at], normed),
            load(7, mixed_hbm.at[at, own], mixed),
        ]

    def block_at(b):
        return rows_at((b % ring) * BLOCK, BLOCK)

    load_first = load(8, first_hbm, line.total.at[block_at(ring - 1)])

    def store(i, src, dst, c):
        return pltpu.make_async_copy(src, dst.at[rows_at(c * BLOCK, BLOCK)], out_sem.at[i])

    def stores(c, which=(0, 1)):
        pairs = ((mid, d_mid_hbm), (dq, dq_hbm))
        return [store(i, *pairs[i], c) for i in which]

    load_second = load(9, second_hbm, line.part.at[block_at(0)])
    load_second.start()
    load(0, w_up_hbm, w_up).start()
    load_dh(1).start()
    load(1, w_out_hbm, w_out).start()
    load_first.start()
    load_down = load(0, w_down_hbm, w_up)

    def load_acts(j):
        return load(2, acts_hbm.at[rows_at(j * BLOCK, BLOCK)], dh)

    def load_mid(j):
        return load(3, mid_hbm.at[rows_at(j * BLOCK, BLOCK)], mid)

    line.greet()
    dkv_ref[...] = jnp.zeros_like(dkv_ref)
    sums_ref[...] = jnp.zeros_like(sums_ref)
    grads[...] = jnp.zeros_like(grads)

    lines = chunks - 1

    def produce(b):
        at = block_at(b)
        load_dh(b).wait()

        def cols(n, carry):
            there = rows_at(n * COLS, COLS)
            line.part[at, there] = dot_t(dh[...], w_up[there, :])
            return carry

        lax.fori_loop(0, width // COLS, cols, 0)

        @pl.when(b + 1 < lines)
        def _():
            load_dh(b + 1).start()

        @pl.when(b + 1 == lines)
        def _():
            load_acts(0).start()
            load_down.start()

    def produce_feed(j):
        at = block_at(lines + j)
        load_acts(j).wait()
        load_mid(j).wait()

        @pl.when(j == 0)
        def _():
            load_down.wait()

        def cols(n, carry):
            there = rows_at(n * COLS, COLS)
            line.part[at, there] = project(dh[...], w_up[:, there])
            return carry

        lax.fori_loop(0, width // COLS, cols, 0)

        @pl.when(m == 0)
        def _():
            line.part[at, :] += mid[...]

        load_acts(j + 1).start()

    def add_grads(first, left, right):
        at = pl.ds(first, own_cols)

        def cols(n, carry):
            there = rows_at(n * COLS, COLS)
            grads[at, there] += dot_down(left, right[:, there])
            return carry

        lax.fori_loop(0, width // COLS, cols, 0)

    def norm_step(c, half):
        def strip(i, carry):
            row = half * (BLOCK // 2) + i * STRIP
            at = rows_at(row, STRIP)
            grad = line.total[rows_at(((c + ring - 1) % ring) * BLOCK + row, STRIP), :]
            d_in, weighted = norm_back_rows(mid[at, :], grad, gain_ref[...])
            cot_rows = cot[at, :].astype(F32)
            d_mid = cot_rows + d_in
            low = d_mid.astype(BF16)
            mid[at, :] = d_mid
            d_branch[at, :] = low
            sums_ref[0] += fold_rows(weighted)
            sums_ref[1] += fold_rows(grad)
            sums_ref[2] += fold_rows(low.astype(F32))
            sums_ref[3] += fold_rows(cot_rows)
            return carry

        lax.fori_loop(0, BLOCK // 2 // STRIP, strip, 0)

    def mixed_step(c):
        def cols(n, carry):
            there = rows_at(n * COLS, COLS)
            d_mixed[:, there] = dot_t(d_branch[...], w_out[there, :]).astype(BF16)
            return carry

        lax.fori_loop(0, width // COLS, cols, 0)
        keys = pl.ds(pl.multiple_of(c * BLOCK, BLOCK), count)
        bias_ref[...] = mask_bias(
            code_ref[keys, :], doc_ref[:, rows_at(c * BLOCK, BLOCK)],
            (c - REACH + 1) * BLOCK, count, c * BLOCK, BLOCK,
        )

    def heads_step(c, g):
        keys = pl.ds(pl.multiple_of(c * BLOCK, BLOCK), count)
        queries = rows_at(c * BLOCK, BLOCK)
        dk = jnp.zeros((count, hd), F32)
        dv = jnp.zeros((count, hd), F32)
        for u in range(GROUP):
            h = g * GROUP + u
            cols = rows_at(h * hd, hd)
            qh = q[:, cols]
            dm = d_mixed[:, cols]
            s = dot_t(kv_ref[keys, pl.ds(0, hd)], qh) * scale + bias_ref[...]
            probs = jnp.exp(s - lse_ref[pl.ds(h, 1), queries])
            d_probs = dot_t(kv_ref[keys, pl.ds(hd, hd)], dm)
            t = probs * d_probs
            inner = jnp.sum(t, axis=0, keepdims=True)
            ds = (t - probs * inner).astype(BF16)
            dqh = project(kt_ref[:, keys], ds) * scale
            dq[:, cols] = dqh.T.astype(BF16)
            dk = dk + project(ds, qh)
            dv = dv + project(probs.astype(BF16), dm)
        dkv_ref[keys, pl.ds(0, hd)] += dk * scale
        dkv_ref[keys, pl.ds(hd, hd)] += dv

    load_second.wait()
    line.meet()
    for k in range(3):
        line.slot(k)
    load(0, w_up_hbm, w_up).wait()
    load(1, w_out_hbm, w_out).wait()
    load_first.wait()

    def cycle(c, carry):
        base = c * slots + 3

        @pl.when(c >= 1)
        def _():
            for i in stores(c - 1):
                i.wait()

        @pl.when(c + 1 >= lines)
        def _():
            load_mid(c + 1 - lines).start()

        line.slot(base)

        @pl.when(c >= 2)
        def _():
            line.free((c - 2) * (BLOCK // PIECE), BLOCK // PIECE)

        @pl.when(c + 1 < lines)
        def _():
            produce(c + 1)

        @pl.when(c + 1 >= lines)
        def _():
            produce_feed(c + 1 - lines)

        for i in load_chunk(c):
            i.start()
        line.slot(base + 1)
        for i in load_chunk(c):
            i.wait()
        norm_step(c, 0)
        line.slot(base + 2)
        norm_step(c, 1)
        stores(c, (0,))[0].start()
        line.slot(base + 3)
        mixed_step(c)
        add_grads(own_cols, mixed[...], d_branch)

        def some_heads(g, carry):
            line.slot(base + 4 + g)
            heads_step(c, g)
            return carry

        lax.fori_loop(0, heads // GROUP, some_heads, 0)
        stores(c, (1,))[0].start()
        add_grads(0, dq[:, own], normed)

        def strip(i, carry):
            sums_ref[4] += fold_rows(dq[rows_at(i * STRIP, STRIP), :].astype(F32))
            return carry

        lax.fori_loop(0, BLOCK // STRIP, strip, 0)
        return carry

    lax.fori_loop(0, chunks, cycle, 0)
    keep_grads = pltpu.make_async_copy(grads, grads_hbm, out_sem.at[3])
    keep_grads.start()

    stores(chunks - 1, (0,))[0].wait()
    load_mid(FEED_EARLY).start()
    load_acts(FEED_EARLY).wait()
    load_mid(FEED_EARLY).wait()
    share = jnp.where(m == 0, 1.0, 0.0)

    def next_cols(n, carry):
        there = rows_at(n * COLS, COLS)
        mid[:, there] = project(dh[...], w_up[:, there]) + mid[:, there] * share
        return carry

    lax.fori_loop(0, width // COLS, next_cols, 0)
    keep_next = pltpu.make_async_copy(mid, feed_next, out_sem.at[2])
    keep_next.start()
    for k in range(chunks * slots + 3, (line.pieces + LATE) // SLOT):
        line.slot(k)
    keep_next.wait()
    stores(chunks - 1, (1,))[0].wait()
    keep_feed = []
    for j, low in enumerate((d_branch, d_mixed)):

        def strip(i, carry, j=j, low=low):
            total = line.total[rows_at((lines + j) % ring * BLOCK + i * STRIP, STRIP), :]
            low[rows_at(i * STRIP, STRIP), :] = (total + b_down_ref[...]).astype(BF16)
            return carry

        lax.fori_loop(0, BLOCK // STRIP, strip, 0)
        keep_feed.append(
            pltpu.make_async_copy(low, feed_out.at[pl.ds(j * BLOCK, BLOCK)], out_sem.at[j])
        )
        keep_feed[j].start()
    for i in keep_feed:
        i.wait()
    keep_grads.wait()
    line.finish((lines - 1) * (BLOCK // PIECE))


def mlp_attend_back(
    d_hidden, w_up, w_out, middle, cotangent, queries, acts, w_down, normed, mixed, first, second, own_cols,
    keyval, keys_t, code_col, doc_row, lse, gain, b_down,
):
    seq, width = queries.shape
    heads = width // keys_t.shape[0]
    vmem = pl.BlockSpec(memory_space=pltpu.VMEM)
    dma = pltpu.SemaphoreType.DMA
    block = lambda dtype: pltpu.VMEM((BLOCK, width), dtype)
    return pl.pallas_call(
        functools.partial(mlp_attend_back_kernel, heads),
        out_shape=(
            jax.ShapeDtypeStruct((seq, width), F32),
            jax.ShapeDtypeStruct((seq, width), BF16),
            jax.ShapeDtypeStruct((FEED_EARLY * BLOCK, width), BF16),
            jax.ShapeDtypeStruct((BLOCK, width), F32),
            jax.ShapeDtypeStruct((2 * own_cols, width), F32),
            jax.ShapeDtypeStruct(keyval.shape, F32),
            jax.ShapeDtypeStruct((5, 8, width), F32),
        ),
        in_specs=[HBM] * 12 + [vmem] * 7,
        out_specs=(HBM, HBM, HBM, HBM, HBM, vmem, vmem),
        scratch_shapes=[
            pltpu.VMEM(w_up.shape, BF16),
            pltpu.VMEM(w_out.shape, BF16),
            pltpu.VMEM((BLOCK, d_hidden.shape[1]), BF16),
            block(F32),
            block(BF16),
            block(BF16),
            block(BF16),
            pltpu.VMEM((BLOCK, own_cols), BF16),
            block(BF16),
            block(BF16),
            block(BF16),
            pltpu.VMEM((2 * own_cols, width), F32),
            pltpu.VMEM((REACH * BLOCK, BLOCK), F32),
            dma((10,)),
            dma((4,)),
        ]
        + LineSum.scratch(seq - BLOCK, (seq + (FEED_EARLY - 1) * BLOCK) // PIECE, width),
        compiler_params=pltpu.CompilerParams(
            collective_id=1, has_side_effects=True, vmem_limit_bytes=VMEM_LIMIT
        ),
        cost_estimate=pl.CostEstimate(
            flops=200 * 10**9, bytes_accessed=2**25, transcendentals=0
        ),
        name="mlp_attend_back",
    )(
        d_hidden, w_up, w_out, middle, cotangent, queries, acts, w_down, normed, mixed, first, second,
        keyval, keys_t, code_col, doc_row, lse, gain.reshape(1, width), b_down.reshape(1, width),
    )


def feed_kernel(
    rounds,
    acts_hbm, w_down_hbm, mid_hbm, dq_hbm, w_q_hbm, in_hbm, d_mid_hbm, normed_hbm, next_hbm,
    dkv_f_ref, w_kv_ref, gain_ref, bias_ref, sums_in, b_up_in,
    out_hbm, in_grad_hbm, table_out, vectors_out,
    w_down, w_q, acts, mid, dq, xs, d_mid, spread, low, in_grad, normed, dkv_ref, sums, trade, trade_in, table, table_in, table_all,
    load_sem, out_sem, t_send, t_recv, h_send, h_recv, d_send, d_recv, *line_refs,
):
    line = LineSum(line_refs)
    rows, width = line.part.shape
    seq = rows + FEED_EARLY * BLOCK
    blocks = seq // BLOCK
    chunks = rows // BLOCK
    slots = BLOCK // (PIECE * SLOT)
    planes, _, cols_q = w_q.shape
    m = lax.axis_index("mp")
    d = lax.axis_index("dp")
    peers = [{"dp": flip_bit(d, 1 << r)} for r in range(rounds)]

    def load(i, src, dst):
        return pltpu.make_async_copy(src, dst, load_sem.at[i])

    def load_feed(c):
        at = rows_at((c + FEED_EARLY) * BLOCK, BLOCK)
        return [load(2, acts_hbm.at[at], acts), load(3, mid_hbm.at[at], mid)]

    def load_grad(c):
        at = rows_at(c * BLOCK, BLOCK)
        return [
            load(4, dq_hbm.at[at], dq),
            load(5, in_hbm.at[at], xs),
            load(6, d_mid_hbm.at[at], d_mid),
        ]

    def store(i, src, dst, c):
        return pltpu.make_async_copy(src, dst.at[rows_at(c * BLOCK, BLOCK)], out_sem.at[i])

    def load_normed(c):
        return load(7, normed_hbm.at[rows_at(c * BLOCK, BLOCK)], normed)

    load_next = load(8, next_hbm, line.part.at[pl.ds(0, BLOCK)])
    load_next.start()
    load(0, w_down_hbm, w_down).start()
    if chunks > 1:
        for i in load_feed(1):
            i.start()
    load_normed(0).start()
    load(1, w_q_hbm, w_q).start()
    for i in load_grad(0):
        i.start()
    line.greet(peers)
    sums[...] = jnp.zeros_like(sums)
    dkv_ref[...] = dkv_f_ref[pl.ds(FRONT, seq), :].astype(BF16)
    hd = dkv_ref.shape[1] // 2

    def produce(c):
        at = rows_at(c * BLOCK, BLOCK)
        for i in load_feed(c):
            i.wait()

        def cols(n, carry):
            there = rows_at(n * COLS, COLS)
            line.part[at, there] = project(acts[...], w_down[:, there])
            return carry

        lax.fori_loop(0, width // COLS, cols, 0)

        @pl.when(m == 0)
        def _():
            line.part[at, :] += mid[...]

        if c + 1 < chunks:
            for i in load_feed(c + 1):
                i.start()

    def output_step(c):
        def strip(i, carry):
            at = rows_at(i * STRIP, STRIP)
            there = rows_at(c * BLOCK + i * STRIP, STRIP)
            low[at, :] = (line.total[there, :] + bias_ref[...]).astype(BF16)
            return carry

        lax.fori_loop(0, BLOCK // STRIP, strip, 0)

    def spread_step(c):
        here = rows_at(c * BLOCK, BLOCK)

        def cols(n, carry):
            there = rows_at(n * COLS, COLS)
            total = dot_t(dkv_ref[here, :], w_kv_ref[there, :])
            for i in range(planes):
                total = total + dot_t(dq[:, pl.ds(i * cols_q, cols_q)], w_q[i, there, :])
            spread[:, there] = total
            return carry

        lax.fori_loop(0, width // COLS, cols, 0)

    def norm_step(c):
        def strip(i, carry):
            at = rows_at(i * STRIP, STRIP)
            grad = spread[at, :]
            d_in, weighted = norm_back_rows(xs[at, :].astype(F32), grad, gain_ref[...])
            in_grad[at, :] = (d_mid[at, :] + d_in).astype(BF16)
            sums[0] += fold_rows(weighted)
            sums[1] += fold_rows(grad)
            return carry

        lax.fori_loop(0, BLOCK // STRIP, strip, 0)

    def swap(r):
        return pltpu.make_async_remote_copy(
            trade.at[r], trade_in.at[r], t_send.at[r], t_recv.at[r],
            device_id=peers[r], device_id_type=MESH,
        )

    def vectors_first():
        trade[0] = jnp.zeros_like(trade.at[0])
        for i in range(2):
            trade[0, i : i + 1] = jnp.sum(sums[i], axis=0, keepdims=True)
        for i in range(sums_in.shape[0]):
            trade[0, 2 + i : 3 + i] = jnp.sum(sums_in[i], axis=0, keepdims=True)
        at = 2 + sums_in.shape[0]
        trade[0, at : at + 1] = b_up_in[...]
        d_values = dkv_f_ref[pl.ds(FRONT, seq), pl.ds(hd, hd)]
        trade[0, at + 1 : at + 2, 0:hd] = jnp.sum(d_values, axis=0, keepdims=True)
        swap(0).start()

    def vectors_next(r):
        swap(r).wait()
        trade[r + 1] = trade[r] + trade_in[r]
        if r + 1 < rounds:
            swap(r + 1).start()
        else:
            vectors_out[...] = trade[r + 1]

    def table_block(c):
        load_normed(c).wait()

        def cols(n, carry):
            there = rows_at(n * COLS, COLS)
            part = dot_down(dkv_ref[pl.ds(c * BLOCK, BLOCK), :], normed[:, there])
            table[:, there] = part if c == 0 else table[:, there] + part
            return carry

        lax.fori_loop(0, width // COLS, cols, 0)
        if c + 1 < blocks:
            load_normed(c + 1).start()

    bits = [lax.rem(lax.div(d, 1 << r), 2) for r in range(rounds)]
    base = [0]
    size = [table.shape[0]]
    for r in range(rounds):
        size.append(size[r] // 2)
        base.append(base[r] + bits[r] * size[r + 1])

    def part_of(start, count):
        return pl.ds(pl.multiple_of(start, 8), count)

    def halve(r):
        away = part_of(base[r] + (1 - bits[r]) * size[r + 1], size[r + 1])
        into = pl.ds(size[0] - size[r], size[r + 1])
        return pltpu.make_async_remote_copy(
            table.at[away], table_in.at[into], h_send.at[r], h_recv.at[r],
            device_id=peers[r], device_id_type=MESH,
        )

    def double(r, mine):
        start = base[r] + (bits[r] if mine else 1 - bits[r]) * size[r + 1]
        at = part_of(start, size[r + 1])
        return pltpu.make_async_remote_copy(
            table_all.at[at], table_all.at[at], d_send.at[r], d_recv.at[r],
            device_id=peers[r], device_id_type=MESH,
        )

    store_table = pltpu.make_async_copy(table_all, table_out, out_sem.at[2])

    def table_step(i):
        if 1 <= i <= rounds:
            r = i - 1
            halve(r).wait()
            at = part_of(base[r + 1], size[r + 1])
            whole = table_all if i == rounds else table
            whole[at, :] = table[at, :] + table_in[pl.ds(size[0] - size[r], size[r + 1]), :]
        elif i > rounds:
            r = 2 * rounds - i
            double(r, True).wait_send()
            double(r, False).wait_recv()
        if i < rounds:
            halve(i).start()
        elif i < 2 * rounds:
            double(2 * rounds - 1 - i, True).start()
        else:
            store_table.start()

    load_next.wait()
    line.meet(peers)
    for k in range(3):
        line.slot(k)
    load(0, w_down_hbm, w_down).wait()
    load(1, w_q_hbm, w_q).wait()

    def spread_block(v):
        for i in load_grad(v):
            i.wait()
        spread_step(v)

    def norm_block(v):
        if v >= 1:
            store(1, in_grad, in_grad_hbm, v - 1).wait()
        norm_step(v)
        store(1, in_grad, in_grad_hbm, v).start()
        if v + 1 < blocks:
            for i in load_grad(v + 1):
                i.start()

    def output_block(c):
        if c >= 1:
            store(0, low, out_hbm, c - 1).wait()
        output_step(c)
        store(0, low, out_hbm, c).start()

    slot_count = (line.pieces + LATE) // SLOT
    steps = [[] for _ in range(max(slot_count, 4 * blocks + 8))]
    for c in range(1, chunks):
        steps[(c - 1) * slots + 3].append(functools.partial(produce, c))
    for c in range(chunks):
        steps[(c + 1) * slots - 1 + LATE // SLOT].append(functools.partial(output_block, c))
    for v in range(blocks):
        steps[3 + 2 * v].append(functools.partial(spread_block, v))
        steps[4 + 2 * v].append(functools.partial(norm_block, v))
        steps[2 + 2 * v].append(functools.partial(table_block, v))
    done = 4 + 2 * blocks
    for i in range(rounds + 1):
        steps[done + i].append(vectors_first if i == 0 else functools.partial(vectors_next, i - 1))
    first = 1 + 2 * blocks
    apart = max(1, min(2, (len(steps) - 1 - first) // (2 * rounds)))
    for i in range(2 * rounds + 1):
        steps[first + i * apart].append(functools.partial(table_step, i))
    for i, todo in enumerate(steps):
        if i >= 3 and i < slot_count:
            line.slot(i)
        for step in todo:
            step()
    store(0, low, out_hbm, chunks - 1).wait()
    store(1, in_grad, in_grad_hbm, blocks - 1).wait()
    store_table.wait()
    line.finish()


def feed_and_input_grad(
    acts, w_down, middle, b_down, d_queries, all_query, d_keyval_sum, w_keyval, inputs, d_middle, gain,
    normed, feed_next, sums, b_up,
):
    seq, width = inputs.shape
    rounds = (lax.axis_size("dp") - 1).bit_length()
    vmem = pl.BlockSpec(memory_space=pltpu.VMEM)
    dma = pltpu.SemaphoreType.DMA
    block = lambda dtype: pltpu.VMEM((BLOCK, width), dtype)
    rest = seq - FEED_EARLY * BLOCK
    shape = jax.ShapeDtypeStruct
    table = (w_keyval.shape[1], width)
    return pl.pallas_call(
        functools.partial(feed_kernel, rounds),
        out_shape=(
            shape((rest, width), BF16),
            shape((seq, width), BF16),
            shape(table, F32),
            shape((16, width), F32),
        ),
        in_specs=[HBM] * 9 + [vmem] * 6,
        out_specs=(HBM, HBM, HBM, vmem),
        scratch_shapes=[
            pltpu.VMEM(w_down.shape, BF16),
            pltpu.VMEM(all_query.shape, BF16),
            pltpu.VMEM((BLOCK, acts.shape[1]), BF16),
            block(F32),
            block(BF16),
            block(BF16),
            block(F32),
            block(F32),
            block(BF16),
            block(BF16),
            block(BF16),
            pltpu.VMEM((seq, w_keyval.shape[1]), BF16),
            pltpu.VMEM((2, 8, width), F32),
            pltpu.VMEM((rounds + 1, 16, width), F32),
            pltpu.VMEM((rounds, 16, width), F32),
            pltpu.VMEM(table, F32),
            pltpu.VMEM(table, F32),
            pltpu.VMEM(table, F32),
            dma((9,)),
            dma((3,)),
            dma((rounds,)),
            dma((rounds,)),
            dma((rounds,)),
            dma((rounds,)),
            dma((rounds,)),
            dma((rounds,)),
        ]
        + LineSum.scratch(rest, rest // PIECE, width),
        compiler_params=pltpu.CompilerParams(
            collective_id=2, has_side_effects=True, vmem_limit_bytes=VMEM_LIMIT
        ),
        cost_estimate=pl.CostEstimate(
            flops=150 * 10**9, bytes_accessed=2**25, transcendentals=0
        ),
        name="feed_and_input_grad",
    )(
        acts, w_down, middle, d_queries, all_query, inputs, d_middle, normed, feed_next,
        d_keyval_sum, w_keyval, gain.reshape(1, width), b_down.reshape(1, width), sums,
        b_up.reshape(1, width),
    )


def shards(
    inputs,
    doc_ids,
    pad_mask,
    attn_gain,
    attn_shift,
    w_query,
    b_query,
    w_keyval,
    b_value,
    w_out,
    b_out,
    mlp_gain,
    mlp_shift,
    w_up,
    b_up,
    w_down,
    b_down,
    cotangent,
):
    seq = doc_ids.shape[1]
    hd = b_value.shape[0]
    width = inputs.shape[1]
    own_cols = w_query.shape[1]
    own = lax.axis_index("mp") * own_cols
    docs = doc_ids[0]
    codes = jnp.where(pad_mask[0] == 1, docs, -1)
    code_col = jnp.pad(codes, (FRONT, 0), constant_values=-2).reshape(-1, 1)
    doc_row = docs.reshape(1, seq)

    all_query, all_out, normed_attn, queries, mixed, d_acts, keyval, keys_t, lse = attention_front(
        inputs, w_query, b_query, w_keyval, b_value, w_out, attn_gain, attn_shift, code_col, doc_row,
        cotangent, w_down,
    )
    middle, acts, d_hidden, grad_w_down, grad_w_up, first, second, grad_b_up = mlp(
        mixed, all_out, inputs, w_up, d_acts, cotangent, b_out, mlp_gain, mlp_shift, b_up
    )
    grad_b_up = jnp.sum(grad_b_up, axis=0)
    grad_w_up = lax.psum_scatter(grad_w_up, "dp", scatter_dimension=0, tiled=True)
    grad_w_down = lax.psum_scatter(grad_w_down, "dp", scatter_dimension=1, tiled=True)

    d_middle, d_queries, out_first, feed_next, grads, d_keyval_sum, sums = mlp_attend_back(
        d_hidden, w_up, all_out, middle, cotangent, queries, acts, w_down, normed_attn, mixed, first, second,
        own_cols,
        keyval, keys_t, code_col, doc_row, lse, mlp_gain, b_down,
    )
    grads, grad_w_down, grad_w_up = lax.optimization_barrier((grads, grad_w_down, grad_w_up))
    grads = lax.psum_scatter(grads, "dp", scatter_dimension=1, tiled=True)
    out_rest, input_grad, grad_w_keyval, totals = feed_and_input_grad(
        acts, w_down, middle, b_down, d_queries, all_query, d_keyval_sum, w_keyval, inputs, d_middle,
        attn_gain, normed_attn, feed_next, sums, grad_b_up,
    )
    outputs = jnp.concatenate([out_first, out_rest], 0)
    grad_w_query, grad_w_out = grads[:own_cols].T, grads[own_cols:]
    grad_w_keyval = grad_w_keyval.T
    grad_attn_gain, grad_attn_shift, grad_mlp_gain, grad_mlp_shift = (totals[i] for i in range(4))
    grad_b_out, grad_b_down, grad_b_query, grad_b_up = (totals[i] for i in range(4, 8))
    grad_b_query = lax.dynamic_slice_in_dim(grad_b_query, own, own_cols, 0)
    grad_b_value = totals[8, :hd]
    return (
        outputs,
        input_grad,
        grad_attn_gain,
        grad_attn_shift,
        grad_w_query,
        grad_b_query,
        grad_w_keyval,
        grad_b_value,
        grad_w_out,
        grad_b_out,
        grad_mlp_gain,
        grad_mlp_shift,
        grad_w_up,
        grad_b_up,
        grad_w_down,
        grad_b_down,
    )


def solution(mesh):
    return jax.shard_map(
        shards,
        mesh=mesh,
        in_specs=(
            P("dp", None),
            P("dp", None),
            P("dp", None),
            P(),
            P(),
            P(None, "mp"),
            P("mp"),
            P(),
            P(),
            P("mp", None),
            P(),
            P(),
            P(),
            P(None, "mp"),
            P("mp"),
            P("mp", None),
            P(),
            P("dp", None),
        ),
        out_specs=(
            P("dp", None),
            P("dp", None),
            P(),
            P(),
            P("dp", "mp"),
            P("mp"),
            P(),
            P(),
            P("mp", "dp"),
            P(),
            P(),
            P(),
            P("dp", "mp"),
            P("mp"),
            P("mp", "dp"),
            P(),
        ),
        check_vma=False,
    )
```

```python
import functools
import math

import jax
import jax.numpy as jnp
from jax import lax
from jax.experimental import pallas as pl
from jax.experimental.pallas import tpu as pltpu
from jax.sharding import PartitionSpec as P

EPS = 1e-05
MESH = pl.DeviceIdType.MESH
F32 = jnp.float32
BF16 = jnp.bfloat16
VMEM_LIMIT = 60 * 2**20
HBM = pl.BlockSpec(memory_space=pl.ANY)


def norm_rows(rows_in, gain, shift):
    center = rows_in - jnp.mean(rows_in, axis=-1, keepdims=True)
    spread = jnp.mean(center * center, axis=-1, keepdims=True)
    return center * lax.rsqrt(spread + EPS) * gain + shift


def project(left, right):
    return jnp.dot(left, right, preferred_element_type=F32)


STRIP = 16
COLS = 512
BLOCK = 256
REACH = 3
GROUP = 4
NEG = -1e30
FRONT = (REACH - 1) * BLOCK


def key_window(c):
    first = max(0, c - REACH + 1) * BLOCK
    return first, (c + 1) * BLOCK - first


def mask_bias(code_col, doc_row, first_key, keys, first_query, queries):
    j = first_key + lax.broadcasted_iota(jnp.int32, (keys, queries), 0)
    i = first_query + lax.broadcasted_iota(jnp.int32, (keys, queries), 1)
    ok = ((j < i) & (code_col == doc_row)) | (j == i)
    return jnp.where(ok, 0.0, NEG)


def dot_t(a, b):
    return lax.dot_general(a, b, (((1,), (1,)), ((), ())), preferred_element_type=F32)


def rows_at(start, count):
    return pl.ds(pl.multiple_of(start, count), count)


def mp_partner(m, r):
    if r == 1:
        return m + 1 - 2 * lax.rem(m, 2)
    if r == 2:
        return m + 2 - 4 * lax.div(m, 2)
    return 3 - m


def flip_bit(d, bit):
    on = lax.rem(lax.div(d, bit), 2)
    return d + bit * (1 - 2 * on)


def front_kernel(
    heads,
    wq, wo, in_hbm, cot_hbm, w_down_hbm, bq, w_kv, gain_ref, shift_ref, bv_ref, code_ref, doc_ref,
    wq_out, wo_out, normed_hbm, q_hbm, mixed_hbm, d_acts_hbm, kv_ref, kt_ref, lse_ref,
    own_q, own_o, gq, go, sq, so, normed, q_ring, mixed_ring, vt, bias_ref, bq_all, cot, down, d_acts,
    load_sem, cot_sem, down_sem, d_acts_sem, ship_sem, o_sem, ring_sem, z_send, z_recv, b_send, b_recv, n_send, n_recv,
):
    m = lax.axis_index("mp")
    d = lax.axis_index("dp")
    dc, dx, dy = flip_bit(d, 1), flip_bit(d, 2), flip_bit(d, 4)
    dxy = flip_bit(dx, 4)
    is_mid = (m == 1) | (m == 2)
    buddy, across = {"mp": mp_partner(m, 1)}, {"mp": 3 - m}
    upper = lax.div(m, 2)
    inner = lax.rem(m + upper, 2)

    def plane_at(s):
        q = (1 - inner, 2, 3)[s]
        return q + upper * (3 - 2 * q)

    g = (gq, go)
    half = (gq.shape[2] // 2, go.shape[2] // 2)
    seq, width = normed.shape
    cols_q = q_ring.shape[2]
    hd = vt.shape[0]
    blocks = seq // BLOCK
    scale = 1.0 / math.sqrt(hd)
    planes = 4

    loads = [
        pltpu.make_async_copy(wq.at[d], own_q, load_sem.at[0]),
        pltpu.make_async_copy(wo.at[d], own_o, load_sem.at[1]),
        pltpu.make_async_copy(in_hbm, normed, load_sem.at[2]),
        pltpu.make_async_copy(wq, sq.at[m], load_sem.at[3]),
        pltpu.make_async_copy(wq, wq_out.at[m], load_sem.at[4]),
        pltpu.make_async_copy(wo, wo_out.at[m], load_sem.at[5]),
    ]
    for c in loads:
        c.start()
    bar = pltpu.get_barrier_semaphore()
    for r in (1, 2, 3):
        pl.semaphore_signal(bar, inc=1, device_id={"mp": mp_partner(m, r)}, device_id_type=MESH)
    for n in (dc, dx, dy):
        pl.semaphore_signal(bar, inc=1, device_id={"dp": n}, device_id_type=MESH)
    loads[0].wait()
    gq[m, d] = own_q[...].astype(F32)
    loads[1].wait()
    go[m, d] = own_o[...].astype(F32)
    bq_all[m] = bq[...]
    pl.semaphore_wait(bar, 6)

    def z_copy(w, plane, to, i):
        ref = g[w].at[plane, d]
        return pltpu.make_async_remote_copy(
            ref, ref, z_send.at[w, i], z_recv.at[w, plane], device_id=to, device_id_type=MESH
        )

    def z_own(w, wait=False):
        def go_or_wait(c):
            if wait:
                c.wait_send()
            else:
                c.start()

        go_or_wait(z_copy(w, m, buddy, 0))

        @pl.when(is_mid)
        def _():
            go_or_wait(z_copy(w, m, across, 1))

    def z_forward(w, s, wait=False):
        @pl.when(is_mid)
        def _():
            c = z_copy(w, plane_at(s), across if s == 0 else buddy, 2 + s)
            if wait:
                c.wait_send()
            else:
                c.start()

    def z_land(w, s):
        z_copy(w, plane_at(s), buddy, 0).wait_recv()

    def bias_copy(r, plane):
        return pltpu.make_async_remote_copy(
            bq_all.at[plane], bq_all.at[plane], b_send.at[r - 1], b_recv.at[r - 1],
            device_id={"mp": mp_partner(m, r)}, device_id_type=MESH,
        )

    sent_eighth = (d, d, d, dx, dy, dx, dy, dxy)
    landed_eighth = (dx, dy, dc, flip_bit(dx, 1), flip_bit(dy, 1), dxy, dxy, flip_bit(dxy, 1))
    sent_to = (dx, dy, dc, dc, dc, dy, dx, dc)

    def near(kind, w, r, eighths):
        q = plane_at(r)
        ref = g[w].at[q, eighths[kind]]
        if kind == 5:
            ref = g[w].at[q, eighths[kind], pl.ds(0, half[w])]
        if kind == 6:
            ref = g[w].at[q, eighths[kind], pl.ds(half[w], half[w])]
        return pltpu.make_async_remote_copy(
            ref, ref, n_send.at[kind, w, r], n_recv.at[kind, w, r],
            device_id={"dp": sent_to[kind]}, device_id_type=MESH,
        )

    def go_near(kind, w, r):
        near(kind, w, r, sent_eighth).start()

    def landed(kind, w, r):
        near(kind, w, r, landed_eighth).wait_recv()

    shipped = []
    ring = so.shape[0]

    def ship(w, r, eighth):
        q = plane_at(r)
        n = sum(1 for v, _ in shipped if v == w)
        if w == 0:
            sq[q, eighth] = gq[q, eighth].astype(BF16)
            c = pltpu.make_async_copy(sq.at[q, eighth], wq_out.at[q, eighth], ship_sem.at[n])
        else:
            slot = n % ring
            if n >= ring:
                [c for v, c in shipped if v == 1][n - ring].wait()
            so[slot] = go[q, eighth].astype(BF16)
            c = pltpu.make_async_copy(so.at[slot], wo_out.at[q, eighth], o_sem.at[slot])
        c.start()
        shipped.append((w, c))

    def store_q(q, c, slot):
        at = pl.ds(c * BLOCK, BLOCK)
        return pltpu.make_async_copy(
            q_ring.at[slot], q_hbm.at[at, rows_at(q * cols_q, cols_q)], ring_sem.at[0, slot]
        )

    def store_mixed(q, c, slot):
        at = pl.ds(c * BLOCK, BLOCK)
        return pltpu.make_async_copy(
            mixed_ring.at[slot], mixed_hbm.at[at, rows_at(q * cols_q, cols_q)], ring_sem.at[1, slot]
        )

    def set_bias(c):
        first, count = key_window(c)
        bias_ref[pl.ds(0, count), :] = mask_bias(
            code_ref[pl.ds(FRONT + first, count), :], doc_ref[:, pl.ds(c * BLOCK, BLOCK)],
            first, count, c * BLOCK, BLOCK,
        )

    def attend_block(q, c, n):
        slot = lax.rem(n, 2) if not isinstance(n, int) else n % 2
        first, count = key_window(c)
        keys, at = pl.ds(FRONT + first, count), pl.ds(c * BLOCK, BLOCK)

        def free():
            store_q(q, c, slot).wait()
            store_mixed(q, c, slot).wait()

        if not isinstance(n, int) or n >= 2:
            free()
        w = sq[q].reshape(width, cols_q)
        q_ring[slot] = (project(normed[at, :], w) + bq_all[q]).astype(BF16)
        store_q(q, c, slot).start()
        for u in range(cols_q // hd):
            head = pl.ds(u * hd, hd)
            s = dot_t(kv_ref[keys, pl.ds(0, hd)], q_ring[slot, :, head]) * scale
            s = s + bias_ref[pl.ds(0, count), :]
            top = jnp.max(s, axis=0, keepdims=True)
            e = jnp.exp(s - top)
            total = jnp.sum(e, axis=0, keepdims=True)
            probs = (e * (1.0 / total)).astype(BF16)
            mixed_ring[slot, :, head] = project(vt[:, pl.ds(first, count)], probs).T.astype(BF16)
            lse_ref[pl.ds(q * (cols_q // hd) + u, 1), at] = top + jnp.log(total)
        store_mixed(q, c, slot).start()

    bands = w_down_hbm.shape[0] // down.shape[1]

    def load_cot(i):
        at = rows_at(lax.rem(i, blocks) * BLOCK, BLOCK)
        slot = lax.rem(i, 2)
        return pltpu.make_async_copy(cot_hbm.at[at], cot.at[slot], cot_sem.at[slot])

    def load_down(n):
        at = pl.ds(n * down.shape[1], down.shape[1])
        return pltpu.make_async_copy(w_down_hbm.at[at], down.at[n % 2], down_sem.at[n % 2])

    def store_d_acts(n, i):
        slot = lax.rem(i, 2)
        rows = rows_at(lax.rem(i, blocks) * BLOCK, BLOCK)
        cols = pl.ds(n * down.shape[1], down.shape[1])
        return pltpu.make_async_copy(
            d_acts.at[slot], d_acts_hbm.at[rows, cols], d_acts_sem.at[slot]
        )

    def d_acts_band(n):
        load_down(n).wait()
        if n + 1 < bands:
            load_down(n + 1).start()

        def one(i, carry):
            slot = lax.rem(i, 2)
            load_cot(i).wait()

            @pl.when(i + 1 < bands * blocks)
            def _():
                load_cot(i + 1).start()

            @pl.when(i >= 2)
            def _():
                store_d_acts(n, i).wait()

            d_acts[slot] = dot_t(cot[slot], down[n % 2])
            store_d_acts(n, i).start()
            return carry

        lax.fori_loop(n * blocks, (n + 1) * blocks, one, 0)

    def own_plane(c):
        set_bias(c)
        attend_block(m, c, c)

    def other_planes(c, first, end):
        if first == 1:
            set_bias(c)

        def one(r, carry):
            attend_block(lax.rem(m + r, planes), c, blocks + c * (planes - 1) + r - 1)
            return carry

        lax.fori_loop(first, end, one, 0)

    stream = [(w, r) for w in (0, 1) for r in range(3)]

    def pass_on(i):
        w, s = stream[i]

        @pl.when(is_mid)
        def _():
            z_land(w, s)
            z_forward(w, s)

        if i == 2:
            z_own(1)

    def from_line(i):
        w, s = stream[i]

        @pl.when(jnp.logical_not(is_mid))
        def _():
            z_land(w, s)

        for kind in (0, 1, 2):
            go_near(kind, w, s)
        ship(w, s, d)

    def from_near(i):
        w, s = stream[i]
        landed(0, w, s)
        go_near(5, w, s)
        go_near(3, w, s)
        ship(w, s, dx)
        landed(1, w, s)
        go_near(6, w, s)
        go_near(4, w, s)
        ship(w, s, dy)
        landed(2, w, s)
        ship(w, s, dc)

    def from_far(i):
        w, s = stream[i]
        landed(5, w, s)
        landed(6, w, s)
        go_near(7, w, s)
        ship(w, s, dxy)
        for kind in (3, 4):
            landed(kind, w, s)
            ship(w, s, landed_eighth[kind])
        landed(7, w, s)
        ship(w, s, landed_eighth[7])

    z_own(0)
    for r in (1, 2, 3):
        bias_copy(r, m).start()

    load_down(0).start()
    load_cot(0).start()
    loads[2].wait()

    def norm_strip(i, carry):
        at = rows_at(i * STRIP, STRIP)
        normed[at, :] = norm_rows(normed[at, :].astype(F32), gain_ref[...], shift_ref[...]).astype(BF16)
        return carry

    lax.fori_loop(0, seq // STRIP, norm_strip, 0)
    keep_normed = pltpu.make_async_copy(normed, normed_hbm, load_sem.at[2])
    keep_normed.start()
    kv_ref[pl.ds(0, FRONT), :] = jnp.zeros((FRONT, 2 * hd), BF16)
    kt_ref[:, pl.ds(0, FRONT)] = jnp.zeros((hd, FRONT), BF16)
    for c in range(blocks):
        at, put = pl.ds(c * BLOCK, BLOCK), pl.ds(FRONT + c * BLOCK, BLOCK)
        kv = project(normed[at, :], w_kv[...])
        keys, values = kv[:, :hd], kv[:, hd:] + bv_ref[...]
        kv_ref[put, pl.ds(0, hd)] = keys.astype(BF16)
        kv_ref[put, pl.ds(hd, hd)] = values.astype(BF16)
        kt_ref[:, put] = keys.T.astype(BF16)
        vt[:, at] = values.T.astype(BF16)
    loads[3].wait()

    def stage(s):
        if s == 0:
            pass_on(0)
        if s + 1 < len(stream):
            pass_on(s + 1)
        if s < len(stream):
            from_line(s)
        if 1 <= s <= len(stream):
            from_near(s - 1)
        if s >= 2:
            from_far(s - 2)

    stage(0)
    own_plane(0)
    own_plane(1)
    stage(1)
    own_plane(2)
    own_plane(3)
    stage(2)
    for n in range(bands // 2):
        d_acts_band(n)
    stage(3)
    for n in range(bands // 2, bands):
        d_acts_band(n)
    for r in (1, 2, 3):
        bias_copy(r, mp_partner(m, r)).wait_recv()
    stage(4)
    other_planes(0, 1, planes)
    other_planes(1, 1, planes)
    from_line(5)
    other_planes(2, 1, 2)
    from_near(4)
    other_planes(2, 2, planes)
    from_far(3)
    other_planes(3, 1, 2)
    from_near(5)
    other_planes(3, 2, planes)
    from_far(4)
    from_far(5)

    for i in (0, 1):
        store_d_acts(0, i).wait()
    for slot in (0, 1):
        store_q(m, 0, slot).wait()
        store_mixed(m, 0, slot).wait()
    for w in (0, 1):
        z_own(w, wait=True)
    for w, r in stream:
        z_forward(w, r, wait=True)
        for kind in range(8):
            near(kind, w, r, sent_eighth).wait_send()
    for r in (1, 2, 3):
        bias_copy(r, m).wait_send()
    rows_o = [c for v, c in shipped if v == 1]
    for c in [c for v, c in shipped if v == 0] + rows_o[-ring:]:
        c.wait()
    keep_normed.wait()
    loads[4].wait()
    loads[5].wait()


def gather_by_sum(shard):
    blank = jnp.zeros((lax.axis_size("mp"),) + shard.shape, F32)
    half = shard.astype(F32) * 0.5
    own = lax.dynamic_update_index_in_dim(blank, half, lax.axis_index("mp"), 0)
    return lax.psum(own, "mp") * 2.0


def attention_front(
    inputs, w_query, b_query, w_keyval, b_value, w_out, gain, shift, code_col, doc_row, cotangent, w_down
):
    dp, mp = lax.axis_size("dp"), lax.axis_size("mp")
    width, cols = w_query.shape
    rows = w_out.shape[0]
    seq = inputs.shape[0]
    hd = w_keyval.shape[1] // 2
    if (dp, mp) != (8, 4):
        all_query, all_out, all_bias = (
            gather_by_sum(a).astype(a.dtype) for a in (w_query, w_out, b_query)
        )
        normed = norm_rows(inputs.astype(F32), gain, shift).astype(BF16)
        kv_bias = jnp.concatenate([jnp.zeros((hd,), F32), b_value])
        keyval = (project(normed, w_keyval) + kv_bias).astype(BF16)
        queries = jnp.concatenate(
            [project(normed, all_query[i]) + all_bias[i] for i in range(mp)], 1
        ).astype(BF16)
        mixed, lse = attend(queries, keyval, code_col[FRONT:], doc_row)
        keyval = jnp.pad(keyval, ((FRONT, 0), (0, 0)))
        keys_t = keyval[:, :hd].T
        d_acts = jnp.einsum("td,fd->tf", cotangent, w_down, preferred_element_type=F32)
        return all_query, all_out.reshape(-1, width), normed, queries, mixed, d_acts, keyval, keys_t, lse
    wq = w_query.reshape(dp, width // dp, cols)
    wo = w_out.reshape(dp, rows // dp, width)
    dma = pltpu.SemaphoreType.DMA
    vmem = pl.BlockSpec(memory_space=pltpu.VMEM)
    full_q, full_o = (mp,) + wq.shape, (mp,) + wo.shape
    heads = mp * cols // hd
    shape = jax.ShapeDtypeStruct
    out_q, out_o, normed, queries, mixed, d_acts, keyval, keys_t, lse = pl.pallas_call(
        functools.partial(front_kernel, heads),
        out_shape=(
            shape(full_q, BF16),
            shape(full_o, BF16),
            shape((seq, width), BF16),
            shape((seq, mp * cols), BF16),
            shape((seq, mp * cols), BF16),
            shape((seq, w_down.shape[0]), F32),
            shape((FRONT + seq, 2 * hd), BF16),
            shape((hd, FRONT + seq), BF16),
            shape((heads, seq), F32),
        ),
        in_specs=[HBM] * 5 + [vmem] * 7,
        out_specs=(HBM,) * 6 + (vmem,) * 3,
        scratch_shapes=[
            pltpu.VMEM(wq.shape[1:], BF16),
            pltpu.VMEM(wo.shape[1:], BF16),
            pltpu.VMEM(full_q, F32),
            pltpu.VMEM(full_o, F32),
            pltpu.VMEM(full_q, BF16),
            pltpu.VMEM((4,) + wo.shape[1:], BF16),
            pltpu.VMEM((seq, width), BF16),
            pltpu.VMEM((2, BLOCK, cols), BF16),
            pltpu.VMEM((2, BLOCK, cols), BF16),
            pltpu.VMEM((hd, seq), BF16),
            pltpu.VMEM((REACH * BLOCK, BLOCK), F32),
            pltpu.VMEM((mp, 1, cols), F32),
            pltpu.VMEM((2, BLOCK, width), BF16),
            pltpu.VMEM((2, COLS, width), BF16),
            pltpu.VMEM((2, BLOCK, COLS), F32),
            dma((6,)),
            dma((2,)),
            dma((2,)),
            dma((2,)),
            dma((3 * dp,)),
            dma((4,)),
            dma((2, 2)),
            dma((2, 5)),
            dma((2, mp)),
            dma((3,)),
            dma((3,)),
            dma((8, 2, 3)),
            dma((8, 2, 3)),
        ],
        compiler_params=pltpu.CompilerParams(
            collective_id=0, has_side_effects=True, vmem_limit_bytes=VMEM_LIMIT
        ),
        name="attention_front",
    )(
        wq, wo, inputs, cotangent, w_down, b_query.reshape(1, cols), w_keyval, gain.reshape(1, width),
        shift.reshape(1, width), b_value.reshape(1, hd), code_col, doc_row,
    )
    return (
        out_q.reshape(mp, width, cols), out_o.reshape(mp * rows, width),
        normed, queries, mixed, d_acts, keyval, keys_t, lse,
    )


PIECE = 32
SLOT = 1
CROSS_LATE = 2 * SLOT
LATE = 5 * SLOT
AHEAD = 3 * SLOT


class LineSum:
    scratch = staticmethod(
        lambda rows, pieces, width: [pltpu.VMEM((rows, width), F32)] * 3
        + [pltpu.SemaphoreType.DMA((pieces,))] * 5
    )

    def __init__(self, refs):
        self.part, self.total, self.cross, *sems = refs
        self.in_send, self.in_recv, self.over_send, self.over_recv, self.out_send = sems
        self.slots = self.part.shape[0] // PIECE
        self.pieces = self.in_send.shape[0]
        m = lax.axis_index("mp")
        self.is_end = (m == 0) | (m == 3)
        self.is_mid = (m == 1) | (m == 2)
        self.buddy = {"mp": mp_partner(m, 1)}
        self.across = {"mp": 3 - m}

    def greet(self, others=()):
        bar = pltpu.get_barrier_semaphore()
        pl.semaphore_signal(bar, inc=1, device_id=self.buddy, device_id_type=MESH)
        for other in others:
            pl.semaphore_signal(bar, inc=1, device_id=other, device_id_type=MESH)

        @pl.when(self.is_mid)
        def _():
            pl.semaphore_signal(bar, inc=1, device_id=self.across, device_id_type=MESH)

    def meet(self, others=()):
        bar = pltpu.get_barrier_semaphore()

        @pl.when(self.is_end)
        def _():
            pl.semaphore_wait(bar, 1 + len(others))

        @pl.when(self.is_mid)
        def _():
            pl.semaphore_wait(bar, 2 + len(others))

    def at(self, k):
        slot = k if self.slots == self.pieces else k % self.slots
        return rows_at(slot * PIECE, PIECE)

    def inward(self, k):
        at = self.at(k)
        return pltpu.make_async_remote_copy(
            self.part.at[at], self.total.at[at], self.in_send.at[k], self.in_recv.at[k],
            device_id=self.buddy, device_id_type=MESH,
        )

    def over(self, k):
        at = self.at(k)
        return pltpu.make_async_remote_copy(
            self.part.at[at], self.cross.at[at], self.over_send.at[k], self.over_recv.at[k],
            device_id=self.across, device_id_type=MESH,
        )

    def outward(self, k):
        at = self.at(k)
        return pltpu.make_async_remote_copy(
            self.total.at[at], self.total.at[at], self.out_send.at[k], self.in_recv.at[k],
            device_id=self.buddy, device_id_type=MESH,
        )

    def slot(self, i):
        for j in range(SLOT):
            self.tick(i * SLOT + j)

    def tick(self, k):
        n = self.pieces

        @pl.when(self.is_end)
        def _():
            @pl.when(k < n)
            def _():
                @pl.when(k >= AHEAD)
                def _():
                    self.inward(k - AHEAD).wait_send()

                self.inward(k).start()

            @pl.when((k >= LATE) & (k < n + LATE))
            def _():
                self.outward(k - LATE).wait_recv()

        @pl.when(self.is_mid)
        def _():
            @pl.when(k < n)
            def _():
                at = self.at(k)
                self.inward(k).wait_recv()
                self.part[at, :] += self.total[at, :]
                self.over(k).start()

            @pl.when((k >= CROSS_LATE) & (k < n + CROSS_LATE))
            def _():
                j = k - CROSS_LATE
                at = self.at(j)
                self.over(j).wait_recv()
                self.total[at, :] = self.part[at, :] + self.cross[at, :]
                self.outward(j).start()

    def free(self, first, count):
        @pl.when(self.is_mid)
        def _():
            def sent(k, c):
                self.over(k).wait_send()
                self.outward(k).wait_send()
                return c

            lax.fori_loop(first, first + count, sent, 0)

    def finish(self, freed=0):
        n = self.pieces

        @pl.when(self.is_end)
        def _():
            for k in range(n - AHEAD, n):
                self.inward(k).wait_send()

        self.free(freed, n - freed)


def attend_kernel(seq, heads, q_ref, kv_ref, vt_ref, code_ref, doc_ref, mixed_ref, lse_ref, bias_ref):
    hd = vt_ref.shape[0]
    scale = 1.0 / math.sqrt(hd)
    for c in range(seq // BLOCK):

        @pl.when(pl.program_id(0) == c)
        def _(c=c):
            first, count = key_window(c)
            keys = pl.ds(first, count)
            bias_ref[pl.ds(0, count), :] = mask_bias(
                code_ref[keys, :], doc_ref[...], first, count, c * BLOCK, BLOCK
            )

            def some_heads(g, carry):
                for u in range(GROUP):
                    h = g * GROUP + u
                    cols = pl.ds(pl.multiple_of(h * hd, hd), hd)
                    s = dot_t(kv_ref[keys, pl.ds(0, hd)], q_ref[:, cols]) * scale
                    s = s + bias_ref[pl.ds(0, count), :]
                    top = jnp.max(s, axis=0, keepdims=True)
                    e = jnp.exp(s - top)
                    total = jnp.sum(e, axis=0, keepdims=True)
                    probs = (e * (1.0 / total)).astype(BF16)
                    mixed = project(vt_ref[:, keys], probs)
                    mixed_ref[:, cols] = mixed.T.astype(BF16)
                    lse_ref[pl.ds(h, 1), :] = top + jnp.log(total)
                return carry

            lax.fori_loop(0, heads // GROUP, some_heads, 0)


def attend(queries, keyval, code_col, doc_row):
    seq, width = queries.shape
    hd = keyval.shape[1] // 2
    heads = width // hd
    values_t = keyval[:, hd:].T
    whole = lambda *shape: pl.BlockSpec(shape, lambda c: (0,) * len(shape))
    return pl.pallas_call(
        functools.partial(attend_kernel, seq, heads),
        grid=(seq // BLOCK,),
        out_shape=(
            jax.ShapeDtypeStruct((seq, width), BF16),
            jax.ShapeDtypeStruct((heads, seq), F32),
        ),
        in_specs=[
            pl.BlockSpec((BLOCK, width), lambda c: (c, 0)),
            whole(seq, 2 * hd),
            whole(hd, seq),
            whole(seq, 1),
            pl.BlockSpec((1, BLOCK), lambda c: (0, c)),
        ],
        out_specs=(
            pl.BlockSpec((BLOCK, width), lambda c: (c, 0)),
            pl.BlockSpec((heads, BLOCK), lambda c: (0, c)),
        ),
        scratch_shapes=[pltpu.VMEM((REACH * BLOCK, BLOCK), F32)],
        compiler_params=pltpu.CompilerParams(vmem_limit_bytes=VMEM_LIMIT),
        name="attend",
    )(queries, keyval, values_t, code_col, doc_row)


def norm_back_rows(x, grad, gain):
    mean = jnp.mean(x, axis=-1, keepdims=True)
    center = x - mean
    scale = lax.rsqrt(jnp.mean(center * center, axis=-1, keepdims=True) + EPS)
    xhat = center * scale
    e = grad * gain
    weighted = grad * xhat
    d_in = scale * (
        e - jnp.mean(e, axis=-1, keepdims=True) - xhat * jnp.mean(e * xhat, axis=-1, keepdims=True)
    )
    return d_in, weighted


def dot_down(a, b):
    return lax.dot_general(a, b, (((0,), (0,)), ((), ())), preferred_element_type=F32)


def fold_rows(x):
    return jnp.sum(x.reshape(-1, 8, x.shape[-1]), axis=0)


FEED_EARLY = 2

GELU_A = math.sqrt(2.0 / math.pi)
GELU_B = 0.044715


def gelu_pair(u):
    square = u * u
    t = jnp.tanh(u * (GELU_A + GELU_A * GELU_B * square))
    cdf = 0.5 * (1.0 + t)
    slope = cdf + 0.5 * u * (1.0 - t * t) * (GELU_A + 3.0 * GELU_A * GELU_B * square)
    return u * cdf, slope


def mlp_kernel(
    mixed_hbm, w_out_hbm, in_hbm, w_up_hbm, d_acts_hbm, cot_hbm,
    b_out_ref, gain_ref, shift_ref, b_up_ref,
    mid_hbm, acts_hbm, dh_hbm, down_hbm, up_hbm, first_hbm, next_hbm, b_up_sum,
    w_out, w_up, normed, acts, dh, cot, mixed, xs, mid, d_acts, turned, tiles,
    load_sem, out_sem, tile_sem, *line_refs,
):
    line = LineSum(line_refs)
    seq, width = normed.shape
    blocks = seq // BLOCK
    hidden = w_up.shape[1]

    def load(i, src, dst):
        return pltpu.make_async_copy(src, dst, load_sem.at[i])

    def load_block(c):
        at = pl.ds(c * BLOCK, BLOCK)
        return [
            load(2, mixed_hbm.at[at], mixed),
            load(3, in_hbm.at[at], xs),
        ]

    def load_d_acts(c):
        return load(4, d_acts_hbm.at[pl.ds(c * BLOCK, BLOCK)], d_acts)

    def store_mid(c):
        return pltpu.make_async_copy(mid, mid_hbm.at[pl.ds(c * BLOCK, BLOCK)], out_sem.at[0])

    store_acts = pltpu.make_async_copy(acts, acts_hbm, out_sem.at[1])
    store_dh = pltpu.make_async_copy(dh, dh_hbm, out_sem.at[2])

    load(0, w_out_hbm, w_out).start()
    for i in load_block(0):
        i.start()
    load(1, w_up_hbm, w_up).start()
    load_d_acts(0).start()
    load(5, cot_hbm, cot).start()
    line.greet()
    b_up_sum[...] = jnp.zeros_like(b_up_sum)

    def middle_step(c):
        for i in load_block(c):
            i.wait()
        if c >= 1:
            store_mid(c - 1).wait()

        def cols(n, carry):
            there = rows_at(n * COLS, COLS)
            mid[:, there] = (
                project(mixed[...], w_out[:, there]) + xs[:, there].astype(F32) + b_out_ref[:, there]
            )
            return carry

        lax.fori_loop(0, width // COLS, cols, 0)
        store_mid(c).start()
        if c + 1 < blocks:
            for i in load_block(c + 1):
                i.start()

    def norm_step(c):
        def strip(i, carry):
            at = rows_at(i * STRIP, STRIP)
            put = rows_at(c * BLOCK + i * STRIP, STRIP)
            normed[put, :] = norm_rows(mid[at, :], gain_ref[...], shift_ref[...]).astype(BF16)
            return carry

        lax.fori_loop(0, BLOCK // STRIP, strip, 0)

    def hidden_step(c):
        at = pl.ds(c * BLOCK, BLOCK)
        load_d_acts(c).wait()

        def cols(n, carry):
            there = rows_at(n * COLS, COLS)
            u = project(normed[at, :], w_up[:, there]) + b_up_ref[:, there]
            value, slope = gelu_pair(u)
            acts[at, there] = value.astype(BF16)
            low = (d_acts[:, there] * slope).astype(BF16)
            dh[at, there] = low
            b_up_sum[:, there] += fold_rows(low.astype(F32))
            return carry

        lax.fori_loop(0, hidden // COLS, cols, 0)
        if c + 1 < blocks:
            load_d_acts(c + 1).start()
        else:
            store_acts.start()
            store_dh.start()

    def produce(c, part):
        def cols(n, carry):
            there = rows_at(n * COLS, COLS)
            part[:, there] = dot_t(dh[pl.ds(c * BLOCK, BLOCK), :], w_up[there, :])
            return carry

        lax.fori_loop(0, width // COLS, cols, 0)

    store_next = pltpu.make_async_copy(mid, next_hbm, out_sem.at[0])

    def produce_next():
        store_mid(blocks - 1).wait()
        produce(1, mid)
        store_next.start()

    tile_rows, tile_cols = tiles.shape[1:]
    tile_list = []
    for left, right, out in ((acts, cot, down_hbm), (normed, dh, up_hbm)):
        for row in range(0, left.shape[1], tile_rows):
            for col in range(0, right.shape[1], tile_cols):
                tile_list.append((left, right, out, row, col))

    def store_tile(i):
        _, _, out, row, col = tile_list[i]
        return pltpu.make_async_copy(
            tiles.at[i % 2], out.at[pl.ds(row, tile_rows), pl.ds(col, tile_cols)], tile_sem.at[i % 2]
        )

    def tile_step(i):
        left, right, _, row, col = tile_list[i]
        if col == 0:
            turned[...] = left[:, pl.ds(row, tile_rows)].T
        if i >= 2:
            store_tile(i - 2).wait()

        def cols(n, carry):
            there, put = rows_at(col + n * COLS, COLS), rows_at(n * COLS, COLS)
            tiles[i % 2, :, put] = project(turned[...], right[:, there])
            return carry

        lax.fori_loop(0, tile_cols // COLS, cols, 0)
        store_tile(i).start()

    load(0, w_out_hbm, w_out).wait()
    middle_step(0)
    norm_step(0)
    load(1, w_up_hbm, w_up).wait()
    hidden_step(0)
    produce(0, line.part)
    line.meet()
    load(5, cot_hbm, cot).wait()
    steps = []
    for c in range(1, blocks):
        steps.append([functools.partial(f, c) for f in (middle_step, norm_step)])
        steps.append([functools.partial(hidden_step, c)])
    steps[-1].append(produce_next)
    slots = (line.pieces + LATE) // SLOT
    count = len(tile_list)
    per = -(-count // max(slots - len(steps), 1))
    for i in range(0, count, per):
        steps.append([functools.partial(tile_step, j) for j in range(i, min(i + per, count))])
    for i in range(max(slots, len(steps))):
        if i < slots:
            line.slot(i)
        if i < len(steps):
            for step in steps[i]:
                step()
    store_first = pltpu.make_async_copy(line.total, first_hbm, out_sem.at[3])
    store_first.start()
    store_tile(count - 2).wait()
    store_tile(count - 1).wait()
    store_next.wait()
    store_acts.wait()
    store_dh.wait()
    store_first.wait()
    line.finish()


def mlp(mixed, w_out, inputs, w_up, d_acts, cotangent, b_out, gain, shift, b_up):
    seq, width = inputs.shape
    hidden = w_up.shape[1]
    vmem = pl.BlockSpec(memory_space=pltpu.VMEM)
    dma = pltpu.SemaphoreType.DMA
    shape = jax.ShapeDtypeStruct
    block = lambda cols, dtype: pltpu.VMEM((BLOCK, cols), dtype)
    return pl.pallas_call(
        mlp_kernel,
        out_shape=(
            shape((seq, width), F32),
            shape((seq, hidden), BF16),
            shape((seq, hidden), BF16),
            shape((hidden, width), F32),
            shape((width, hidden), F32),
            shape((BLOCK, width), F32),
            shape((BLOCK, width), F32),
            shape((8, hidden), F32),
        ),
        in_specs=[HBM] * 6 + [vmem] * 4,
        out_specs=(HBM,) * 7 + (vmem,),
        scratch_shapes=[
            pltpu.VMEM(w_out.shape, BF16),
            pltpu.VMEM(w_up.shape, BF16),
            pltpu.VMEM((seq, width), BF16),
            pltpu.VMEM((seq, hidden), BF16),
            pltpu.VMEM((seq, hidden), BF16),
            pltpu.VMEM((seq, width), BF16),
            block(w_out.shape[0], BF16),
            block(width, BF16),
            block(width, F32),
            block(hidden, F32),
            pltpu.VMEM((2 * BLOCK, seq), BF16),
            pltpu.VMEM((2, 2 * BLOCK, width // 2), F32),
            dma((6,)),
            dma((4,)),
            dma((2,)),
        ]
        + LineSum.scratch(BLOCK, BLOCK // PIECE, width),
        compiler_params=pltpu.CompilerParams(
            collective_id=3, has_side_effects=True, vmem_limit_bytes=VMEM_LIMIT
        ),
        cost_estimate=pl.CostEstimate(flops=60 * 10**9, bytes_accessed=2**26, transcendentals=0),
        name="mlp",
    )(
        mixed, w_out, inputs, w_up, d_acts, cotangent, b_out.reshape(1, width),
        gain.reshape(1, width), shift.reshape(1, width), b_up.reshape(1, hidden),
    )


def mlp_attend_back_kernel(
    heads,
    dh_hbm, w_up_hbm, w_out_hbm, mid_hbm, cot_hbm, q_hbm, acts_hbm, w_down_hbm, normed_hbm, mixed_hbm,
    first_hbm, second_hbm,
    kv_ref, kt_ref, code_ref, doc_ref, lse_ref, gain_ref, b_down_ref,
    d_mid_hbm, dq_hbm, feed_out, feed_next, grads_hbm, dkv_ref, sums_ref,
    w_up, w_out, dh, mid, cot, q, normed, mixed, d_branch, d_mixed, dq, grads, bias_ref,
    load_sem, out_sem, *line_refs,
):
    line = LineSum(line_refs)
    seq, width = q_hbm.shape
    m = lax.axis_index("mp")
    own_cols = mixed.shape[1]
    own = rows_at(m * own_cols, own_cols)
    ring = line.part.shape[0] // BLOCK
    hd = kt_ref.shape[0]
    chunks = seq // BLOCK
    slots = BLOCK // (PIECE * SLOT)
    count = REACH * BLOCK
    scale = 1.0 / math.sqrt(hd)

    def load(i, src, dst):
        return pltpu.make_async_copy(src, dst, load_sem.at[i])

    def load_dh(b):
        return load(2, dh_hbm.at[rows_at((b + 1) * BLOCK, BLOCK)], dh)

    def load_chunk(c):
        at = rows_at(c * BLOCK, BLOCK)
        return [
            load(3, mid_hbm.at[at], mid),
            load(4, cot_hbm.at[at], cot),
            load(5, q_hbm.at[at], q),
            load(6, normed_hbm.at[at], normed),
            load(7, mixed_hbm.at[at, own], mixed),
        ]

    def block_at(b):
        return rows_at((b % ring) * BLOCK, BLOCK)

    load_first = load(8, first_hbm, line.total.at[block_at(ring - 1)])

    def store(i, src, dst, c):
        return pltpu.make_async_copy(src, dst.at[rows_at(c * BLOCK, BLOCK)], out_sem.at[i])

    def stores(c, which=(0, 1)):
        pairs = ((mid, d_mid_hbm), (dq, dq_hbm))
        return [store(i, *pairs[i], c) for i in which]

    load_second = load(9, second_hbm, line.part.at[block_at(0)])
    load_second.start()
    load(0, w_up_hbm, w_up).start()
    load_dh(1).start()
    load(1, w_out_hbm, w_out).start()
    load_first.start()
    load_down = load(0, w_down_hbm, w_up)

    def load_acts(j):
        return load(2, acts_hbm.at[rows_at(j * BLOCK, BLOCK)], dh)

    def load_mid(j):
        return load(3, mid_hbm.at[rows_at(j * BLOCK, BLOCK)], mid)

    line.greet()
    dkv_ref[...] = jnp.zeros_like(dkv_ref)
    sums_ref[...] = jnp.zeros_like(sums_ref)
    grads[...] = jnp.zeros_like(grads)

    lines = chunks - 1

    def produce(b):
        at = block_at(b)
        load_dh(b).wait()

        def cols(n, carry):
            there = rows_at(n * COLS, COLS)
            line.part[at, there] = dot_t(dh[...], w_up[there, :])
            return carry

        lax.fori_loop(0, width // COLS, cols, 0)

        @pl.when(b + 1 < lines)
        def _():
            load_dh(b + 1).start()

        @pl.when(b + 1 == lines)
        def _():
            load_acts(0).start()
            load_down.start()

    def produce_feed(j):
        at = block_at(lines + j)
        load_acts(j).wait()
        load_mid(j).wait()

        @pl.when(j == 0)
        def _():
            load_down.wait()

        def cols(n, carry):
            there = rows_at(n * COLS, COLS)
            line.part[at, there] = project(dh[...], w_up[:, there])
            return carry

        lax.fori_loop(0, width // COLS, cols, 0)

        @pl.when(m == 0)
        def _():
            line.part[at, :] += mid[...]

        load_acts(j + 1).start()

    def add_grads(first, left, right):
        at = pl.ds(first, own_cols)

        def cols(n, carry):
            there = rows_at(n * COLS, COLS)
            grads[at, there] += dot_down(left, right[:, there])
            return carry

        lax.fori_loop(0, width // COLS, cols, 0)

    def norm_step(c, half):
        def strip(i, carry):
            row = half * (BLOCK // 2) + i * STRIP
            at = rows_at(row, STRIP)
            grad = line.total[rows_at(((c + ring - 1) % ring) * BLOCK + row, STRIP), :]
            d_in, weighted = norm_back_rows(mid[at, :], grad, gain_ref[...])
            cot_rows = cot[at, :].astype(F32)
            d_mid = cot_rows + d_in
            low = d_mid.astype(BF16)
            mid[at, :] = d_mid
            d_branch[at, :] = low
            sums_ref[0] += fold_rows(weighted)
            sums_ref[1] += fold_rows(grad)
            sums_ref[2] += fold_rows(low.astype(F32))
            sums_ref[3] += fold_rows(cot_rows)
            return carry

        lax.fori_loop(0, BLOCK // 2 // STRIP, strip, 0)

    def mixed_step(c):
        def cols(n, carry):
            there = rows_at(n * COLS, COLS)
            d_mixed[:, there] = dot_t(d_branch[...], w_out[there, :]).astype(BF16)
            return carry

        lax.fori_loop(0, width // COLS, cols, 0)
        keys = pl.ds(pl.multiple_of(c * BLOCK, BLOCK), count)
        bias_ref[...] = mask_bias(
            code_ref[keys, :], doc_ref[:, rows_at(c * BLOCK, BLOCK)],
            (c - REACH + 1) * BLOCK, count, c * BLOCK, BLOCK,
        )

    def heads_step(c, g):
        keys = pl.ds(pl.multiple_of(c * BLOCK, BLOCK), count)
        queries = rows_at(c * BLOCK, BLOCK)
        dk = jnp.zeros((count, hd), F32)
        dv = jnp.zeros((count, hd), F32)
        for u in range(GROUP):
            h = g * GROUP + u
            cols = rows_at(h * hd, hd)
            qh = q[:, cols]
            dm = d_mixed[:, cols]
            s = dot_t(kv_ref[keys, pl.ds(0, hd)], qh) * scale + bias_ref[...]
            probs = jnp.exp(s - lse_ref[pl.ds(h, 1), queries])
            d_probs = dot_t(kv_ref[keys, pl.ds(hd, hd)], dm)
            t = probs * d_probs
            inner = jnp.sum(t, axis=0, keepdims=True)
            ds = (t - probs * inner).astype(BF16)
            dqh = project(kt_ref[:, keys], ds) * scale
            dq[:, cols] = dqh.T.astype(BF16)
            dk = dk + project(ds, qh)
            dv = dv + project(probs.astype(BF16), dm)
        dkv_ref[keys, pl.ds(0, hd)] += dk * scale
        dkv_ref[keys, pl.ds(hd, hd)] += dv

    load_second.wait()
    line.meet()
    for k in range(3):
        line.slot(k)
    load(0, w_up_hbm, w_up).wait()
    load(1, w_out_hbm, w_out).wait()
    load_first.wait()

    def cycle(c, carry):
        base = c * slots + 3

        @pl.when(c >= 1)
        def _():
            for i in stores(c - 1):
                i.wait()

        @pl.when(c + 1 >= lines)
        def _():
            load_mid(c + 1 - lines).start()

        line.slot(base)

        @pl.when(c >= 2)
        def _():
            line.free((c - 2) * (BLOCK // PIECE), BLOCK // PIECE)

        @pl.when(c + 1 < lines)
        def _():
            produce(c + 1)

        @pl.when(c + 1 >= lines)
        def _():
            produce_feed(c + 1 - lines)

        for i in load_chunk(c):
            i.start()
        line.slot(base + 1)
        for i in load_chunk(c):
            i.wait()
        norm_step(c, 0)
        line.slot(base + 2)
        norm_step(c, 1)
        stores(c, (0,))[0].start()
        line.slot(base + 3)
        mixed_step(c)
        add_grads(own_cols, mixed[...], d_branch)

        def some_heads(g, carry):
            line.slot(base + 4 + g)
            heads_step(c, g)
            return carry

        lax.fori_loop(0, heads // GROUP, some_heads, 0)
        stores(c, (1,))[0].start()
        add_grads(0, dq[:, own], normed)

        def strip(i, carry):
            sums_ref[4] += fold_rows(dq[rows_at(i * STRIP, STRIP), :].astype(F32))
            return carry

        lax.fori_loop(0, BLOCK // STRIP, strip, 0)
        return carry

    lax.fori_loop(0, chunks, cycle, 0)
    keep_grads = pltpu.make_async_copy(grads, grads_hbm, out_sem.at[3])
    keep_grads.start()

    stores(chunks - 1, (0,))[0].wait()
    load_mid(FEED_EARLY).start()
    load_acts(FEED_EARLY).wait()
    load_mid(FEED_EARLY).wait()
    share = jnp.where(m == 0, 1.0, 0.0)

    def next_cols(n, carry):
        there = rows_at(n * COLS, COLS)
        mid[:, there] = project(dh[...], w_up[:, there]) + mid[:, there] * share
        return carry

    lax.fori_loop(0, width // COLS, next_cols, 0)
    keep_next = pltpu.make_async_copy(mid, feed_next, out_sem.at[2])
    keep_next.start()
    for k in range(chunks * slots + 3, (line.pieces + LATE) // SLOT):
        line.slot(k)
    keep_next.wait()
    stores(chunks - 1, (1,))[0].wait()
    keep_feed = []
    for j, low in enumerate((d_branch, d_mixed)):

        def strip(i, carry, j=j, low=low):
            total = line.total[rows_at((lines + j) % ring * BLOCK + i * STRIP, STRIP), :]
            low[rows_at(i * STRIP, STRIP), :] = (total + b_down_ref[...]).astype(BF16)
            return carry

        lax.fori_loop(0, BLOCK // STRIP, strip, 0)
        keep_feed.append(
            pltpu.make_async_copy(low, feed_out.at[pl.ds(j * BLOCK, BLOCK)], out_sem.at[j])
        )
        keep_feed[j].start()
    for i in keep_feed:
        i.wait()
    keep_grads.wait()
    line.finish((lines - 1) * (BLOCK // PIECE))


def mlp_attend_back(
    d_hidden, w_up, w_out, middle, cotangent, queries, acts, w_down, normed, mixed, first, second, own_cols,
    keyval, keys_t, code_col, doc_row, lse, gain, b_down,
):
    seq, width = queries.shape
    heads = width // keys_t.shape[0]
    vmem = pl.BlockSpec(memory_space=pltpu.VMEM)
    dma = pltpu.SemaphoreType.DMA
    block = lambda dtype: pltpu.VMEM((BLOCK, width), dtype)
    return pl.pallas_call(
        functools.partial(mlp_attend_back_kernel, heads),
        out_shape=(
            jax.ShapeDtypeStruct((seq, width), F32),
            jax.ShapeDtypeStruct((seq, width), BF16),
            jax.ShapeDtypeStruct((FEED_EARLY * BLOCK, width), BF16),
            jax.ShapeDtypeStruct((BLOCK, width), F32),
            jax.ShapeDtypeStruct((2 * own_cols, width), F32),
            jax.ShapeDtypeStruct(keyval.shape, F32),
            jax.ShapeDtypeStruct((5, 8, width), F32),
        ),
        in_specs=[HBM] * 12 + [vmem] * 7,
        out_specs=(HBM, HBM, HBM, HBM, HBM, vmem, vmem),
        scratch_shapes=[
            pltpu.VMEM(w_up.shape, BF16),
            pltpu.VMEM(w_out.shape, BF16),
            pltpu.VMEM((BLOCK, d_hidden.shape[1]), BF16),
            block(F32),
            block(BF16),
            block(BF16),
            block(BF16),
            pltpu.VMEM((BLOCK, own_cols), BF16),
            block(BF16),
            block(BF16),
            block(BF16),
            pltpu.VMEM((2 * own_cols, width), F32),
            pltpu.VMEM((REACH * BLOCK, BLOCK), F32),
            dma((10,)),
            dma((4,)),
        ]
        + LineSum.scratch(seq - BLOCK, (seq + (FEED_EARLY - 1) * BLOCK) // PIECE, width),
        compiler_params=pltpu.CompilerParams(
            collective_id=1, has_side_effects=True, vmem_limit_bytes=VMEM_LIMIT
        ),
        cost_estimate=pl.CostEstimate(
            flops=200 * 10**9, bytes_accessed=2**25, transcendentals=0
        ),
        name="mlp_attend_back",
    )(
        d_hidden, w_up, w_out, middle, cotangent, queries, acts, w_down, normed, mixed, first, second,
        keyval, keys_t, code_col, doc_row, lse, gain.reshape(1, width), b_down.reshape(1, width),
    )


def feed_kernel(
    rounds,
    acts_hbm, w_down_hbm, mid_hbm, dq_hbm, w_q_hbm, in_hbm, d_mid_hbm, normed_hbm, next_hbm,
    dkv_f_ref, w_kv_ref, gain_ref, bias_ref, sums_in, b_up_in,
    out_hbm, in_grad_hbm, table_out, vectors_out,
    w_down, w_q, acts, mid, dq, xs, d_mid, spread, low, in_grad, normed, dkv_ref, sums, trade, trade_in, table, table_in, table_all, turned,
    load_sem, out_sem, t_send, t_recv, h_send, h_recv, d_send, d_recv, *line_refs,
):
    line = LineSum(line_refs)
    rows, width = line.part.shape
    seq = rows + FEED_EARLY * BLOCK
    blocks = seq // BLOCK
    chunks = rows // BLOCK
    slots = BLOCK // (PIECE * SLOT)
    planes, _, cols_q = w_q.shape
    m = lax.axis_index("mp")
    d = lax.axis_index("dp")
    peers = [{"dp": flip_bit(d, 1 << r)} for r in range(rounds)]

    def load(i, src, dst):
        return pltpu.make_async_copy(src, dst, load_sem.at[i])

    def load_feed(c):
        at = rows_at((c + FEED_EARLY) * BLOCK, BLOCK)
        return [load(2, acts_hbm.at[at], acts), load(3, mid_hbm.at[at], mid)]

    def load_grad(c):
        at = rows_at(c * BLOCK, BLOCK)
        return [
            load(4, dq_hbm.at[at], dq),
            load(5, in_hbm.at[at], xs),
            load(6, d_mid_hbm.at[at], d_mid),
        ]

    def store(i, src, dst, c):
        return pltpu.make_async_copy(src, dst.at[rows_at(c * BLOCK, BLOCK)], out_sem.at[i])

    def load_normed(c):
        return load(7, normed_hbm.at[rows_at(c * BLOCK, BLOCK)], normed)

    load_next = load(8, next_hbm, line.part.at[pl.ds(0, BLOCK)])
    load_next.start()
    load(0, w_down_hbm, w_down).start()
    if chunks > 1:
        for i in load_feed(1):
            i.start()
    load_normed(0).start()
    load(1, w_q_hbm, w_q).start()
    for i in load_grad(0):
        i.start()
    line.greet(peers)
    sums[...] = jnp.zeros_like(sums)
    dkv_ref[...] = dkv_f_ref[pl.ds(FRONT, seq), :].astype(BF16)
    hd = dkv_ref.shape[1] // 2

    def produce(c):
        at = rows_at(c * BLOCK, BLOCK)
        for i in load_feed(c):
            i.wait()

        def cols(n, carry):
            there = rows_at(n * COLS, COLS)
            line.part[at, there] = project(acts[...], w_down[:, there])
            return carry

        lax.fori_loop(0, width // COLS, cols, 0)

        @pl.when(m == 0)
        def _():
            line.part[at, :] += mid[...]

        if c + 1 < chunks:
            for i in load_feed(c + 1):
                i.start()

    def output_step(c):
        def strip(i, carry):
            at = rows_at(i * STRIP, STRIP)
            there = rows_at(c * BLOCK + i * STRIP, STRIP)
            low[at, :] = (line.total[there, :] + bias_ref[...]).astype(BF16)
            return carry

        lax.fori_loop(0, BLOCK // STRIP, strip, 0)

    def spread_step(c):
        here = rows_at(c * BLOCK, BLOCK)

        def cols(n, carry):
            there = rows_at(n * COLS, COLS)
            total = dot_t(dkv_ref[here, :], w_kv_ref[there, :])
            for i in range(planes):
                total = total + dot_t(dq[:, pl.ds(i * cols_q, cols_q)], w_q[i, there, :])
            spread[:, there] = total
            return carry

        lax.fori_loop(0, width // COLS, cols, 0)

    def norm_step(c):
        def strip(i, carry):
            at = rows_at(i * STRIP, STRIP)
            grad = spread[at, :]
            d_in, weighted = norm_back_rows(xs[at, :].astype(F32), grad, gain_ref[...])
            in_grad[at, :] = (d_mid[at, :] + d_in).astype(BF16)
            sums[0] += fold_rows(weighted)
            sums[1] += fold_rows(grad)
            return carry

        lax.fori_loop(0, BLOCK // STRIP, strip, 0)

    def swap(r):
        return pltpu.make_async_remote_copy(
            trade.at[r], trade_in.at[r], t_send.at[r], t_recv.at[r],
            device_id=peers[r], device_id_type=MESH,
        )

    def vectors_first():
        trade[0] = jnp.zeros_like(trade.at[0])
        for i in range(2):
            trade[0, i : i + 1] = jnp.sum(sums[i], axis=0, keepdims=True)
        for i in range(sums_in.shape[0]):
            trade[0, 2 + i : 3 + i] = jnp.sum(sums_in[i], axis=0, keepdims=True)
        at = 2 + sums_in.shape[0]
        trade[0, at : at + 1] = b_up_in[...]
        d_values = dkv_f_ref[pl.ds(FRONT, seq), pl.ds(hd, hd)]
        trade[0, at + 1 : at + 2, 0:hd] = jnp.sum(d_values, axis=0, keepdims=True)
        swap(0).start()

    def vectors_next(r):
        swap(r).wait()
        trade[r + 1] = trade[r] + trade_in[r]
        if r + 1 < rounds:
            swap(r + 1).start()
        else:
            vectors_out[...] = trade[r + 1]

    def table_block(c):
        load_normed(c).wait()

        def cols(n, carry):
            there = rows_at(n * COLS, COLS)
            part = dot_down(dkv_ref[pl.ds(c * BLOCK, BLOCK), :], normed[:, there])
            table[:, there] = part if c == 0 else table[:, there] + part
            return carry

        lax.fori_loop(0, width // COLS, cols, 0)
        if c + 1 < blocks:
            load_normed(c + 1).start()

    bits = [lax.rem(lax.div(d, 1 << r), 2) for r in range(rounds)]
    base = [0]
    size = [table.shape[0]]
    for r in range(rounds):
        size.append(size[r] // 2)
        base.append(base[r] + bits[r] * size[r + 1])

    def part_of(start, count):
        return pl.ds(pl.multiple_of(start, 8), count)

    def halve(r):
        away = part_of(base[r] + (1 - bits[r]) * size[r + 1], size[r + 1])
        into = pl.ds(size[0] - size[r], size[r + 1])
        return pltpu.make_async_remote_copy(
            table.at[away], table_in.at[into], h_send.at[r], h_recv.at[r],
            device_id=peers[r], device_id_type=MESH,
        )

    def double(r, mine):
        start = base[r] + (bits[r] if mine else 1 - bits[r]) * size[r + 1]
        at = part_of(start, size[r + 1])
        return pltpu.make_async_remote_copy(
            table_all.at[at], table_all.at[at], d_send.at[r], d_recv.at[r],
            device_id=peers[r], device_id_type=MESH,
        )

    store_table = pltpu.make_async_copy(turned, table_out, out_sem.at[2])

    def table_step(i):
        if 1 <= i <= rounds:
            r = i - 1
            halve(r).wait()
            at = part_of(base[r + 1], size[r + 1])
            whole = table_all if i == rounds else table
            whole[at, :] = table[at, :] + table_in[pl.ds(size[0] - size[r], size[r + 1]), :]
        elif i > rounds:
            r = 2 * rounds - i
            double(r, True).wait_send()
            double(r, False).wait_recv()
        if i < rounds:
            halve(i).start()
        elif i < 2 * rounds:
            double(2 * rounds - 1 - i, True).start()
        else:
            for n in range(width // COLS):
                at = pl.ds(n * COLS, COLS)
                turned[at, :] = table_all[:, at].T
            store_table.start()

    load_next.wait()
    line.meet(peers)
    for k in range(3):
        line.slot(k)
    load(0, w_down_hbm, w_down).wait()
    load(1, w_q_hbm, w_q).wait()

    def spread_block(v):
        for i in load_grad(v):
            i.wait()
        spread_step(v)

    def norm_block(v):
        if v >= 1:
            store(1, in_grad, in_grad_hbm, v - 1).wait()
        norm_step(v)
        store(1, in_grad, in_grad_hbm, v).start()
        if v + 1 < blocks:
            for i in load_grad(v + 1):
                i.start()

    def output_block(c):
        if c >= 1:
            store(0, low, out_hbm, c - 1).wait()
        output_step(c)
        store(0, low, out_hbm, c).start()

    slot_count = (line.pieces + LATE) // SLOT
    steps = [[] for _ in range(max(slot_count, 4 * blocks + 8))]
    for c in range(1, chunks):
        steps[(c - 1) * slots + 3].append(functools.partial(produce, c))
    for c in range(chunks):
        steps[(c + 1) * slots - 1 + LATE // SLOT].append(functools.partial(output_block, c))
    for v in range(blocks):
        steps[3 + 2 * v].append(functools.partial(spread_block, v))
        steps[4 + 2 * v].append(functools.partial(norm_block, v))
        steps[2 + 2 * v].append(functools.partial(table_block, v))
    done = 4 + 2 * blocks
    for i in range(rounds + 1):
        steps[done + i].append(vectors_first if i == 0 else functools.partial(vectors_next, i - 1))
    first = 1 + 2 * blocks
    apart = max(1, min(2, (len(steps) - 1 - first) // (2 * rounds)))
    for i in range(2 * rounds + 1):
        steps[first + i * apart].append(functools.partial(table_step, i))
    for i, todo in enumerate(steps):
        if i >= 3 and i < slot_count:
            line.slot(i)
        for step in todo:
            step()
    store(0, low, out_hbm, chunks - 1).wait()
    store(1, in_grad, in_grad_hbm, blocks - 1).wait()
    store_table.wait()
    line.finish()


def feed_and_input_grad(
    acts, w_down, middle, b_down, d_queries, all_query, d_keyval_sum, w_keyval, inputs, d_middle, gain,
    normed, feed_next, sums, b_up,
):
    seq, width = inputs.shape
    rounds = (lax.axis_size("dp") - 1).bit_length()
    vmem = pl.BlockSpec(memory_space=pltpu.VMEM)
    dma = pltpu.SemaphoreType.DMA
    block = lambda dtype: pltpu.VMEM((BLOCK, width), dtype)
    rest = seq - FEED_EARLY * BLOCK
    shape = jax.ShapeDtypeStruct
    table = (w_keyval.shape[1], width)
    return pl.pallas_call(
        functools.partial(feed_kernel, rounds),
        out_shape=(
            shape((rest, width), BF16),
            shape((seq, width), BF16),
            shape(table[::-1], F32),
            shape((16, width), F32),
        ),
        in_specs=[HBM] * 9 + [vmem] * 6,
        out_specs=(HBM, HBM, HBM, vmem),
        scratch_shapes=[
            pltpu.VMEM(w_down.shape, BF16),
            pltpu.VMEM(all_query.shape, BF16),
            pltpu.VMEM((BLOCK, acts.shape[1]), BF16),
            block(F32),
            block(BF16),
            block(BF16),
            block(F32),
            block(F32),
            block(BF16),
            block(BF16),
            block(BF16),
            pltpu.VMEM((seq, w_keyval.shape[1]), BF16),
            pltpu.VMEM((2, 8, width), F32),
            pltpu.VMEM((rounds + 1, 16, width), F32),
            pltpu.VMEM((rounds, 16, width), F32),
            pltpu.VMEM(table, F32),
            pltpu.VMEM(table, F32),
            pltpu.VMEM(table, F32),
            pltpu.VMEM(table[::-1], F32),
            dma((9,)),
            dma((3,)),
            dma((rounds,)),
            dma((rounds,)),
            dma((rounds,)),
            dma((rounds,)),
            dma((rounds,)),
            dma((rounds,)),
        ]
        + LineSum.scratch(rest, rest // PIECE, width),
        compiler_params=pltpu.CompilerParams(
            collective_id=2, has_side_effects=True, vmem_limit_bytes=VMEM_LIMIT
        ),
        cost_estimate=pl.CostEstimate(
            flops=150 * 10**9, bytes_accessed=2**25, transcendentals=0
        ),
        name="feed_and_input_grad",
    )(
        acts, w_down, middle, d_queries, all_query, inputs, d_middle, normed, feed_next,
        d_keyval_sum, w_keyval, gain.reshape(1, width), b_down.reshape(1, width), sums,
        b_up.reshape(1, width),
    )


def shards(
    inputs,
    doc_ids,
    pad_mask,
    attn_gain,
    attn_shift,
    w_query,
    b_query,
    w_keyval,
    b_value,
    w_out,
    b_out,
    mlp_gain,
    mlp_shift,
    w_up,
    b_up,
    w_down,
    b_down,
    cotangent,
):
    seq = doc_ids.shape[1]
    hd = b_value.shape[0]
    width = inputs.shape[1]
    own_cols = w_query.shape[1]
    own = lax.axis_index("mp") * own_cols
    docs = doc_ids[0]
    codes = jnp.where(pad_mask[0] == 1, docs, -1)
    code_col = jnp.pad(codes, (FRONT, 0), constant_values=-2).reshape(-1, 1)
    doc_row = docs.reshape(1, seq)

    all_query, all_out, normed_attn, queries, mixed, d_acts, keyval, keys_t, lse = attention_front(
        inputs, w_query, b_query, w_keyval, b_value, w_out, attn_gain, attn_shift, code_col, doc_row,
        cotangent, w_down,
    )
    middle, acts, d_hidden, grad_w_down, grad_w_up, first, second, grad_b_up = mlp(
        mixed, all_out, inputs, w_up, d_acts, cotangent, b_out, mlp_gain, mlp_shift, b_up
    )
    grad_b_up = jnp.sum(grad_b_up, axis=0)
    grad_w_up = lax.psum_scatter(grad_w_up, "dp", scatter_dimension=0, tiled=True)
    grad_w_down = lax.psum_scatter(grad_w_down, "dp", scatter_dimension=1, tiled=True)

    d_middle, d_queries, out_first, feed_next, grads, d_keyval_sum, sums = mlp_attend_back(
        d_hidden, w_up, all_out, middle, cotangent, queries, acts, w_down, normed_attn, mixed, first, second,
        own_cols,
        keyval, keys_t, code_col, doc_row, lse, mlp_gain, b_down,
    )
    grads, grad_w_down, grad_w_up = lax.optimization_barrier((grads, grad_w_down, grad_w_up))
    grads = lax.psum_scatter(grads, "dp", scatter_dimension=1, tiled=True)
    out_rest, input_grad, grad_w_keyval, totals = feed_and_input_grad(
        acts, w_down, middle, b_down, d_queries, all_query, d_keyval_sum, w_keyval, inputs, d_middle,
        attn_gain, normed_attn, feed_next, sums, grad_b_up,
    )
    outputs = jnp.concatenate([out_first, out_rest], 0)
    grad_w_query, grad_w_out = grads[:own_cols].T, grads[own_cols:]
    grad_attn_gain, grad_attn_shift, grad_mlp_gain, grad_mlp_shift = (totals[i] for i in range(4))
    grad_b_out, grad_b_down, grad_b_query, grad_b_up = (totals[i] for i in range(4, 8))
    grad_b_query = lax.dynamic_slice_in_dim(grad_b_query, own, own_cols, 0)
    grad_b_value = totals[8, :hd]
    return (
        outputs,
        input_grad,
        grad_attn_gain,
        grad_attn_shift,
        grad_w_query,
        grad_b_query,
        grad_w_keyval,
        grad_b_value,
        grad_w_out,
        grad_b_out,
        grad_mlp_gain,
        grad_mlp_shift,
        grad_w_up,
        grad_b_up,
        grad_w_down,
        grad_b_down,
    )


def solution(mesh):
    return jax.shard_map(
        shards,
        mesh=mesh,
        in_specs=(
            P("dp", None),
            P("dp", None),
            P("dp", None),
            P(),
            P(),
            P(None, "mp"),
            P("mp"),
            P(),
            P(),
            P("mp", None),
            P(),
            P(),
            P(),
            P(None, "mp"),
            P("mp"),
            P("mp", None),
            P(),
            P("dp", None),
        ),
        out_specs=(
            P("dp", None),
            P("dp", None),
            P(),
            P(),
            P("dp", "mp"),
            P("mp"),
            P(),
            P(),
            P("mp", "dp"),
            P(),
            P(),
            P(),
            P("dp", "mp"),
            P("mp"),
            P("mp", "dp"),
            P(),
        ),
        check_vma=False,
    )
```
